32 devices in a mesh: dp: 16 (over z, y, x), tensor: 2 (over core).
Axes of the slice: x: 2, y: 2, z: 4, core: 2. Of those that a mesh axis runs over, the one named last changes fastest.
Arguments:
- layer_input: bfloat16 [8192, 2048], P(('dp', 'tensor')), may hold values from -6 to 6
- ln1_gain: bfloat16 [2048], replicated, may hold values from 0.5 to 1.5
- ln1_bias: bfloat16 [2048], replicated, may hold values from -1.1953125 to 1.1953125
- ln2_gain: bfloat16 [2048], replicated, may hold values from 0.5 to 1.5
- ln2_bias: bfloat16 [2048], replicated, may hold values from -1.1953125 to 1.1953125
- qkv_weight: bfloat16 [2048, 6144], P('dp', 'tensor'), may hold values from -0.125 to 0.125
- qkv_bias: bfloat16 [6144], P('tensor'), may hold values from -1.1953125 to 1.1953125
- dense_weight: bfloat16 [2048, 2048], P('tensor', 'dp'), may hold values from -1 to 1
- dense_bias: bfloat16 [2048], replicated, may hold values from -1.1953125 to 1.1953125
- fc1_weight: bfloat16 [2048, 8192], P('dp', 'tensor'), may hold values from -0.125 to 0.125
- fc1_bias: bfloat16 [8192], P('tensor'), may hold values from -1.1953125 to 1.1953125
- fc2_weight: bfloat16 [8192, 2048], P('tensor', 'dp'), may hold values from -0.0625 to 0.0625
- fc2_bias: bfloat16 [2048], replicated, may hold values from -1.1953125 to 1.1953125
- seq_ids: int32 [8192], P('dp'), may hold values from 0 to 2, as said below
- cotangent: bfloat16 [8192, 2048], P(('dp', 'tensor')), may hold values from -6 to 6
Outputs:
- layer_output: bfloat16 [8192, 2048], P(('dp', 'tensor'))
- input_grad: float32 [8192, 2048], P(('dp', 'tensor'))
- ln1_gain_grad: float32 [2048], replicated
- ln1_bias_grad: float32 [2048], replicated
- ln2_gain_grad: float32 [2048], replicated
- ln2_bias_grad: float32 [2048], replicated
- qkv_weight_grad: float32 [2048, 6144], P('dp', 'tensor')
- qkv_bias_grad: float32 [6144], P('tensor')
- dense_weight_grad: float32 [2048, 2048], P('tensor', 'dp')
- dense_bias_grad: float32 [2048], replicated
- fc1_weight_grad: float32 [2048, 8192], P('dp', 'tensor')
- fc1_bias_grad: float32 [8192], P('tensor')
- fc2_weight_grad: float32 [8192, 2048], P('tensor', 'dp')
- fc2_bias_grad: float32 [2048], replicated
The draws below stay inside these ranges and needn't reach their ends.
Inputs may be any that keep to these rules, and one draw needn't show every extreme that they name: `seq_ids`: within each group of 512 tokens the numbers start at 0 and never fall. A group is either one sequence (all 0) or three sequences of 128, 256 and 128 tokens (0, 1, 2); at least one group has three.
All inputs are finite; a program needn't handle non-finite values.
Results may differ from the reference program's by a relative error of at most 0.0089.
Values may be sent and summed in bfloat16 or wider, within the bound.
A program may use at most 256 MiB of HBM per device.

```python
import math
import jax
import jax.numpy as jnp
from jax import lax

D = 2048
FF = 8192
HEADS = 8
GROUP_TOK = 512
HEAD_DIM = 256
ROT = 64
TOKENS = 8192


def draw_seq_ids(key, part):
    key = jax.random.fold_in(key, 11)
    key_pattern = jax.random.fold_in(key, 1)
    key_forced = jax.random.fold_in(key, 2)
    group_count = TOKENS // GROUP_TOK
    pattern = jax.random.randint(key_pattern, (group_count,), 0, 2).astype(jnp.int32)
    forced = jax.random.randint(key_forced, (), 0, group_count).astype(jnp.int32)
    pattern = jnp.maximum(pattern, (jnp.arange(group_count, dtype=jnp.int32) == forced).astype(jnp.int32))
    places = jnp.arange(GROUP_TOK, dtype=jnp.int32)
    three_way = (places >= GROUP_TOK // 4).astype(jnp.int32) + (places >= 3 * (GROUP_TOK // 4)).astype(jnp.int32)
    numbers = pattern[:, None] * three_way[None, :]
    return numbers.reshape(-1).astype(jnp.int32)


def with_spikes(entries, rng, source, target, blocks, factor):
    def block_of(dim):
        return (jnp.arange(entries.shape[dim]) // (entries.shape[dim] // blocks)).reshape((-1,) + (1,) * (entries.ndim - 1 - dim))

    first = jax.random.permutation(rng, blocks)[block_of(target)]
    far = (block_of(target) + blocks // 2) % blocks
    return jnp.where((block_of(source) == first) | (block_of(source) == far), factor * entries, entries)


def levels(own_key, dims, pieces, smallest, top_value):
    def one(dim, parts):
        steps = jax.random.uniform(jax.random.fold_in(jax.random.fold_in(own_key, 6), dim), (parts,), jnp.float32, smallest / len(pieces), top_value / len(pieces))
        return jnp.repeat(jnp.exp(steps), dims[dim] // parts).reshape((-1,) + (1,) * (len(dims) - dim - 1))

    level = one(*pieces[0])
    for cut in pieces[1:]:
        level = level * one(*cut)
    return level


def noise(rng, shape, deviation, limit, shards=(), kind=jnp.bfloat16):
    result = deviation * jax.random.normal(rng, shape, jnp.float32)
    if shards:
        result = result * levels(rng, shape, shards, -0.22, 0.18)
    return jnp.clip(result, -limit, limit).astype(kind)


def noise_with(own_key, extent, deviation, bound, split, heavy, kind=jnp.bfloat16):
    result = deviation * jax.random.normal(own_key, extent, jnp.float32)
    if split:
        result = result * levels(own_key, extent, split, -0.22, 0.18)
    return jnp.clip(with_spikes(result, jax.random.fold_in(own_key, 3), *heavy), -bound, bound).astype(kind)


def setup_inputs(seed: int = 0) -> dict:
    seeds = jax.random.split(jax.random.key(seed), 16)
    layer_input = noise_with(seeds[0], (TOKENS, D), 1.0, 6.0, ((0, 32),), (0, 1, 32, 2.75))
    ln1_gain = jnp.clip(1.0 + 0.1 * jax.random.normal(seeds[1], (D,), jnp.float32), 0.5, 1.5).astype(jnp.bfloat16)
    ln1_bias = noise(seeds[2], (D,), 0.2, 1.1953125)
    ln2_gain = jnp.clip(1.0 + 0.1 * jax.random.normal(seeds[3], (D,), jnp.float32), 0.5, 1.5).astype(jnp.bfloat16)
    ln2_bias = noise(seeds[4], (D,), 0.2, 1.1953125)
    qkv_weight = noise(seeds[5], (D, 3 * D), D ** -0.5, 0.125, ((0, 16), (1, 2)))
    qkv_bias = noise(seeds[6], (3 * D,), 0.2, 1.1953125, ((0, 2),))
    dense_weight = noise(seeds[7], (D, D), (D // 64) ** -0.5, 1.0, ((0, 2), (1, 16)))
    dense_bias = noise(seeds[8], (D,), 0.2, 1.1953125)
    fc1_weight = noise(seeds[9], (D, FF), D ** -0.5, 0.125, ((0, 16), (1, 2)))
    fc1_bias = noise(seeds[10], (FF,), 0.2, 1.1953125, ((0, 2),))
    fc2_weight = noise(seeds[11], (FF, D), FF ** -0.5, 0.0625, ((0, 2), (1, 16)))
    fc2_bias = noise(seeds[12], (D,), 0.2, 1.1953125)
    seq_ids = draw_seq_ids(jax.random.fold_in(seeds[15], 71), 0)
    cotangent = noise_with(seeds[14], (TOKENS, D), 1.0, 6.0, ((0, 32),), (0, 1, 32, 2.75))
    return {"layer_input": layer_input, "ln1_gain": ln1_gain, "ln1_bias": ln1_bias, "ln2_gain": ln2_gain, "ln2_bias": ln2_bias, "qkv_weight": qkv_weight, "qkv_bias": qkv_bias, "dense_weight": dense_weight, "dense_bias": dense_bias, "fc1_weight": fc1_weight, "fc1_bias": fc1_bias, "fc2_weight": fc2_weight, "fc2_bias": fc2_bias, "seq_ids": seq_ids, "cotangent": cotangent}


HIGHEST_PRECISION = lax.Precision.HIGHEST

@jax.custom_vjp
def low(v):
    return lax.optimization_barrier(v.astype(jnp.bfloat16)).astype(jnp.float32)

@jax.custom_vjp
def low_back(v):
    return v

def low_keep(v):
    return (low(v), None)

def low_pass(kept, grad):
    return (grad,)

def back_keep(v):
    return (v, None)

def back_low(kept, grad):
    return (low(grad),)
low.defvjp(low_keep, low_pass)
low_back.defvjp(back_keep, back_low)

def layer_norm(values, gain, shift):
    center = values - lax.optimization_barrier(jnp.mean(values, axis=-1, keepdims=True))
    spread = lax.optimization_barrier(jnp.mean(center * center, axis=-1, keepdims=True))
    return center * lax.rsqrt(spread + 1e-05) * gain + shift

def turn_angles(group_ids):
    places = jnp.arange(group_ids.shape[-1], dtype=jnp.int32)
    starts_flag = jnp.concatenate([jnp.ones_like(group_ids[..., :1], dtype=bool), group_ids[..., 1:] != group_ids[..., :-1]], axis=-1)
    starts = lax.cummax(jnp.where(starts_flag, places, 0), axis=group_ids.ndim - 1)
    position = (places - starts).astype(jnp.float32)
    steps_rot = jnp.arange(ROT // 2, dtype=jnp.float32)
    inverse = jnp.exp(steps_rot * (-2.0 * math.log(10000.0) / ROT))
    angles = position[..., None] * inverse
    angles = jnp.concatenate([angles, angles], axis=-1)
    return (jnp.cos(angles), jnp.sin(angles))

def rotary(vectors, cosine_table, sine_table):
    half_rot = ROT // 2
    rot_part = vectors[..., :ROT]
    rot_rest = vectors[..., ROT:]
    turned = jnp.concatenate([-rot_part[..., half_rot:], rot_part[..., :half_rot]], axis=-1)
    rotated = rot_part * cosine_table[:, None, :] + turned * sine_table[:, None, :]
    return jnp.concatenate([rotated, rot_rest], axis=-1)

def attend_group(qkv_group, cosine_table, sine_table, allowed_mask):
    query = low(rotary(qkv_group[:, :, 0], cosine_table, sine_table))
    keys = low(rotary(qkv_group[:, :, 1], cosine_table, sine_table))
    values = low(qkv_group[:, :, 2])
    scores = low_back(jnp.einsum('qhd,khd->hqk', query, keys, precision=HIGHEST_PRECISION) * 0.0625)
    scores = jnp.where(allowed_mask[None] > 0.5, scores, -1e+30)
    highest = lax.optimization_barrier(jnp.max(scores, axis=-1, keepdims=True))
    weights = jnp.exp(scores - highest)
    probability = low(weights / lax.optimization_barrier(jnp.sum(weights, axis=-1, keepdims=True)))
    attended = jnp.einsum('hqk,khd->qhd', probability, values, precision=HIGHEST_PRECISION)
    return low(low_back(attended))

def forward(layer_input, ln1_gain, ln1_bias, ln2_gain, ln2_bias, qkv_weight, qkv_bias, dense_weight, dense_bias, fc1_weight, fc1_bias, fc2_weight, fc2_bias, cosine_table, sine_table, allowed_mask):
    normed_attn = low(layer_norm(layer_input, ln1_gain, ln1_bias))
    normed_ffn = low(layer_norm(layer_input, ln2_gain, ln2_bias))
    qkv_full = low_back(jnp.dot(normed_attn, qkv_weight, precision=HIGHEST_PRECISION) + qkv_bias)
    group_count = allowed_mask.shape[0]
    qkv_full = qkv_full.reshape(group_count, GROUP_TOK, HEADS, 3, HEAD_DIM)
    attended = lax.map(jax.checkpoint(lambda packed: attend_group(*packed)), (qkv_full, cosine_table, sine_table, allowed_mask))
    attended = attended.reshape(layer_input.shape[0], D)
    ffn_input = low_back(jnp.dot(normed_ffn, fc1_weight, precision=HIGHEST_PRECISION) + fc1_bias)
    hidden = low(jax.nn.gelu(ffn_input, approximate=False))
    branch = jnp.dot(attended, dense_weight, precision=HIGHEST_PRECISION) + jnp.dot(hidden, fc2_weight, precision=HIGHEST_PRECISION)
    return layer_input + branch + dense_bias + fc2_bias

def reference(layer_input, ln1_gain, ln1_bias, ln2_gain, ln2_bias, qkv_weight, qkv_bias, dense_weight, dense_bias, fc1_weight, fc1_bias, fc2_weight, fc2_bias, seq_ids, cotangent):
    floats = [value.astype(jnp.float32) for value in (layer_input, ln1_gain, ln1_bias, ln2_gain, ln2_bias, qkv_weight, qkv_bias, dense_weight, dense_bias, fc1_weight, fc1_bias, fc2_weight, fc2_bias)]
    group_ids = seq_ids.reshape(-1, GROUP_TOK)
    cosine_table, sine_table = turn_angles(group_ids)
    places = jnp.arange(GROUP_TOK, dtype=jnp.int32)
    allowed_mask = ((group_ids[:, :, None] == group_ids[:, None, :]) & (places[None, None, :] <= places[None, :, None])).astype(jnp.float32)
    layer_out, pullback = jax.vjp(lambda *params: forward(*params, cosine_table, sine_table, allowed_mask), *floats)
    gradients = pullback(cotangent.astype(jnp.float32))
    return (layer_out.astype(jnp.bfloat16), gradients[0], gradients[1], gradients[2], gradients[3], gradients[4], gradients[5], gradients[6], gradients[7], gradients[8], gradients[9], gradients[10], gradients[11], gradients[12])
```

```python
import math

import jax
import jax.numpy as jnp
from jax import lax
from jax.sharding import PartitionSpec as P

HEAD_DIM = 256
ROT = 64
BIT_X, BIT_Y, BIT_ZL, FIRST_ZH = 0, 1, 2, 3
F32, BF16 = jnp.float32, jnp.bfloat16
NN = (((1,), (0,)), ((), ()))
NT = (((1,), (1,)), ((), ()))
TN = (((0,), (0,)), ((), ()))


def mm(a, b, dims):
    return lax.dot_general(a, b, dims, preferred_element_type=F32)


def turn_angles(group_ids):
    places = jnp.arange(group_ids.shape[-1], dtype=jnp.int32)
    starts_flag = jnp.concatenate(
        [jnp.ones_like(group_ids[..., :1], dtype=bool), group_ids[..., 1:] != group_ids[..., :-1]],
        axis=-1,
    )
    starts = lax.cummax(jnp.where(starts_flag, places, 0), axis=group_ids.ndim - 1)
    position = (places - starts).astype(F32)
    steps_rot = jnp.arange(ROT // 2, dtype=F32)
    inverse = jnp.exp(steps_rot * (-2.0 * math.log(10000.0) / ROT))
    angles = position[..., None] * inverse
    angles = jnp.concatenate([angles, angles], axis=-1)
    return (jnp.cos(angles), jnp.sin(angles))


def rotary(vectors, cosine_table, sine_table):
    half_rot = ROT // 2
    rot_part = vectors[..., :ROT]
    rot_rest = vectors[..., ROT:]
    turned = jnp.concatenate([-rot_part[..., half_rot:], rot_part[..., :half_rot]], axis=-1)
    rotated = rot_part * cosine_table + turned * sine_table
    return jnp.concatenate([rotated, rot_rest], axis=-1)


def rotary_back(vectors, cosine_table, sine_table):
    half_rot = ROT // 2
    rot_part = vectors[..., :ROT]
    rot_rest = vectors[..., ROT:]
    turned = jnp.concatenate([rot_part[..., half_rot:], -rot_part[..., :half_rot]], axis=-1)
    rotated = rot_part * cosine_table + turned * sine_table
    return jnp.concatenate([rotated, rot_rest], axis=-1)


def local(
    layer_input,
    ln1_gain,
    ln1_bias,
    ln2_gain,
    ln2_bias,
    qkv_weight,
    qkv_bias,
    dense_weight,
    dense_bias,
    fc1_weight,
    fc1_bias,
    fc2_weight,
    fc2_bias,
    seq_ids,
    cotangent,
):
    n = lax.axis_size("dp")
    bits = n.bit_length() - 1
    me = lax.axis_index("dp")
    core = lax.axis_index("tensor")
    bit = [(me >> k) & 1 for k in range(bits)]
    zh_bits = tuple(range(FIRST_ZH, bits))
    rows_here, d_model = layer_input.shape
    feature = 2 * bit[BIT_ZL] + bit[BIT_X]

    def swap(v, k):
        return lax.ppermute(v, "dp", [(i, i ^ (1 << k)) for i in range(n)])

    def swap_core(v):
        return lax.ppermute(v, "tensor", [(0, 1), (1, 0)])

    def pick(v, b, axis):
        return lax.dynamic_index_in_dim(v, b, axis, keepdims=False)

    def ordered(b, own, other, axis):
        return jnp.stack(
            [jnp.where(b == 0, own, other), jnp.where(b == 0, other, own)], axis=axis
        )

    def gather_rows(v):
        v = jnp.stack([v, swap(v, BIT_ZL)], axis=0)
        v = jnp.concatenate([v, swap(v, BIT_X)], axis=0)
        return v

    def gather_tokens(v):
        v = gather_rows(v)
        return ordered(core, v, swap_core(v), 1).reshape(4 * 2 * rows_here, d_model)

    def scatter_tokens(v):
        v = v.reshape(4, 2, rows_here, d_model)
        keep = pick(v, core, 1)
        v = keep + swap_core(pick(v, 1 - core, 1).astype(BF16))
        v = v[:2] + swap(v[2:].astype(BF16), BIT_X)
        return v[0] + swap(v[1].astype(BF16), BIT_ZL)

    def gather_weight(w):
        rows, width = w.shape
        w = w.reshape(rows, 2, 2, width // 4)
        w = ordered(bit[BIT_X], pick(w, bit[BIT_X], 2), swap(pick(w, 1 - bit[BIT_X], 2), BIT_X), 0)
        w = ordered(bit[BIT_ZL], pick(w, bit[BIT_ZL], 2), swap(pick(w, 1 - bit[BIT_ZL], 2), BIT_ZL), 0)
        for k in zh_bits:
            w = ordered(bit[k], w, swap(w, k), 0)
        w = ordered(bit[BIT_Y], w, swap(w, BIT_Y), w.ndim - 3)
        return w.reshape(rows * n, width // 4)

    def scatter_grad(g):
        rows, width = g.shape[0] // n, g.shape[1]
        g = g.reshape((2,) * bits + (rows, width))
        axis = bits - 1 - BIT_Y
        g = pick(g, bit[BIT_Y], axis) + swap(pick(g, 1 - bit[BIT_Y], axis).astype(BF16), BIT_Y)
        for k in reversed(zh_bits):
            g = pick(g, bit[k], 0) + swap(pick(g, 1 - bit[k], 0).astype(BF16), k)
        g = g.astype(BF16)
        g = ordered(bit[BIT_ZL], pick(g, bit[BIT_ZL], 0), swap(pick(g, 1 - bit[BIT_ZL], 0), BIT_ZL), 2)
        g = ordered(bit[BIT_X], pick(g, bit[BIT_X], 0), swap(pick(g, 1 - bit[BIT_X], 0), BIT_X), 2)
        return g.reshape(rows, 4 * width).astype(F32)

    def take_block(v, parts):
        return lax.dynamic_slice_in_dim(v, feature * (v.shape[0] // parts), v.shape[0] // parts, 0)

    gains = [v.astype(F32) for v in (ln1_gain, ln1_bias, ln2_gain, ln2_bias)]

    rows_in = gather_tokens(layer_input)
    w_fc1 = gather_weight(fc1_weight)
    cot = gather_tokens(cotangent)
    w_fc2 = gather_weight(fc2_weight.T)
    w_qkv = gather_weight(qkv_weight)
    w_dense = gather_weight(dense_weight.T)
    ids = gather_rows(seq_ids)
    group_len = seq_ids.shape[0]

    def normalize(v):
        v = v.astype(F32)
        center = v - jnp.mean(v, axis=-1, keepdims=True)
        spread = jnp.mean(center * center, axis=-1, keepdims=True)
        scale = lax.rsqrt(spread + 1e-05)
        return center * scale, scale

    xhat, _ = normalize(rows_in)
    normed_attn = (xhat * gains[0] + gains[1]).astype(BF16)
    normed_ffn = (xhat * gains[2] + gains[3]).astype(BF16)

    ffn_input = mm(normed_ffn, w_fc1, NN) + take_block(fc1_bias, 4).astype(F32)
    cdf = 0.5 * (1.0 + lax.erf(ffn_input * (1.0 / math.sqrt(2.0))))
    density = jnp.exp(-0.5 * ffn_input * ffn_input) * (1.0 / math.sqrt(2.0 * math.pi))
    hidden = (ffn_input * cdf).astype(BF16)
    slope = cdf + ffn_input * density
    grad_fc2 = mm(cot, hidden, TN)
    out_fc2 = scatter_grad(grad_fc2).T

    grad_ffn = (mm(cot, w_fc2, NN) * slope).astype(BF16)
    grad_fc1 = mm(normed_ffn, grad_ffn, TN)
    out_fc1 = scatter_grad(grad_fc1)

    qkv = mm(normed_attn, w_qkv, NN) + take_block(qkv_bias, 4).astype(F32)
    qkv = qkv.reshape(4, group_len, 3, HEAD_DIM)
    cosines, sines = turn_angles(ids)
    query = rotary(qkv[:, :, 0], cosines, sines).astype(BF16)
    keys = rotary(qkv[:, :, 1], cosines, sines).astype(BF16)
    values = qkv[:, :, 2].astype(BF16)
    places = jnp.arange(group_len, dtype=jnp.int32)
    allowed = (ids[:, :, None] == ids[:, None, :]) & (places[None, None, :] <= places[None, :, None])
    scores = jnp.einsum("gqd,gkd->gqk", query, keys, preferred_element_type=F32) * 0.0625
    scores = jnp.where(allowed, scores, -1e30)
    weights = jnp.exp(scores - jnp.max(scores, axis=-1, keepdims=True))
    probability = weights / jnp.sum(weights, axis=-1, keepdims=True)
    prob_low = probability.astype(BF16)
    attended = jnp.einsum("gqk,gkd->gqd", prob_low, values, preferred_element_type=F32)
    attended = attended.astype(BF16).reshape(-1, HEAD_DIM)

    partial = mm(attended, w_dense, NT) + mm(hidden, w_fc2, NT)
    branch = scatter_tokens(partial)
    layer_output = (
        layer_input.astype(F32) + branch + dense_bias.astype(F32) + fc2_bias.astype(F32)
    ).astype(BF16)

    grad_dense = mm(cot, attended, TN)
    grad_attended = mm(cot, w_dense, NN).astype(BF16).reshape(4, group_len, HEAD_DIM)
    grad_prob = jnp.einsum("gqd,gkd->gqk", grad_attended, values, preferred_element_type=F32)
    row_dot = jnp.sum(probability * grad_prob, axis=-1, keepdims=True)
    grad_scores = (probability * (grad_prob - row_dot)).astype(BF16)
    grad_query = jnp.einsum("gqk,gkd->gqd", grad_scores, keys, preferred_element_type=F32) * 0.0625
    grad_keys = jnp.einsum("gqk,gqd->gkd", grad_scores, query, preferred_element_type=F32) * 0.0625
    grad_values = jnp.einsum("gqk,gqd->gkd", prob_low, grad_attended, preferred_element_type=F32)
    qkv_grad = jnp.concatenate(
        [
            rotary_back(grad_query, cosines, sines).astype(BF16),
            rotary_back(grad_keys, cosines, sines).astype(BF16),
            grad_values.astype(BF16),
        ],
        axis=-1,
    ).reshape(-1, 3 * HEAD_DIM)
    out_qkv = scatter_grad(mm(normed_attn, qkv_grad, TN))
    out_dense = scatter_grad(grad_dense).T

    attn_part = mm(qkv_grad, w_qkv, NT)
    ffn_part = mm(grad_ffn, w_fc1, NT)
    e_rows = scatter_tokens(attn_part * gains[0] + ffn_part * gains[2])
    own_hat, own_scale = normalize(layer_input)
    cot_rows = cotangent.astype(F32)
    input_grad = cot_rows + own_scale * (
        e_rows
        - jnp.mean(e_rows, axis=-1, keepdims=True)
        - own_hat * jnp.mean(e_rows * own_hat, axis=-1, keepdims=True)
    )

    small = jnp.stack(
        [
            jnp.sum(attn_part * xhat, axis=0),
            jnp.sum(attn_part, axis=0),
            jnp.sum(ffn_part * xhat, axis=0),
            jnp.sum(ffn_part, axis=0),
            jnp.sum(cot_rows, axis=0),
        ]
    )
    small = small + swap_core(small)
    for k in range(bits):
        small = small + swap(small, k)
    columns = jnp.concatenate(
        [jnp.sum(qkv_grad.astype(F32), axis=0), jnp.sum(grad_ffn.astype(F32), axis=0)]
    )
    for k in (BIT_Y,) + zh_bits:
        columns = columns + swap(columns, k)
    columns = ordered(bit[BIT_X], columns, swap(columns, BIT_X), 0)
    columns = ordered(bit[BIT_ZL], columns, swap(columns, BIT_ZL), 0).reshape(4, -1)
    out_qkv_bias = columns[:, : 3 * HEAD_DIM].reshape(-1)
    out_fc1_bias = columns[:, 3 * HEAD_DIM :].reshape(-1)

    return (
        layer_output,
        input_grad,
        small[0],
        small[1],
        small[2],
        small[3],
        out_qkv,
        out_qkv_bias,
        out_dense,
        small[4],
        out_fc1,
        out_fc1_bias,
        out_fc2,
        small[4],
    )


def solution(mesh):
    in_specs = (
        P(("dp", "tensor"), None),
        P(),
        P(),
        P(),
        P(),
        P("dp", "tensor"),
        P("tensor"),
        P("tensor", "dp"),
        P(),
        P("dp", "tensor"),
        P("tensor"),
        P("tensor", "dp"),
        P(),
        P("dp"),
        P(("dp", "tensor"), None),
    )
    out_specs = (
        P(("dp", "tensor"), None),
        P(("dp", "tensor"), None),
        P(),
        P(),
        P(),
        P(),
        P("dp", "tensor"),
        P("tensor"),
        P("tensor", "dp"),
        P(),
        P("dp", "tensor"),
        P("tensor"),
        P("tensor", "dp"),
        P(),
    )
    return jax.shard_map(local, mesh=mesh, in_specs=in_specs, out_specs=out_specs, check_vma=False)
```

```python
import functools
import math

import jax
import jax.numpy as jnp
from jax import lax
from jax.experimental import pallas as pl
from jax.experimental.pallas import tpu as pltpu
from jax.sharding import PartitionSpec as P

HEAD_DIM = 256
ROT = 64
BIT_X, BIT_Y, BIT_ZL, FIRST_ZH = 0, 1, 2, 3
F32, BF16 = jnp.float32, jnp.bfloat16
MESH = pl.DeviceIdType.MESH
NN = (((1,), (0,)), ((), ()))
NT = (((1,), (1,)), ((), ()))
TN = (((0,), (0,)), ((), ()))


def mm(a, b, dims):
    return lax.dot_general(a, b, dims, preferred_element_type=F32)


def turn_angles(group_ids):
    places = jnp.arange(group_ids.shape[-1], dtype=jnp.int32)
    starts_flag = jnp.concatenate(
        [jnp.ones_like(group_ids[..., :1], dtype=bool), group_ids[..., 1:] != group_ids[..., :-1]],
        axis=-1,
    )
    starts = lax.cummax(jnp.where(starts_flag, places, 0), axis=group_ids.ndim - 1)
    position = (places - starts).astype(F32)
    steps_rot = jnp.arange(ROT // 2, dtype=F32)
    inverse = jnp.exp(steps_rot * (-2.0 * math.log(10000.0) / ROT))
    angles = position[..., None] * inverse
    angles = jnp.concatenate([angles, angles], axis=-1)
    return (jnp.cos(angles), jnp.sin(angles))


def rotary(vectors, cosine_table, sine_table):
    half_rot = ROT // 2
    rot_part = vectors[..., :ROT]
    rot_rest = vectors[..., ROT:]
    turned = jnp.concatenate([-rot_part[..., half_rot:], rot_part[..., :half_rot]], axis=-1)
    rotated = rot_part * cosine_table + turned * sine_table
    return jnp.concatenate([rotated, rot_rest], axis=-1)


def rotary_back(vectors, cosine_table, sine_table):
    half_rot = ROT // 2
    rot_part = vectors[..., :ROT]
    rot_rest = vectors[..., ROT:]
    turned = jnp.concatenate([rot_part[..., half_rot:], -rot_part[..., :half_rot]], axis=-1)
    rotated = rot_part * cosine_table + turned * sine_table
    return jnp.concatenate([rotated, rot_rest], axis=-1)


def local_pairs(
    layer_input,
    ln1_gain,
    ln1_bias,
    ln2_gain,
    ln2_bias,
    qkv_weight,
    qkv_bias,
    dense_weight,
    dense_bias,
    fc1_weight,
    fc1_bias,
    fc2_weight,
    fc2_bias,
    seq_ids,
    cotangent,
):
    n = lax.axis_size("dp")
    bits = n.bit_length() - 1
    me = lax.axis_index("dp")
    core = lax.axis_index("tensor")
    bit = [(me >> k) & 1 for k in range(bits)]
    zh_bits = tuple(range(FIRST_ZH, bits))
    rows_here, d_model = layer_input.shape
    feature = 2 * bit[BIT_ZL] + bit[BIT_X]

    def swap(v, k):
        return lax.ppermute(v, "dp", [(i, i ^ (1 << k)) for i in range(n)])

    def swap_core(v):
        return lax.ppermute(v, "tensor", [(0, 1), (1, 0)])

    def pick(v, b, axis):
        return lax.dynamic_index_in_dim(v, b, axis, keepdims=False)

    def ordered(b, own, other, axis):
        return jnp.stack(
            [jnp.where(b == 0, own, other), jnp.where(b == 0, other, own)], axis=axis
        )

    def gather_rows(v):
        v = jnp.stack([v, swap(v, BIT_ZL)], axis=0)
        v = jnp.concatenate([v, swap(v, BIT_X)], axis=0)
        return v

    def gather_tokens(v):
        v = gather_rows(v)
        return ordered(core, v, swap_core(v), 1).reshape(4 * 2 * rows_here, d_model)

    def scatter_tokens(v):
        v = v.reshape(4, 2, rows_here, d_model)
        keep = pick(v, core, 1)
        v = keep + swap_core(pick(v, 1 - core, 1).astype(BF16))
        v = v[:2] + swap(v[2:].astype(BF16), BIT_X)
        return v[0] + swap(v[1].astype(BF16), BIT_ZL)

    def gather_weight(w):
        rows, width = w.shape
        w = w.reshape(rows, 2, 2, width // 4)
        w = ordered(bit[BIT_X], pick(w, bit[BIT_X], 2), swap(pick(w, 1 - bit[BIT_X], 2), BIT_X), 0)
        w = ordered(bit[BIT_ZL], pick(w, bit[BIT_ZL], 2), swap(pick(w, 1 - bit[BIT_ZL], 2), BIT_ZL), 0)
        for k in zh_bits:
            w = ordered(bit[k], w, swap(w, k), 0)
        w = ordered(bit[BIT_Y], w, swap(w, BIT_Y), w.ndim - 3)
        return w.reshape(rows * n, width // 4)

    def scatter_grad(g):
        rows, width = g.shape[0] // n, g.shape[1]
        g = g.reshape((2,) * bits + (rows, width))
        axis = bits - 1 - BIT_Y
        g = pick(g, bit[BIT_Y], axis) + swap(pick(g, 1 - bit[BIT_Y], axis).astype(BF16), BIT_Y)
        for k in reversed(zh_bits):
            g = pick(g, bit[k], 0) + swap(pick(g, 1 - bit[k], 0).astype(BF16), k)
        g = g.astype(BF16)
        g = ordered(bit[BIT_ZL], pick(g, bit[BIT_ZL], 0), swap(pick(g, 1 - bit[BIT_ZL], 0), BIT_ZL), 2)
        g = ordered(bit[BIT_X], pick(g, bit[BIT_X], 0), swap(pick(g, 1 - bit[BIT_X], 0), BIT_X), 2)
        return g.reshape(rows, 4 * width).astype(F32)

    def take_block(v, parts):
        return lax.dynamic_slice_in_dim(v, feature * (v.shape[0] // parts), v.shape[0] // parts, 0)

    gains = [v.astype(F32) for v in (ln1_gain, ln1_bias, ln2_gain, ln2_bias)]

    rows_in = gather_tokens(layer_input)
    w_fc1 = gather_weight(fc1_weight)
    cot = gather_tokens(cotangent)
    w_fc2 = gather_weight(fc2_weight.T)
    w_qkv = gather_weight(qkv_weight)
    w_dense = gather_weight(dense_weight.T)
    ids = gather_rows(seq_ids)
    group_len = seq_ids.shape[0]

    def normalize(v):
        v = v.astype(F32)
        center = v - jnp.mean(v, axis=-1, keepdims=True)
        spread = jnp.mean(center * center, axis=-1, keepdims=True)
        scale = lax.rsqrt(spread + 1e-05)
        return center * scale, scale

    xhat, _ = normalize(rows_in)
    normed_attn = (xhat * gains[0] + gains[1]).astype(BF16)
    normed_ffn = (xhat * gains[2] + gains[3]).astype(BF16)

    ffn_input = mm(normed_ffn, w_fc1, NN) + take_block(fc1_bias, 4).astype(F32)
    cdf = 0.5 * (1.0 + lax.erf(ffn_input * (1.0 / math.sqrt(2.0))))
    density = jnp.exp(-0.5 * ffn_input * ffn_input) * (1.0 / math.sqrt(2.0 * math.pi))
    hidden = (ffn_input * cdf).astype(BF16)
    slope = cdf + ffn_input * density
    grad_fc2 = mm(cot, hidden, TN)
    out_fc2 = scatter_grad(grad_fc2).T

    grad_ffn = (mm(cot, w_fc2, NN) * slope).astype(BF16)
    grad_fc1 = mm(normed_ffn, grad_ffn, TN)
    out_fc1 = scatter_grad(grad_fc1)

    qkv = mm(normed_attn, w_qkv, NN) + take_block(qkv_bias, 4).astype(F32)
    qkv = qkv.reshape(4, group_len, 3, HEAD_DIM)
    cosines, sines = turn_angles(ids)
    query = rotary(qkv[:, :, 0], cosines, sines).astype(BF16)
    keys = rotary(qkv[:, :, 1], cosines, sines).astype(BF16)
    values = qkv[:, :, 2].astype(BF16)
    places = jnp.arange(group_len, dtype=jnp.int32)
    allowed = (ids[:, :, None] == ids[:, None, :]) & (places[None, None, :] <= places[None, :, None])
    scores = jnp.einsum("gqd,gkd->gqk", query, keys, preferred_element_type=F32) * 0.0625
    scores = jnp.where(allowed, scores, -1e30)
    weights = jnp.exp(scores - jnp.max(scores, axis=-1, keepdims=True))
    probability = weights / jnp.sum(weights, axis=-1, keepdims=True)
    prob_low = probability.astype(BF16)
    attended = jnp.einsum("gqk,gkd->gqd", prob_low, values, preferred_element_type=F32)
    attended = attended.astype(BF16).reshape(-1, HEAD_DIM)

    partial = mm(attended, w_dense, NT) + mm(hidden, w_fc2, NT)
    branch = scatter_tokens(partial)
    layer_output = (
        layer_input.astype(F32) + branch + dense_bias.astype(F32) + fc2_bias.astype(F32)
    ).astype(BF16)

    grad_dense = mm(cot, attended, TN)
    grad_attended = mm(cot, w_dense, NN).astype(BF16).reshape(4, group_len, HEAD_DIM)
    grad_prob = jnp.einsum("gqd,gkd->gqk", grad_attended, values, preferred_element_type=F32)
    row_dot = jnp.sum(probability * grad_prob, axis=-1, keepdims=True)
    grad_scores = (probability * (grad_prob - row_dot)).astype(BF16)
    grad_query = jnp.einsum("gqk,gkd->gqd", grad_scores, keys, preferred_element_type=F32) * 0.0625
    grad_keys = jnp.einsum("gqk,gqd->gkd", grad_scores, query, preferred_element_type=F32) * 0.0625
    grad_values = jnp.einsum("gqk,gqd->gkd", prob_low, grad_attended, preferred_element_type=F32)
    qkv_grad = jnp.concatenate(
        [
            rotary_back(grad_query, cosines, sines).astype(BF16),
            rotary_back(grad_keys, cosines, sines).astype(BF16),
            grad_values.astype(BF16),
        ],
        axis=-1,
    ).reshape(-1, 3 * HEAD_DIM)
    out_qkv = scatter_grad(mm(normed_attn, qkv_grad, TN))
    out_dense = scatter_grad(grad_dense).T

    attn_part = mm(qkv_grad, w_qkv, NT)
    ffn_part = mm(grad_ffn, w_fc1, NT)
    e_rows = scatter_tokens(attn_part * gains[0] + ffn_part * gains[2])
    own_hat, own_scale = normalize(layer_input)
    cot_rows = cotangent.astype(F32)
    input_grad = cot_rows + own_scale * (
        e_rows
        - jnp.mean(e_rows, axis=-1, keepdims=True)
        - own_hat * jnp.mean(e_rows * own_hat, axis=-1, keepdims=True)
    )

    small = jnp.stack(
        [
            jnp.sum(attn_part * xhat, axis=0),
            jnp.sum(attn_part, axis=0),
            jnp.sum(ffn_part * xhat, axis=0),
            jnp.sum(ffn_part, axis=0),
            jnp.sum(cot_rows, axis=0),
        ]
    )
    small = small + swap_core(small)
    for k in range(bits):
        small = small + swap(small, k)
    columns = jnp.concatenate(
        [jnp.sum(qkv_grad.astype(F32), axis=0), jnp.sum(grad_ffn.astype(F32), axis=0)]
    )
    for k in (BIT_Y,) + zh_bits:
        columns = columns + swap(columns, k)
    columns = ordered(bit[BIT_X], columns, swap(columns, BIT_X), 0)
    columns = ordered(bit[BIT_ZL], columns, swap(columns, BIT_ZL), 0).reshape(4, -1)
    out_qkv_bias = columns[:, : 3 * HEAD_DIM].reshape(-1)
    out_fc1_bias = columns[:, 3 * HEAD_DIM :].reshape(-1)

    return (
        layer_output,
        input_grad,
        small[0],
        small[1],
        small[2],
        small[3],
        out_qkv,
        out_qkv_bias,
        out_dense,
        small[4],
        out_fc1,
        out_fc1_bias,
        out_fc2,
        small[4],
    )


NEAR = (1, 4, 8, 5, 9, 12, 13)


def place():
    return lax.axis_index("dp"), lax.axis_index("tensor")


def feature_of(d):
    return 2 * ((d >> BIT_ZL) & 1) + (d & 1)


def greet(peers):
    barrier = pltpu.get_barrier_semaphore()
    for peer in peers:
        pl.semaphore_signal(barrier, inc=1, device_id=peer, device_id_type=MESH)
    pl.semaphore_wait(barrier, len(peers))


class Copies:
    def __init__(self, local_sems, send_sems, recv_sems):
        self.sems = (local_sems, send_sems, recv_sems)
        self.sent, self.kept = [], []

    def remote(self, source, target, device):
        k = len(self.sent)
        copy = pltpu.make_async_remote_copy(
            src_ref=source,
            dst_ref=target,
            send_sem=self.sems[1].at[k],
            recv_sem=self.sems[2].at[k],
            device_id=device,
            device_id_type=MESH,
        )
        copy.start()
        self.sent.append(copy)
        return copy

    def local(self, source, target):
        copy = pltpu.make_async_copy(source, target, self.sems[0].at[len(self.kept)])
        copy.start()
        self.kept.append(copy)
        return copy

    def finish(self):
        for copy in self.sent:
            copy.wait_send()


GATHER_SEQUENCE = "x0 s1 f1a x1 s2 x2 f1b x3 c0 sq sd f2 c1 c2 fq c3 fd x4 c4"


def gather_kernel(
    x_ref, c_ref, w1, w2, wq, wd, xg, cg, g1, g2, gq, gd, local_sems, send_sems, recv_sems
):
    me, core = place()
    rows = w1.shape[0]
    greet([(me ^ d, core) for d in NEAR] + [(me ^ 2, core), (me, 1 - core)])
    copies = Copies(local_sems, send_sems, recv_sems)
    weights = {"1": (w1, g1, 1), "2": (w2, g2, 0), "q": (wq, gq, 1), "d": (wd, gd, 0)}
    tokens = {"x": (x_ref, xg), "c": (c_ref, cg)}

    def block(w, dim, d):
        size = w.shape[dim] // 4
        cut = pl.ds(feature_of(d) * size, size)
        return w.at[cut, :] if dim == 0 else w.at[:, cut]

    def slot(g, dim, d):
        cut = pl.ds(d * rows, rows)
        return g.at[:, cut] if dim == 0 else g.at[cut, :]

    state, last, kept = {}, [], []
    for step in GATHER_SEQUENCE.split():
        kind, name = step[0], step[1]
        if kind == "s":
            w, g, dim = weights[name]
            kept.append(copies.local(block(w, dim, me), slot(g, dim, me)))
            last.append(copies.remote(block(w, dim, me ^ 2), slot(g, dim, me), (me ^ 2, core)))
            state[name] = [
                copies.remote(block(w, dim, me ^ d), slot(g, dim, me), (me ^ d, core)) for d in NEAR
            ]
        elif kind == "f":
            w, g, dim = weights[name]
            part = {"a": (0, 3), "b": (3, 7)}.get(step[2:], (0, 7))
            for k in range(*part):
                state[name][k].wait_recv()
                held = slot(g, dim, me ^ NEAR[k])
                last.append(copies.remote(held, held, (me ^ 2, core)))
        else:
            source, g = tokens[kind]
            if name == "0":
                kept.append(copies.local(source, g.at[0, core]))
                state[kind] = [
                    copies.remote(source, g.at[2, core], (me ^ 4, core)),
                    copies.remote(source, g.at[1, core], (me ^ 1, core)),
                ]
                last.append(copies.remote(source, g.at[0, core], (me, 1 - core)))
            elif name == "1":
                state[kind][0].wait_recv()
                state[kind].append(copies.remote(g.at[2, core], g.at[3, core], (me ^ 1, core)))
                last.append(copies.remote(g.at[2, core], g.at[2, core], (me, 1 - core)))
            elif name == "2":
                state[kind][1].wait_recv()
                last.append(copies.remote(g.at[1, core], g.at[1, core], (me, 1 - core)))
            elif name == "3":
                state[kind][2].wait_recv()
                last.append(copies.remote(g.at[3, core], g.at[3, core], (me, 1 - core)))
    for copy in last:
        copy.wait_recv()
    for copy in kept:
        copy.wait()
    copies.finish()


def in_hbm(count):
    return [pl.BlockSpec(memory_space=pltpu.HBM)] * count


def gather_all(x, c, w1, w2, wq, wd):
    rows = w1.shape[0]
    n = lax.axis_size("dp")
    shapes = [(4, 2) + x.shape] * 2 + [
        (rows * n, w1.shape[1] // 4),
        (w2.shape[0] // 4, rows * n),
        (rows * n, wq.shape[1] // 4),
        (wd.shape[0] // 4, rows * n),
    ]
    return pl.pallas_call(
        gather_kernel,
        out_shape=[jax.ShapeDtypeStruct(s, BF16) for s in shapes],
        in_specs=in_hbm(6),
        out_specs=in_hbm(6),
        scratch_shapes=[
            pltpu.SemaphoreType.DMA((6,)),
            pltpu.SemaphoreType.DMA((78,)),
            pltpu.SemaphoreType.DMA((78,)),
        ],
        compiler_params=pltpu.CompilerParams(collective_id=1, has_side_effects=True),
        name="gather_all",
    )(x, c, w1, w2, wq, wd)


def scatter_kernel(
    g1, g2, gq, gd, p_out, p_in, vec,
    f1, f2, fq, fd, out_keep, out_got, in_keep, in_got, vec_out,
    r1, r2, rq, rd, s1, s2, sq, sd, a_out, a_in, c_out, c_in, x_out, x_in, vec_got,
    local_sems, send_sems, recv_sems,
):
    me, core = place()
    by, upper = (me >> 1) & 1, me >> 2
    n = lax.axis_size("dp")
    greet([(me ^ d, core) for d in NEAR] + [(me ^ 2, core), (me, 1 - core)])
    copies = Copies(local_sems, send_sems, recv_sems)
    grads = {
        "1": (g1, f1, r1, s1, 0), "2": (g2, f2, r2, s2, 1), "q": (gq, fq, rq, sq, 0), "d": (gd, fd, rd, sd, 1)
    }
    rows = g1.shape[0] // n

    def cut(ref, dim, start, size):
        start = pl.multiple_of(start * size, size)
        return ref.at[pl.ds(start, size), :] if dim == 0 else ref.at[:, pl.ds(start, size)]

    token_sets = {"o": (p_out, out_keep, out_got, a_out, c_out, x_out), "i": (p_in, in_keep, in_got, a_in, c_in, x_in)}
    state = {}
    for name in "oi":
        p, _, _, acc, got, _ = token_sets[name]
        state[name] = (
            [copies.remote(p.at[g, 1 - core], got.at[g], (me, 1 - core)) for g in range(4)],
            [copies.local(p.at[g, core], acc.at[g]) for g in range(4)],
        )
    hops = [(me, 1 - core), (me ^ 2, core), (me ^ 1, core), (me ^ 4, core), (me ^ 8, core)]
    vec_out[...] = vec[...]

    def vector_hop(k):
        copy = copies.remote(vec_out, vec_got.at[k], hops[k])
        copies.sent.pop()
        copies.sent.append(None)
        copy.wait()
        if k == 0:
            vec_out[:8, :] += vec_got[0, :8, :]
        else:
            vec_out[...] += vec_got[k]

    for name in "21qd":
        g, f, r, s, dim = grads[name]
        state[name] = [
            copies.remote(
                cut(g, dim, ((upper ^ u) * 2 + 1 - by), 2 * rows), cut(r, dim, u, 2 * rows), (me ^ 2, core)
            )
            for u in range(4)
        ]
    landed, kept = [], []

    def forward(name):
        g, f, r, s, dim = grads[name]
        for u in (2, 3, 1, 0):
            state[name][u].wait_recv()
            mine = cut(g, dim, (upper ^ u) * 2 + by, 2 * rows)
            total = mine[...].astype(F32) + cut(r, dim, u, 2 * rows)[...].astype(F32)
            cut(s, dim, u, 2 * rows)[...] = total.astype(BF16)
            for x in (1, 0):
                piece = cut(s, dim, u * 2 + ((me & 1) ^ x), rows)
                size = f.shape[2 - dim] // 4
                start = feature_of(me) * size
                target = f.at[me >> 3, :, pl.ds(start, size)] if dim == 0 else f.at[me >> 3, pl.ds(start, size), :]
                if u == 0 and x == 0:
                    kept.append(copies.local(piece, target))
                else:
                    landed.append(copies.remote(piece, target, (me ^ (4 * u + x), core)))

    def tokens_core(name):
        _, _, _, acc, got, over = token_sets[name]
        sent, loaded = state[name]
        for g in (1, 3, 0, 2):
            sent[g].wait_recv()
            loaded[g].wait()
            acc[g] = (acc[g].astype(F32) + got[g].astype(F32)).astype(BF16)
            if g & 1:
                state[name + str(g)] = copies.remote(acc.at[g], over.at[g // 2], (me ^ 1, core))

    def tokens_x(name):
        _, keep, end, acc, got, over = token_sets[name]
        state[name + "3"].wait_recv()
        acc[2] = (acc[2].astype(F32) + over[1].astype(F32)).astype(BF16)
        landed.append(copies.remote(acc.at[2], end, (me ^ 4, core)))
        state[name + "1"].wait_recv()
        acc[0] = (acc[0].astype(F32) + over[0].astype(F32)).astype(BF16)
        kept.append(copies.local(acc.at[0], keep))

    tokens_core("o")
    vector_hop(0)
    forward("2")
    tokens_x("o")
    vector_hop(1)
    tokens_core("i")
    forward("1")
    tokens_x("i")
    vector_hop(2)
    forward("q")
    vector_hop(3)
    forward("d")
    vector_hop(4)
    for copy in landed:
        copy.wait_recv()
    for copy in kept:
        copy.wait()
    for copy in copies.sent:
        if copy is not None:
            copy.wait_send()


def scatter_all(g1, g2, gq, gd, p_out, p_in, vec):
    n = lax.axis_size("dp")
    d_model = p_out.shape[-1]
    rows, tok = d_model // n, p_out.shape[2]
    shapes = [
        (n // 8, rows, 4 * g1.shape[1]),
        (n // 8, 4 * g2.shape[0], rows),
        (n // 8, rows, 4 * gq.shape[1]),
        (n // 8, 4 * gd.shape[0], rows),
    ] + [(tok, d_model)] * 4
    vmem = pl.BlockSpec(memory_space=pltpu.VMEM)
    half = [
        pltpu.VMEM((d_model // 2, g1.shape[1]), BF16),
        pltpu.VMEM((g2.shape[0], d_model // 2), BF16),
        pltpu.VMEM((d_model // 2, gq.shape[1]), BF16),
        pltpu.VMEM((gd.shape[0], d_model // 2), BF16),
    ]
    return pl.pallas_call(
        scatter_kernel,
        out_shape=[jax.ShapeDtypeStruct(s, BF16) for s in shapes]
        + [jax.ShapeDtypeStruct(vec.shape, F32)],
        in_specs=[vmem] * 4 + in_hbm(2) + [vmem],
        out_specs=in_hbm(8) + [vmem],
        scratch_shapes=half
        + half
        + [pltpu.VMEM((4, tok, d_model), BF16)] * 4
        + [pltpu.VMEM((2, tok, d_model), BF16)] * 2
        + [
            pltpu.VMEM((5,) + vec.shape, F32),
            pltpu.SemaphoreType.DMA((20,)),
            pltpu.SemaphoreType.DMA((64,)),
            pltpu.SemaphoreType.DMA((64,)),
        ],
        compiler_params=pltpu.CompilerParams(
            collective_id=2, has_side_effects=True, vmem_limit_bytes=60 << 20
        ),
        name="scatter_all",
    )(g1, g2, gq, gd, p_out, p_in, vec)


def local_fast(
    layer_input,
    ln1_gain,
    ln1_bias,
    ln2_gain,
    ln2_bias,
    qkv_weight,
    qkv_bias,
    dense_weight,
    dense_bias,
    fc1_weight,
    fc1_bias,
    fc2_weight,
    fc2_bias,
    seq_ids,
    cotangent,
):
    me, core = place()
    rows_here, d_model = layer_input.shape
    feature = feature_of(me)

    def swap(v, k):
        return lax.ppermute(v, "dp", [(i, i ^ (1 << k)) for i in range(16)])

    def take_block(v, parts):
        return lax.dynamic_slice_in_dim(v, feature * (v.shape[0] // parts), v.shape[0] // parts, 0)

    gains = [v.astype(F32) for v in (ln1_gain, ln1_bias, ln2_gain, ln2_bias)]
    ids = jnp.stack([seq_ids, swap(seq_ids, BIT_X)], axis=0)
    ids = jnp.concatenate([ids, swap(ids, BIT_ZL)], axis=0)
    group_len = seq_ids.shape[0]
    tokens = 4 * group_len

    xg, cg, w_fc1, w_fc2, w_qkv, w_dense = gather_all(
        layer_input, cotangent, fc1_weight, fc2_weight, qkv_weight, dense_weight
    )
    rows_in = xg.reshape(tokens, d_model)
    cot = cg.reshape(tokens, d_model)

    def normalize(v):
        v = v.astype(F32)
        center = v - jnp.mean(v, axis=-1, keepdims=True)
        spread = jnp.mean(center * center, axis=-1, keepdims=True)
        scale = lax.rsqrt(spread + 1e-05)
        return center * scale, scale

    xhat, _ = normalize(rows_in)
    normed_attn = (xhat * gains[0] + gains[1]).astype(BF16)
    normed_ffn = (xhat * gains[2] + gains[3]).astype(BF16)

    ffn_input = mm(normed_ffn, w_fc1, NN) + take_block(fc1_bias, 4).astype(F32)
    cdf = 0.5 * (1.0 + lax.erf(ffn_input * (1.0 / math.sqrt(2.0))))
    density = jnp.exp(-0.5 * ffn_input * ffn_input) * (1.0 / math.sqrt(2.0 * math.pi))
    hidden = (ffn_input * cdf).astype(BF16)
    slope = cdf + ffn_input * density
    grad_fc2 = mm(hidden, cot, TN).astype(BF16)
    grad_ffn = (mm(cot, w_fc2, NT) * slope).astype(BF16)
    grad_fc1 = mm(normed_ffn, grad_ffn, TN).astype(BF16)

    qkv = mm(normed_attn, w_qkv, NN) + take_block(qkv_bias, 4).astype(F32)
    qkv = qkv.reshape(4, group_len, 3 * HEAD_DIM)
    cosines, sines = turn_angles(ids)
    query = rotary(qkv[:, :, :HEAD_DIM], cosines, sines).astype(BF16)
    keys = rotary(qkv[:, :, HEAD_DIM : 2 * HEAD_DIM], cosines, sines).astype(BF16)
    values = qkv[:, :, 2 * HEAD_DIM :].astype(BF16)
    places = jnp.arange(group_len, dtype=jnp.int32)
    allowed = (ids[:, :, None] == ids[:, None, :]) & (places[None, None, :] <= places[None, :, None])
    scores = jnp.einsum("gqd,gkd->gqk", query, keys, preferred_element_type=F32) * 0.0625
    scores = jnp.where(allowed, scores, -1e30)
    weights = jnp.exp(scores - jnp.max(scores, axis=-1, keepdims=True))
    probability = weights / jnp.sum(weights, axis=-1, keepdims=True)
    prob_low = probability.astype(BF16)
    attended = jnp.einsum("gqk,gkd->gqd", prob_low, values, preferred_element_type=F32)
    attended = attended.astype(BF16).reshape(tokens, HEAD_DIM)

    partial_out = (mm(attended, w_dense, NN) + mm(hidden, w_fc2, NN)).astype(BF16)

    grad_dense = mm(attended, cot, TN).astype(BF16)
    grad_attended = mm(cot, w_dense, NT).astype(BF16).reshape(4, group_len, HEAD_DIM)
    grad_prob = jnp.einsum("gqd,gkd->gqk", grad_attended, values, preferred_element_type=F32)
    row_dot = jnp.sum(probability * grad_prob, axis=-1, keepdims=True)
    grad_scores = (probability * (grad_prob - row_dot)).astype(BF16)
    grad_query = jnp.einsum("gqk,gkd->gqd", grad_scores, keys, preferred_element_type=F32) * 0.0625
    grad_keys = jnp.einsum("gqk,gqd->gkd", grad_scores, query, preferred_element_type=F32) * 0.0625
    grad_values = jnp.einsum("gqk,gqd->gkd", prob_low, grad_attended, preferred_element_type=F32)
    qkv_grad = jnp.concatenate(
        [
            rotary_back(grad_query, cosines, sines).astype(BF16),
            rotary_back(grad_keys, cosines, sines).astype(BF16),
            grad_values.astype(BF16),
        ],
        axis=-1,
    ).reshape(tokens, 3 * HEAD_DIM)
    grad_qkv = mm(normed_attn, qkv_grad, TN).astype(BF16)

    attn_part = mm(qkv_grad, w_qkv, NT)
    ffn_part = mm(grad_ffn, w_fc1, NT)
    partial_in = (attn_part * gains[0] + ffn_part * gains[2]).astype(BF16)
    cot_rows = cotangent.astype(F32)
    small = jnp.stack(
        [
            jnp.sum(attn_part * xhat, axis=0),
            jnp.sum(attn_part, axis=0),
            jnp.sum(ffn_part * xhat, axis=0),
            jnp.sum(ffn_part, axis=0),
            jnp.sum(cot_rows, axis=0),
        ]
    )
    columns = jnp.concatenate(
        [jnp.sum(qkv_grad.astype(F32), axis=0), jnp.sum(grad_ffn.astype(F32), axis=0)]
    )
    columns = jnp.pad(columns, (0, d_model - columns.shape[0]))
    ours = jnp.arange(8)[:, None] == feature
    vec = jnp.concatenate(
        [jnp.pad(small, ((0, 3), (0, 0))), jnp.where(ours, columns[None], 0.0)], axis=0
    )

    f1, f2, fq, fd, out_keep, out_got, in_keep, in_got, vec = scatter_all(
        grad_fc1,
        grad_fc2,
        grad_qkv,
        grad_dense,
        partial_out.reshape(4, 2, rows_here, d_model),
        partial_in.reshape(4, 2, rows_here, d_model),
        vec,
    )
    out_fc1, out_fc2, out_qkv, out_dense = (
        jnp.sum(v.astype(F32), axis=0) for v in (f1, f2, fq, fd)
    )
    layer_output = (
        layer_input.astype(F32)
        + (out_keep.astype(F32) + out_got.astype(F32))
        + dense_bias.astype(F32)
        + fc2_bias.astype(F32)
    ).astype(BF16)
    own_hat, own_scale = normalize(layer_input)
    e_rows = in_keep.astype(F32) + in_got.astype(F32)
    input_grad = cot_rows + own_scale * (
        e_rows
        - jnp.mean(e_rows, axis=-1, keepdims=True)
        - own_hat * jnp.mean(e_rows * own_hat, axis=-1, keepdims=True)
    )
    blocks = vec[8:12]
    out_qkv_bias = blocks[:, : 3 * HEAD_DIM].reshape(-1)
    out_fc1_bias = blocks[:, 3 * HEAD_DIM : 3 * HEAD_DIM + w_fc1.shape[1]].reshape(-1)
    return (
        layer_output,
        input_grad,
        vec[0],
        vec[1],
        vec[2],
        vec[3],
        out_qkv,
        out_qkv_bias,
        out_dense,
        vec[4],
        out_fc1,
        out_fc1_bias,
        out_fc2,
        vec[4],
    )


def solution(mesh):
    local = local_fast if mesh.shape["dp"] == 16 else local_pairs
    in_specs = (
        P(("dp", "tensor"), None),
        P(),
        P(),
        P(),
        P(),
        P("dp", "tensor"),
        P("tensor"),
        P("tensor", "dp"),
        P(),
        P("dp", "tensor"),
        P("tensor"),
        P("tensor", "dp"),
        P(),
        P("dp"),
        P(("dp", "tensor"), None),
    )
    out_specs = (
        P(("dp", "tensor"), None),
        P(("dp", "tensor"), None),
        P(),
        P(),
        P(),
        P(),
        P("dp", "tensor"),
        P("tensor"),
        P("tensor", "dp"),
        P(),
        P("dp", "tensor"),
        P("tensor"),
        P("tensor", "dp"),
        P(),
    )
    return jax.shard_map(local, mesh=mesh, in_specs=in_specs, out_specs=out_specs, check_vma=False)
```

```python
import math

import jax
import jax.numpy as jnp
import numpy as np
from jax import lax
from jax.experimental import pallas as pl
from jax.experimental.pallas import tpu as pltpu
from jax.sharding import PartitionSpec as P

HEAD_DIM = 256
ROT = 64
BIT_X, BIT_Y, BIT_ZL, FIRST_ZH = 0, 1, 2, 3
F32, BF16 = jnp.float32, jnp.bfloat16
MESH = pl.DeviceIdType.MESH
NN = (((1,), (0,)), ((), ()))
NT = (((1,), (1,)), ((), ()))
TN = (((0,), (0,)), ((), ()))


def mm(a, b, dims):
    return lax.dot_general(a, b, dims, preferred_element_type=F32)


def turn_angles(group_ids):
    places = jnp.arange(group_ids.shape[-1], dtype=jnp.int32)
    starts_flag = jnp.concatenate(
        [jnp.ones_like(group_ids[..., :1], dtype=bool), group_ids[..., 1:] != group_ids[..., :-1]],
        axis=-1,
    )
    starts = lax.cummax(jnp.where(starts_flag, places, 0), axis=group_ids.ndim - 1)
    position = (places - starts).astype(F32)
    steps_rot = jnp.arange(ROT // 2, dtype=F32)
    inverse = jnp.exp(steps_rot * (-2.0 * math.log(10000.0) / ROT))
    angles = position[..., None] * inverse
    angles = jnp.concatenate([angles, angles], axis=-1)
    return (jnp.cos(angles), jnp.sin(angles))


def rotary(vectors, cosine_table, sine_table):
    half_rot = ROT // 2
    rot_part = vectors[..., :ROT]
    rot_rest = vectors[..., ROT:]
    turned = jnp.concatenate([-rot_part[..., half_rot:], rot_part[..., :half_rot]], axis=-1)
    rotated = rot_part * cosine_table + turned * sine_table
    return jnp.concatenate([rotated, rot_rest], axis=-1)


def rotary_back(vectors, cosine_table, sine_table):
    half_rot = ROT // 2
    rot_part = vectors[..., :ROT]
    rot_rest = vectors[..., ROT:]
    turned = jnp.concatenate([rot_part[..., half_rot:], -rot_part[..., :half_rot]], axis=-1)
    rotated = rot_part * cosine_table + turned * sine_table
    return jnp.concatenate([rotated, rot_rest], axis=-1)


def local_pairs(
    layer_input,
    ln1_gain,
    ln1_bias,
    ln2_gain,
    ln2_bias,
    qkv_weight,
    qkv_bias,
    dense_weight,
    dense_bias,
    fc1_weight,
    fc1_bias,
    fc2_weight,
    fc2_bias,
    seq_ids,
    cotangent,
):
    n = lax.axis_size("dp")
    bits = n.bit_length() - 1
    me = lax.axis_index("dp")
    core = lax.axis_index("tensor")
    bit = [(me >> k) & 1 for k in range(bits)]
    zh_bits = tuple(range(FIRST_ZH, bits))
    rows_here, d_model = layer_input.shape
    feature = 2 * bit[BIT_ZL] + bit[BIT_X]

    def swap(v, k):
        return lax.ppermute(v, "dp", [(i, i ^ (1 << k)) for i in range(n)])

    def swap_core(v):
        return lax.ppermute(v, "tensor", [(0, 1), (1, 0)])

    def pick(v, b, axis):
        return lax.dynamic_index_in_dim(v, b, axis, keepdims=False)

    def ordered(b, own, other, axis):
        return jnp.stack(
            [jnp.where(b == 0, own, other), jnp.where(b == 0, other, own)], axis=axis
        )

    def gather_rows(v):
        v = jnp.stack([v, swap(v, BIT_ZL)], axis=0)
        v = jnp.concatenate([v, swap(v, BIT_X)], axis=0)
        return v

    def gather_tokens(v):
        v = gather_rows(v)
        return ordered(core, v, swap_core(v), 1).reshape(4 * 2 * rows_here, d_model)

    def scatter_tokens(v):
        v = v.reshape(4, 2, rows_here, d_model)
        keep = pick(v, core, 1)
        v = keep + swap_core(pick(v, 1 - core, 1).astype(BF16))
        v = v[:2] + swap(v[2:].astype(BF16), BIT_X)
        return v[0] + swap(v[1].astype(BF16), BIT_ZL)

    def gather_weight(w):
        rows, width = w.shape
        w = w.reshape(rows, 2, 2, width // 4)
        w = ordered(bit[BIT_X], pick(w, bit[BIT_X], 2), swap(pick(w, 1 - bit[BIT_X], 2), BIT_X), 0)
        w = ordered(bit[BIT_ZL], pick(w, bit[BIT_ZL], 2), swap(pick(w, 1 - bit[BIT_ZL], 2), BIT_ZL), 0)
        for k in zh_bits:
            w = ordered(bit[k], w, swap(w, k), 0)
        w = ordered(bit[BIT_Y], w, swap(w, BIT_Y), w.ndim - 3)
        return w.reshape(rows * n, width // 4)

    def scatter_grad(g):
        rows, width = g.shape[0] // n, g.shape[1]
        g = g.reshape((2,) * bits + (rows, width))
        axis = bits - 1 - BIT_Y
        g = pick(g, bit[BIT_Y], axis) + swap(pick(g, 1 - bit[BIT_Y], axis).astype(BF16), BIT_Y)
        for k in reversed(zh_bits):
            g = pick(g, bit[k], 0) + swap(pick(g, 1 - bit[k], 0).astype(BF16), k)
        g = g.astype(BF16)
        g = ordered(bit[BIT_ZL], pick(g, bit[BIT_ZL], 0), swap(pick(g, 1 - bit[BIT_ZL], 0), BIT_ZL), 2)
        g = ordered(bit[BIT_X], pick(g, bit[BIT_X], 0), swap(pick(g, 1 - bit[BIT_X], 0), BIT_X), 2)
        return g.reshape(rows, 4 * width).astype(F32)

    def take_block(v, parts):
        return lax.dynamic_slice_in_dim(v, feature * (v.shape[0] // parts), v.shape[0] // parts, 0)

    gains = [v.astype(F32) for v in (ln1_gain, ln1_bias, ln2_gain, ln2_bias)]

    rows_in = gather_tokens(layer_input)
    w_fc1 = gather_weight(fc1_weight)
    cot = gather_tokens(cotangent)
    w_fc2 = gather_weight(fc2_weight.T)
    w_qkv = gather_weight(qkv_weight)
    w_dense = gather_weight(dense_weight.T)
    ids = gather_rows(seq_ids)
    group_len = seq_ids.shape[0]

    def normalize(v):
        v = v.astype(F32)
        center = v - jnp.mean(v, axis=-1, keepdims=True)
        spread = jnp.mean(center * center, axis=-1, keepdims=True)
        scale = lax.rsqrt(spread + 1e-05)
        return center * scale, scale

    xhat, _ = normalize(rows_in)
    normed_attn = (xhat * gains[0] + gains[1]).astype(BF16)
    normed_ffn = (xhat * gains[2] + gains[3]).astype(BF16)

    ffn_input = mm(normed_ffn, w_fc1, NN) + take_block(fc1_bias, 4).astype(F32)
    cdf = 0.5 * (1.0 + lax.erf(ffn_input * (1.0 / math.sqrt(2.0))))
    density = jnp.exp(-0.5 * ffn_input * ffn_input) * (1.0 / math.sqrt(2.0 * math.pi))
    hidden = (ffn_input * cdf).astype(BF16)
    slope = cdf + ffn_input * density
    grad_fc2 = mm(cot, hidden, TN)
    out_fc2 = scatter_grad(grad_fc2).T

    grad_ffn = (mm(cot, w_fc2, NN) * slope).astype(BF16)
    grad_fc1 = mm(normed_ffn, grad_ffn, TN)
    out_fc1 = scatter_grad(grad_fc1)

    qkv = mm(normed_attn, w_qkv, NN) + take_block(qkv_bias, 4).astype(F32)
    qkv = qkv.reshape(4, group_len, 3, HEAD_DIM)
    cosines, sines = turn_angles(ids)
    query = rotary(qkv[:, :, 0], cosines, sines).astype(BF16)
    keys = rotary(qkv[:, :, 1], cosines, sines).astype(BF16)
    values = qkv[:, :, 2].astype(BF16)
    places = jnp.arange(group_len, dtype=jnp.int32)
    allowed = (ids[:, :, None] == ids[:, None, :]) & (places[None, None, :] <= places[None, :, None])
    scores = jnp.einsum("gqd,gkd->gqk", query, keys, preferred_element_type=F32) * 0.0625
    scores = jnp.where(allowed, scores, -1e30)
    weights = jnp.exp(scores - jnp.max(scores, axis=-1, keepdims=True))
    probability = weights / jnp.sum(weights, axis=-1, keepdims=True)
    prob_low = probability.astype(BF16)
    attended = jnp.einsum("gqk,gkd->gqd", prob_low, values, preferred_element_type=F32)
    attended = attended.astype(BF16).reshape(-1, HEAD_DIM)

    partial = mm(attended, w_dense, NT) + mm(hidden, w_fc2, NT)
    branch = scatter_tokens(partial)
    layer_output = (
        layer_input.astype(F32) + branch + dense_bias.astype(F32) + fc2_bias.astype(F32)
    ).astype(BF16)

    grad_dense = mm(cot, attended, TN)
    grad_attended = mm(cot, w_dense, NN).astype(BF16).reshape(4, group_len, HEAD_DIM)
    grad_prob = jnp.einsum("gqd,gkd->gqk", grad_attended, values, preferred_element_type=F32)
    row_dot = jnp.sum(probability * grad_prob, axis=-1, keepdims=True)
    grad_scores = (probability * (grad_prob - row_dot)).astype(BF16)
    grad_query = jnp.einsum("gqk,gkd->gqd", grad_scores, keys, preferred_element_type=F32) * 0.0625
    grad_keys = jnp.einsum("gqk,gqd->gkd", grad_scores, query, preferred_element_type=F32) * 0.0625
    grad_values = jnp.einsum("gqk,gqd->gkd", prob_low, grad_attended, preferred_element_type=F32)
    qkv_grad = jnp.concatenate(
        [
            rotary_back(grad_query, cosines, sines).astype(BF16),
            rotary_back(grad_keys, cosines, sines).astype(BF16),
            grad_values.astype(BF16),
        ],
        axis=-1,
    ).reshape(-1, 3 * HEAD_DIM)
    out_qkv = scatter_grad(mm(normed_attn, qkv_grad, TN))
    out_dense = scatter_grad(grad_dense).T

    attn_part = mm(qkv_grad, w_qkv, NT)
    ffn_part = mm(grad_ffn, w_fc1, NT)
    e_rows = scatter_tokens(attn_part * gains[0] + ffn_part * gains[2])
    own_hat, own_scale = normalize(layer_input)
    cot_rows = cotangent.astype(F32)
    input_grad = cot_rows + own_scale * (
        e_rows
        - jnp.mean(e_rows, axis=-1, keepdims=True)
        - own_hat * jnp.mean(e_rows * own_hat, axis=-1, keepdims=True)
    )

    small = jnp.stack(
        [
            jnp.sum(attn_part * xhat, axis=0),
            jnp.sum(attn_part, axis=0),
            jnp.sum(ffn_part * xhat, axis=0),
            jnp.sum(ffn_part, axis=0),
            jnp.sum(cot_rows, axis=0),
        ]
    )
    small = small + swap_core(small)
    for k in range(bits):
        small = small + swap(small, k)
    columns = jnp.concatenate(
        [jnp.sum(qkv_grad.astype(F32), axis=0), jnp.sum(grad_ffn.astype(F32), axis=0)]
    )
    for k in (BIT_Y,) + zh_bits:
        columns = columns + swap(columns, k)
    columns = ordered(bit[BIT_X], columns, swap(columns, BIT_X), 0)
    columns = ordered(bit[BIT_ZL], columns, swap(columns, BIT_ZL), 0).reshape(4, -1)
    out_qkv_bias = columns[:, : 3 * HEAD_DIM].reshape(-1)
    out_fc1_bias = columns[:, 3 * HEAD_DIM :].reshape(-1)

    return (
        layer_output,
        input_grad,
        small[0],
        small[1],
        small[2],
        small[3],
        out_qkv,
        out_qkv_bias,
        out_dense,
        small[4],
        out_fc1,
        out_fc1_bias,
        out_fc2,
        small[4],
    )


NEAR = (1, 4, 8, 5, 9, 12, 13)
FAR_FIRST = (2, 3, 1, 0)
TILE = 256
ORDER = """
g0 x0 s1 L0o f1a x1 x2 c0 s2 L2o L1o f1b x3 L3o L0p c1 c2 L2p L1p L3p W1 Pa f2a c3 Pb f2b sq sd C
G2 W2 H fq G1 fd r2 A0 r1 A2 Gd Gq o0 rd rq o1 o2 i0 i1 i2 v
"""


def place():
    return lax.axis_index("dp"), lax.axis_index("tensor")


def feature_of(d):
    return 2 * ((d >> BIT_ZL) & 1) + (d & 1)


def greet(peers):
    barrier = pltpu.get_barrier_semaphore()
    for peer in peers:
        pl.semaphore_signal(barrier, inc=1, device_id=peer, device_id_type=MESH)
    pl.semaphore_wait(barrier, len(peers))


class Copies:
    def __init__(self, local_sems, send_sems, recv_sems):
        self.sems = (local_sems, send_sems, recv_sems)
        self.count, self.open, self.locals = 0, [], 0

    def remote(self, source, target, device):
        copy = pltpu.make_async_remote_copy(
            src_ref=source,
            dst_ref=target,
            send_sem=self.sems[1].at[self.count],
            recv_sem=self.sems[2].at[self.count],
            device_id=device,
            device_id_type=MESH,
        )
        copy.start()
        self.count += 1
        self.open.append(copy)
        return copy

    def local(self, source, target):
        copy = pltpu.make_async_copy(source, target, self.sems[0].at[self.locals])
        copy.start()
        self.locals += 1
        return copy

    def now(self, *pairs):
        for copy in [self.local(*pair) for pair in pairs]:
            copy.wait()

    def finish(self):
        for copy in self.open:
            copy.wait_send()


def rows_at(start, size):
    return pl.ds(pl.multiple_of(start * size, size), size)


def fold(v):
    return jnp.sum(v.reshape(v.shape[0] // 8, 8, v.shape[1]), axis=0)


def rope(v, tables, sign):
    first = v[:, :128]
    turned = pltpu.roll(first, 96, 1) * tables[1] + pltpu.roll(first, 32, 1) * tables[2]
    return jnp.concatenate([first * tables[0] + sign * turned, v[:, 128:]], axis=1)


def layer_kernel(
    x_ref, c_ref, w1, w2, wq, wd, flag, norms, turns,
    f1, f2, fq, fd, out_keep, out_got, in_keep, in_got, vec,
    xg, cg, g1, g2, gq, gd, na, r1, r2, rq, rd, co, ci, xo, xi, flags,
    big1, big2, wa, wb, wqv, wdv, hid, gf, qkv, att, d1, d2, dq, dd, xt, st, stats, sums, cols, vec_got, fl,
    local_sems, send_sems, recv_sems,
):
    me, core = place()
    by, upper, mine = (me >> 1) & 1, me >> 2, feature_of(me)
    rows = w1.shape[0]
    d_model = x_ref.shape[1]
    greet([(me ^ d, core) for d in NEAR] + [(me ^ 2, core), (me, 1 - core)])
    copies = Copies(local_sems, send_sems, recv_sems)
    weights = {"1": (w1, g1, 1), "2": (w2, g2, 0), "q": (wq, gq, 1), "d": (wd, gd, 0)}
    tokens = {"x": (x_ref, xg), "c": (c_ref, cg)}
    grads = {"1": (d1, f1, r1, 0), "2": (d2, f2, r2, 1), "q": (dq, fq, rq, 0), "d": (dd, fd, rd, 1)}
    state, kept, landed = {}, [], []
    pieces = {name: [] for name in weights}

    def block(w, dim, d):
        size = w.shape[dim] // 4
        cut = pl.ds(feature_of(d) * size, size)
        return w.at[cut, :] if dim == 0 else w.at[:, cut]

    def slot(g, dim, d):
        cut = pl.ds(d * rows, rows)
        return g.at[:, cut] if dim == 0 else g.at[cut, :]

    def send_flag():
        kept.append(copies.local(flag, flags.at[0]))
        state["flags"] = [copies.remote(flag, flags.at[k], (me ^ d, core)) for k, d in ((1, 1), (2, 4), (3, 5))]

    def send_weight(name):
        w, g, dim = weights[name]
        pieces[name].append(copies.local(block(w, dim, me), slot(g, dim, me)))
        pieces[name].append(copies.remote(block(w, dim, me ^ 2), slot(g, dim, me), (me ^ 2, core)))
        state[name] = [copies.remote(block(w, dim, me ^ d), slot(g, dim, me), (me ^ d, core)) for d in NEAR]

    def forward_weight(name, part):
        w, g, dim = weights[name]
        for k in range(*{"a": (0, 3), "b": (3, 7)}.get(part, (0, 7))):
            state[name][k].wait_recv()
            held = slot(g, dim, me ^ NEAR[k])
            pieces[name].append(copies.remote(held, held, (me ^ 2, core)))

    def weight_ready(name):
        for copy in pieces[name]:
            if copy is pieces[name][0]:
                copy.wait()
            else:
                copy.wait_recv()

    def token_step(kind, step):
        source, g = tokens[kind]
        if step == "0":
            state[kind] = [
                copies.remote(source, g.at[2, core], (me ^ 4, core)),
                copies.remote(source, g.at[1, core], (me ^ 1, core)),
            ]
            state[kind + "p0"] = copies.remote(source, g.at[0, core], (me, 1 - core))
        elif step == "1":
            state[kind][0].wait_recv()
            state[kind].append(copies.remote(g.at[2, core], g.at[3, core], (me ^ 1, core)))
            state[kind + "p2"] = copies.remote(g.at[2, core], g.at[2, core], (me, 1 - core))
        elif step == "2":
            state[kind][1].wait_recv()
            state[kind + "p1"] = copies.remote(g.at[1, core], g.at[1, core], (me, 1 - core))
        elif step == "3":
            state[kind][2].wait_recv()
            state[kind + "p3"] = copies.remote(g.at[3, core], g.at[3, core], (me, 1 - core))

    def normalize(rel, half):
        if half == "o":
            which = core
            copies.now((x_ref if rel == 0 else xg.at[rel, core], xt.at[0]))
        else:
            which = 1 - core
            state["xp%d" % rel].wait_recv()
            copies.now((xg.at[rel, which], xt.at[0]))
        tile = rel * 2 + which

        @pl.loop(0, TILE // 32)
        def _(k):
            r = rows_at(k, 32)
            here = rows_at(tile * (TILE // 32) + k, 32)
            v = xt[0, r, :].astype(F32)
            mean = jnp.mean(v, axis=-1, keepdims=True)
            center = v - mean
            scale = lax.rsqrt(jnp.mean(center * center, axis=-1, keepdims=True) + 1e-05)
            xhat = center * scale
            xt[1, r, :] = (xhat * norms[0:1, :] + norms[1:2, :]).astype(BF16)
            big1[here, :] = (xhat * norms[2:3, :] + norms[3:4, :]).astype(BF16)
            stats[here, 0:1] = mean
            stats[here, 1:2] = scale

        copies.now((xt.at[1], na.at[rows_at(tile, TILE), :]))

    def up(lo, hi):
        @pl.loop(lo, hi)
        def _(i):
            r = rows_at(i, TILE)
            for j in range(0, wa.shape[1], 512):
                c = slice(j, j + 512)
                v = mm(big1[r, :], wa[:, c], NN) + norms[4:5, c]
                cdf = 0.5 * (1.0 + lax.erf(v * (1.0 / math.sqrt(2.0))))
                density = jnp.exp(-0.5 * v * v) * (1.0 / math.sqrt(2.0 * math.pi))
                hid[r, c] = (v * cdf).astype(BF16)
                gf[r, c] = (cdf + v * density).astype(BF16)

    def load_cotangent():
        for k in range(4):
            state["cp%d" % k].wait_recv()
        pairs = [(c_ref, big2.at[rows_at(core, TILE), :])]
        pairs += [(cg.at[0, 1 - core], big2.at[rows_at(1 - core, TILE), :])]
        pairs += [
            (cg.at[k, h], big2.at[(k * 2 + h) * TILE : (k * 2 + h + 1) * TILE, :])
            for k in (1, 2, 3)
            for h in (0, 1)
        ]
        copies.now(*pairs)

        @pl.loop(0, TILE // 32)
        def _(k):
            part = fold(big2[rows_at(core * (TILE // 32) + k, 32), :].astype(F32))
            sums[4] = jnp.where(k == 0, part, sums[4] + part)

    def cut(ref, dim, start, size):
        start = pl.multiple_of(start * size, size)
        return ref.at[pl.ds(start, size), :] if dim == 0 else ref.at[:, pl.ds(start, size)]

    def send_grad(name):
        d, f, r, dim = grads[name]

        def product(pair):
            c = rows_at(pair, 2 * rows)
            if name == "1":
                d[c, :] = mm(big1[:, c], gf[...], TN).astype(BF16)
            elif name == "q":
                d[c, :] = mm(big1[:, c], qkv[...], TN).astype(BF16)
            elif name == "2":
                for j in (0, 512):
                    d[j : j + 512, c] = mm(hid[:, j : j + 512], big2[:, c], TN).astype(BF16)
            else:
                d[:, c] = mm(att[...], big2[:, c], TN).astype(BF16)

        state["r" + name] = {}
        for u in FAR_FIRST:
            pair = (upper ^ u) * 2 + 1 - by
            product(pair)
            state["r" + name][u] = copies.remote(
                cut(d, dim, pair, 2 * rows), cut(r, dim, u, 2 * rows), (me ^ 2, core)
            )

        @pl.loop(0, 4)
        def _(u):
            product(u * 2 + by)

    def forward_grad(name):
        d, f, r, dim = grads[name]
        for u in FAR_FIRST:
            state["r" + name][u].wait_recv()
            own = cut(d, dim, (upper ^ u) * 2 + by, 2 * rows)
            if name == "2":
                stage = st
            else:
                stage = xt.at[0, :, pl.ds(0, d.shape[1] if dim == 0 else 2 * rows)]
            copies.now((cut(r, dim, u, 2 * rows), stage))
            own[...] = (own[...].astype(F32) + stage[...].astype(F32)).astype(BF16)
            for x in (1, 0):
                piece = cut(d, dim, (upper ^ u) * 4 + by * 2 + ((me & 1) ^ x), rows)
                size = f.shape[2 - dim] // 4
                c = pl.ds(mine * size, size)
                target = f.at[me >> 3, :, c] if dim == 0 else f.at[me >> 3, c, :]
                if u == 0 and x == 0:
                    kept.append(copies.local(piece, target))
                else:
                    landed.append(copies.remote(piece, target, (me ^ (4 * u + x), core)))

    def hidden_grad():
        cols[...] = jnp.zeros_like(cols)

        @pl.loop(0, 8)
        def _(i):
            r = rows_at(i, TILE)
            for j in range(0, gf.shape[1], 512):
                c = slice(j, j + 512)
                g = (mm(big2[r, :], wb[c, :], NT) * gf[r, c].astype(F32)).astype(BF16)
                gf[r, c] = g
                at = slice(3 * HEAD_DIM + j, 3 * HEAD_DIM + j + 512)
                cols[:, at] += fold(g.astype(F32))

    def attention(lo, hi):
        @pl.loop(lo, hi)
        def _(number):
            attend(number)

    def attend(number):
        size, half = 2 * TILE, TILE
        quarter = size // 4

        def at_rows(start, length):
            return pl.ds(pl.multiple_of(number * size + start, TILE), length)

        three = fl[number, 0:1, 0:1] > 0.5
        tables = []
        for k in range(3):
            again = jnp.concatenate([turns[k, :quarter], turns[k, : 2 * quarter], turns[k, :quarter]], axis=0)
            tables.append(jnp.where(three, again, turns[k]))
        everything = at_rows(0, size)
        full = mm(big1[everything, :], wqv[...], NN) + norms[5:6, : 3 * HEAD_DIM]
        qkv[everything, :HEAD_DIM] = rope(full[:, :HEAD_DIM], tables, 1.0).astype(BF16)
        qkv[everything, HEAD_DIM : 2 * HEAD_DIM] = rope(full[:, HEAD_DIM : 2 * HEAD_DIM], tables, 1.0).astype(BF16)
        qkv[everything, 2 * HEAD_DIM :] = full[:, 2 * HEAD_DIM :].astype(BF16)
        grad_q, grad_k, grad_v = {}, {}, {}
        for i in (1, 0):
            r = at_rows(i * half, half)
            seen = (i + 1) * half
            q = qkv[r, :HEAD_DIM]
            k = qkv[at_rows(0, seen), HEAD_DIM : 2 * HEAD_DIM]
            v = qkv[at_rows(0, seen), 2 * HEAD_DIM :]
            ti = lax.broadcasted_iota(jnp.int32, (half, seen), 0) + i * half
            tj = lax.broadcasted_iota(jnp.int32, (half, seen), 1)
            part_i = (ti >= quarter).astype(jnp.int32) + (ti >= 3 * quarter).astype(jnp.int32)
            part_j = (tj >= quarter).astype(jnp.int32) + (tj >= 3 * quarter).astype(jnp.int32)
            s = mm(q, k, NT) * 0.0625
            s = jnp.where(tj <= ti, s, -1e30)
            s = jnp.where((part_i != part_j) & three, -1e30, s)
            w = jnp.exp(s - jnp.max(s, axis=-1, keepdims=True))
            p = w / jnp.sum(w, axis=-1, keepdims=True)
            low = p.astype(BF16)
            att[r, :] = mm(low, v, NN).astype(BF16)
            ga = mm(big2[r, :], wdv[...], NT).astype(BF16)
            gp = mm(ga, v, NT)
            gs = (p * (gp - jnp.sum(p * gp, axis=-1, keepdims=True))).astype(BF16)
            grad_q[i] = mm(gs, k, NN) * 0.0625
            grad_k[i] = mm(gs, q, TN) * 0.0625
            grad_v[i] = mm(low, ga, TN)

        def put(k, total):
            total = total.astype(BF16)
            at = slice(k * HEAD_DIM, (k + 1) * HEAD_DIM)
            qkv[everything, at] = total
            cols[:, at] += fold(total.astype(F32))

        def joined(one, two):
            return jnp.concatenate([one + two[:half], two[half:]], axis=0)

        put(0, rope(jnp.concatenate([grad_q[0], grad_q[1]], axis=0), tables, -1.0))
        put(1, rope(joined(grad_k[0], grad_k[1]), tables, -1.0))
        put(2, joined(grad_v[0], grad_v[1]))

    sets = {"o": (out_keep, out_got, big1, co, xo), "i": (in_keep, in_got, big2, ci, xi)}

    def token_product(name, rel, which, buffer, at, received):
        tile = rel * 2 + which
        r = rows_at(tile, TILE)
        if name == "i":
            copies.now((x_ref if rel == 0 and received else xg.at[rel, which], xt.at[0]))

        @pl.loop(0, d_model // 512)
        def _(j):
            c = rows_at(j, 512)
            if name == "o":
                total = mm(att[r, :], wdv[:, c], NN) + mm(hid[r, :], wb[:, c], NN)
            else:
                a = mm(qkv[r, :], wqv[c, :], NT)
                f = mm(gf[r, :], wa[c, :], NT)
                xhat = (xt[0, :, c].astype(F32) - stats[r, 0:1]) * stats[r, 1:2]
                sums[0, :, c] += fold(a * xhat)
                sums[1, :, c] += fold(a)
                sums[2, :, c] += fold(f * xhat)
                sums[3, :, c] += fold(f)
                total = a * norms[0:1, c] + f * norms[2:3, c]
            if received:
                total = total + xt[1, :, c].astype(F32)
            buffer[at * TILE : (at + 1) * TILE, c] = total.astype(BF16)

    def tile_of(buffer, at):
        return buffer.at[at * TILE : (at + 1) * TILE, :]

    def token_sum(name, step):
        keep, end, buffer, got, over = sets[name]
        if step == "0":
            if name == "i":
                sums[0:4] = jnp.zeros_like(sums[0:4])
            state[name] = {}
            for rel in (1, 3, 2, 0):
                token_product(name, rel, 1 - core, buffer, rel, False)
                state[name][rel] = copies.remote(tile_of(buffer, rel), got.at[rel], (me, 1 - core))
        elif step == "1":
            for rel in (3, 1, 2, 0):
                state[name][rel].wait_recv()
                copies.now((got.at[rel], xt.at[1]))
                token_product(name, rel, core, buffer, 4 + rel, True)
                if rel & 1:
                    state[name + str(rel)] = copies.remote(
                        tile_of(buffer, 4 + rel), over.at[rel // 2], (me ^ 1, core)
                    )
        else:
            for rel in (2, 0):
                state[name + str(rel + 1)].wait_recv()
                copies.now((over.at[rel // 2], xt.at[1]))

                @pl.loop(0, TILE // 32)
                def _(k):
                    r = rows_at((4 + rel) * (TILE // 32) + k, 32)
                    buffer[r, :] = (
                        buffer[r, :].astype(F32) + xt[1, rows_at(k, 32), :].astype(F32)
                    ).astype(BF16)

                if rel == 2:
                    landed.append(copies.remote(tile_of(buffer, 6), end, (me ^ 4, core)))
                else:
                    kept.append(copies.local(tile_of(buffer, 4), keep))

    def vectors():
        vec[...] = jnp.zeros_like(vec)
        for k in range(5):
            vec[k : k + 1, :] = jnp.sum(sums[k], axis=0, keepdims=True)
        for k in range(4):
            ours = jnp.where(mine == k, 1.0, 0.0)
            vec[8 + k : 9 + k, :] = jnp.sum(cols[...], axis=0, keepdims=True) * ours
        hops = [(me, 1 - core), (me ^ 2, core), (me ^ 1, core), (me ^ 4, core), (me ^ 8, core)]
        for k, device in enumerate(hops):
            copy = copies.remote(vec, vec_got.at[k], device)
            copies.open.pop()
            copy.wait()
            if k == 0:
                vec[:8, :] += vec_got[0, :8, :]
            else:
                vec[...] += vec_got[k]

    for op in ORDER.split():
        kind, rest = op[0], op[1:]
        if kind == "g":
            send_flag()
        elif kind in "xc":
            token_step(kind, rest)
        elif kind == "s":
            send_weight(rest)
        elif kind == "f":
            forward_weight(rest[0], rest[1:])
        elif kind == "L":
            normalize(int(rest[0]), rest[1])
        elif kind == "W":
            weight_ready(rest)
            copies.now((g1, wa) if rest == "1" else (g2, wb))
        elif kind == "P":
            up(*((0, 4) if rest == "a" else (4, 8)))
        elif kind == "C":
            load_cotangent()
        elif kind == "G":
            send_grad(rest)
        elif kind == "H":
            hidden_grad()
        elif kind == "r":
            forward_grad(rest)
        elif kind == "A":
            if rest == "0":
                for name in "qd":
                    weight_ready(name)
                for copy in state["flags"]:
                    copy.wait_recv()
                kept.pop(0).wait()
                copies.now((gq, wqv), (gd, wdv), (na, big1), (flags, fl))
            attention(int(rest), int(rest) + 2)
        elif kind in "oi":
            token_sum(kind, rest)
        else:
            vectors()
    for copy in landed:
        copy.wait_recv()
    for copy in kept:
        copy.wait()
    copies.finish()


def turn_tables(group_len):
    inverse = np.exp(
        np.arange(ROT // 2, dtype=np.float32) * np.float32(-2.0 * math.log(10000.0) / ROT)
    ).astype(np.float32)
    angles = np.arange(group_len).astype(np.float32)[:, None] * inverse
    tables = np.zeros((3, group_len, 128), np.float32)
    tables[0] = 1.0
    tables[0, :, : ROT // 2] = tables[0, :, ROT // 2 : ROT] = np.cos(angles)
    tables[1, :, : ROT // 2] = -np.sin(angles)
    tables[2, :, ROT // 2 : ROT] = np.sin(angles)
    return tables


def layer_call(x, c, w1, w2, wq, wd, flag, norms, turns):
    n = lax.axis_size("dp")
    tok, d = x.shape
    rows, u1, uq, ud = w1.shape[0], w1.shape[1] // 4, wq.shape[1] // 4, wd.shape[0] // 4
    many = 8 * tok
    vmem = pl.BlockSpec(memory_space=pltpu.VMEM)
    hbm = pl.BlockSpec(memory_space=pltpu.HBM)

    def low(*shape):
        return jax.ShapeDtypeStruct(shape, BF16)

    results = [low(n // 8, rows, 4 * u1), low(n // 8, 4 * u1, rows), low(n // 8, rows, 4 * uq), low(n // 8, 4 * ud, rows)]
    results += [low(tok, d)] * 4 + [jax.ShapeDtypeStruct((16, d), F32)]
    spare = [low(4, 2, tok, d)] * 2 + [low(d, u1), low(u1, d), low(d, uq), low(ud, d), low(many, d)]
    spare += [low(d // 2, u1), low(u1, d // 2), low(d // 2, uq), low(ud, d // 2)]
    spare += [low(4, tok, d)] * 2 + [low(2, tok, d)] * 2 + [jax.ShapeDtypeStruct((4, 8, 128), F32)]
    scratch = [
        (many, d), (many, d), (d, u1), (u1, d), (d, uq), (ud, d), (many, u1), (many, u1), (many, uq), (many, ud),
        (d, u1), (u1, d), (d, uq), (ud, d), (2, tok, d), (u1, 2 * rows),
    ]
    flops = 2 * 3 * many * d * (2 * u1 + uq + ud)
    return pl.pallas_call(
        layer_kernel,
        out_shape=results + spare,
        in_specs=[hbm] * 7 + [vmem] * 2,
        out_specs=[hbm] * 8 + [vmem] + [hbm] * len(spare),
        scratch_shapes=[pltpu.VMEM(s, BF16) for s in scratch]
        + [
            pltpu.VMEM((many, 2), F32),
            pltpu.VMEM((5, 8, d), F32),
            pltpu.VMEM((8, d), F32),
            pltpu.VMEM((5, 16, d), F32),
            pltpu.VMEM((4, 8, 128), F32),
            pltpu.SemaphoreType.DMA((96,)),
            pltpu.SemaphoreType.DMA((144,)),
            pltpu.SemaphoreType.DMA((144,)),
        ],
        compiler_params=pltpu.CompilerParams(
            collective_id=1, has_side_effects=True, vmem_limit_bytes=65000 << 10
        ),
        cost_estimate=pl.CostEstimate(flops=flops, bytes_accessed=200 << 20, transcendentals=0),
        name="layer",
    )(x, c, w1, w2, wq, wd, flag, norms, turns)[:9]


def local_fast(
    layer_input,
    ln1_gain,
    ln1_bias,
    ln2_gain,
    ln2_bias,
    qkv_weight,
    qkv_bias,
    dense_weight,
    dense_bias,
    fc1_weight,
    fc1_bias,
    fc2_weight,
    fc2_bias,
    seq_ids,
    cotangent,
):
    me, core = place()
    rows_here, d_model = layer_input.shape
    feature = feature_of(me)
    units, width = fc1_weight.shape[1] // 4, 3 * HEAD_DIM

    def take_block(v, size):
        return jnp.pad(lax.dynamic_slice_in_dim(v, feature * size, size, 0), (0, d_model - size))

    zero = jnp.zeros_like(ln1_gain)
    norms = jnp.stack(
        [ln1_gain, ln1_bias, ln2_gain, ln2_bias, take_block(fc1_bias, units), take_block(qkv_bias, width), zero, zero]
    ).astype(F32)
    flag = jnp.broadcast_to(jnp.max(seq_ids) > 0, (8, 128)).astype(F32)
    f1, f2, fq, fd, out_keep, out_got, in_keep, in_got, vec = layer_call(
        layer_input,
        cotangent,
        fc1_weight,
        fc2_weight,
        qkv_weight,
        dense_weight,
        flag,
        norms,
        turn_tables(seq_ids.shape[0]),
    )
    out_fc1, out_fc2, out_qkv, out_dense = (
        jnp.sum(v.astype(F32), axis=0) for v in (f1, f2, fq, fd)
    )
    own = layer_input.astype(F32)
    layer_output = (
        own
        + (out_keep.astype(F32) + out_got.astype(F32))
        + dense_bias.astype(F32)
        + fc2_bias.astype(F32)
    ).astype(BF16)
    center = own - jnp.mean(own, axis=-1, keepdims=True)
    scale = lax.rsqrt(jnp.mean(center * center, axis=-1, keepdims=True) + 1e-05)
    xhat = center * scale
    e_rows = in_keep.astype(F32) + in_got.astype(F32)
    input_grad = cotangent.astype(F32) + scale * (
        e_rows
        - jnp.mean(e_rows, axis=-1, keepdims=True)
        - xhat * jnp.mean(e_rows * xhat, axis=-1, keepdims=True)
    )
    blocks = vec[8:12]
    out_qkv_bias = blocks[:, :width].reshape(-1)
    out_fc1_bias = blocks[:, width : width + units].reshape(-1)
    return (
        layer_output,
        input_grad,
        vec[0],
        vec[1],
        vec[2],
        vec[3],
        out_qkv,
        out_qkv_bias,
        out_dense,
        vec[4],
        out_fc1,
        out_fc1_bias,
        out_fc2,
        vec[4],
    )


def solution(mesh):
    local = local_fast if mesh.shape["dp"] == 16 else local_pairs
    in_specs = (
        P(("dp", "tensor"), None),
        P(),
        P(),
        P(),
        P(),
        P("dp", "tensor"),
        P("tensor"),
        P("tensor", "dp"),
        P(),
        P("dp", "tensor"),
        P("tensor"),
        P("tensor", "dp"),
        P(),
        P("dp"),
        P(("dp", "tensor"), None),
    )
    out_specs = (
        P(("dp", "tensor"), None),
        P(("dp", "tensor"), None),
        P(),
        P(),
        P(),
        P(),
        P("dp", "tensor"),
        P("tensor"),
        P("tensor", "dp"),
        P(),
        P("dp", "tensor"),
        P("tensor"),
        P("tensor", "dp"),
        P(),
    )
    return jax.shard_map(local, mesh=mesh, in_specs=in_specs, out_specs=out_specs, check_vma=False)
```

```python
import math

import jax
import jax.numpy as jnp
import numpy as np
from jax import lax
from jax.experimental import pallas as pl
from jax.experimental.pallas import tpu as pltpu
from jax.sharding import PartitionSpec as P

HEAD_DIM = 256
ROT = 64
BIT_X, BIT_Y, BIT_ZL, FIRST_ZH = 0, 1, 2, 3
F32, BF16 = jnp.float32, jnp.bfloat16
MESH = pl.DeviceIdType.MESH
NN = (((1,), (0,)), ((), ()))
NT = (((1,), (1,)), ((), ()))
TN = (((0,), (0,)), ((), ()))


def mm(a, b, dims):
    return lax.dot_general(a, b, dims, preferred_element_type=F32)


def turn_angles(group_ids):
    places = jnp.arange(group_ids.shape[-1], dtype=jnp.int32)
    starts_flag = jnp.concatenate(
        [jnp.ones_like(group_ids[..., :1], dtype=bool), group_ids[..., 1:] != group_ids[..., :-1]],
        axis=-1,
    )
    starts = lax.cummax(jnp.where(starts_flag, places, 0), axis=group_ids.ndim - 1)
    position = (places - starts).astype(F32)
    steps_rot = jnp.arange(ROT // 2, dtype=F32)
    inverse = jnp.exp(steps_rot * (-2.0 * math.log(10000.0) / ROT))
    angles = position[..., None] * inverse
    angles = jnp.concatenate([angles, angles], axis=-1)
    return (jnp.cos(angles), jnp.sin(angles))


def rotary(vectors, cosine_table, sine_table):
    half_rot = ROT // 2
    rot_part = vectors[..., :ROT]
    rot_rest = vectors[..., ROT:]
    turned = jnp.concatenate([-rot_part[..., half_rot:], rot_part[..., :half_rot]], axis=-1)
    rotated = rot_part * cosine_table + turned * sine_table
    return jnp.concatenate([rotated, rot_rest], axis=-1)


def rotary_back(vectors, cosine_table, sine_table):
    half_rot = ROT // 2
    rot_part = vectors[..., :ROT]
    rot_rest = vectors[..., ROT:]
    turned = jnp.concatenate([rot_part[..., half_rot:], -rot_part[..., :half_rot]], axis=-1)
    rotated = rot_part * cosine_table + turned * sine_table
    return jnp.concatenate([rotated, rot_rest], axis=-1)


def local_pairs(
    layer_input,
    ln1_gain,
    ln1_bias,
    ln2_gain,
    ln2_bias,
    qkv_weight,
    qkv_bias,
    dense_weight,
    dense_bias,
    fc1_weight,
    fc1_bias,
    fc2_weight,
    fc2_bias,
    seq_ids,
    cotangent,
):
    n = lax.axis_size("dp")
    bits = n.bit_length() - 1
    me = lax.axis_index("dp")
    core = lax.axis_index("tensor")
    bit = [(me >> k) & 1 for k in range(bits)]
    zh_bits = tuple(range(FIRST_ZH, bits))
    rows_here, d_model = layer_input.shape
    feature = 2 * bit[BIT_ZL] + bit[BIT_X]

    def swap(v, k):
        return lax.ppermute(v, "dp", [(i, i ^ (1 << k)) for i in range(n)])

    def swap_core(v):
        return lax.ppermute(v, "tensor", [(0, 1), (1, 0)])

    def pick(v, b, axis):
        return lax.dynamic_index_in_dim(v, b, axis, keepdims=False)

    def ordered(b, own, other, axis):
        return jnp.stack(
            [jnp.where(b == 0, own, other), jnp.where(b == 0, other, own)], axis=axis
        )

    def gather_rows(v):
        v = jnp.stack([v, swap(v, BIT_ZL)], axis=0)
        v = jnp.concatenate([v, swap(v, BIT_X)], axis=0)
        return v

    def gather_tokens(v):
        v = gather_rows(v)
        return ordered(core, v, swap_core(v), 1).reshape(4 * 2 * rows_here, d_model)

    def scatter_tokens(v):
        v = v.reshape(4, 2, rows_here, d_model)
        keep = pick(v, core, 1)
        v = keep + swap_core(pick(v, 1 - core, 1).astype(BF16))
        v = v[:2] + swap(v[2:].astype(BF16), BIT_X)
        return v[0] + swap(v[1].astype(BF16), BIT_ZL)

    def gather_weight(w):
        rows, width = w.shape
        w = w.reshape(rows, 2, 2, width // 4)
        w = ordered(bit[BIT_X], pick(w, bit[BIT_X], 2), swap(pick(w, 1 - bit[BIT_X], 2), BIT_X), 0)
        w = ordered(bit[BIT_ZL], pick(w, bit[BIT_ZL], 2), swap(pick(w, 1 - bit[BIT_ZL], 2), BIT_ZL), 0)
        for k in zh_bits:
            w = ordered(bit[k], w, swap(w, k), 0)
        w = ordered(bit[BIT_Y], w, swap(w, BIT_Y), w.ndim - 3)
        return w.reshape(rows * n, width // 4)

    def scatter_grad(g):
        rows, width = g.shape[0] // n, g.shape[1]
        g = g.reshape((2,) * bits + (rows, width))
        axis = bits - 1 - BIT_Y
        g = pick(g, bit[BIT_Y], axis) + swap(pick(g, 1 - bit[BIT_Y], axis).astype(BF16), BIT_Y)
        for k in reversed(zh_bits):
            g = pick(g, bit[k], 0) + swap(pick(g, 1 - bit[k], 0).astype(BF16), k)
        g = g.astype(BF16)
        g = ordered(bit[BIT_ZL], pick(g, bit[BIT_ZL], 0), swap(pick(g, 1 - bit[BIT_ZL], 0), BIT_ZL), 2)
        g = ordered(bit[BIT_X], pick(g, bit[BIT_X], 0), swap(pick(g, 1 - bit[BIT_X], 0), BIT_X), 2)
        return g.reshape(rows, 4 * width).astype(F32)

    def take_block(v, parts):
        return lax.dynamic_slice_in_dim(v, feature * (v.shape[0] // parts), v.shape[0] // parts, 0)

    gains = [v.astype(F32) for v in (ln1_gain, ln1_bias, ln2_gain, ln2_bias)]

    rows_in = gather_tokens(layer_input)
    w_fc1 = gather_weight(fc1_weight)
    cot = gather_tokens(cotangent)
    w_fc2 = gather_weight(fc2_weight.T)
    w_qkv = gather_weight(qkv_weight)
    w_dense = gather_weight(dense_weight.T)
    ids = gather_rows(seq_ids)
    group_len = seq_ids.shape[0]

    def normalize(v):
        v = v.astype(F32)
        center = v - jnp.mean(v, axis=-1, keepdims=True)
        spread = jnp.mean(center * center, axis=-1, keepdims=True)
        scale = lax.rsqrt(spread + 1e-05)
        return center * scale, scale

    xhat, _ = normalize(rows_in)
    normed_attn = (xhat * gains[0] + gains[1]).astype(BF16)
    normed_ffn = (xhat * gains[2] + gains[3]).astype(BF16)

    ffn_input = mm(normed_ffn, w_fc1, NN) + take_block(fc1_bias, 4).astype(F32)
    cdf = 0.5 * (1.0 + lax.erf(ffn_input * (1.0 / math.sqrt(2.0))))
    density = jnp.exp(-0.5 * ffn_input * ffn_input) * (1.0 / math.sqrt(2.0 * math.pi))
    hidden = (ffn_input * cdf).astype(BF16)
    slope = cdf + ffn_input * density
    grad_fc2 = mm(cot, hidden, TN)
    out_fc2 = scatter_grad(grad_fc2).T

    grad_ffn = (mm(cot, w_fc2, NN) * slope).astype(BF16)
    grad_fc1 = mm(normed_ffn, grad_ffn, TN)
    out_fc1 = scatter_grad(grad_fc1)

    qkv = mm(normed_attn, w_qkv, NN) + take_block(qkv_bias, 4).astype(F32)
    qkv = qkv.reshape(4, group_len, 3, HEAD_DIM)
    cosines, sines = turn_angles(ids)
    query = rotary(qkv[:, :, 0], cosines, sines).astype(BF16)
    keys = rotary(qkv[:, :, 1], cosines, sines).astype(BF16)
    values = qkv[:, :, 2].astype(BF16)
    places = jnp.arange(group_len, dtype=jnp.int32)
    allowed = (ids[:, :, None] == ids[:, None, :]) & (places[None, None, :] <= places[None, :, None])
    scores = jnp.einsum("gqd,gkd->gqk", query, keys, preferred_element_type=F32) * 0.0625
    scores = jnp.where(allowed, scores, -1e30)
    weights = jnp.exp(scores - jnp.max(scores, axis=-1, keepdims=True))
    probability = weights / jnp.sum(weights, axis=-1, keepdims=True)
    prob_low = probability.astype(BF16)
    attended = jnp.einsum("gqk,gkd->gqd", prob_low, values, preferred_element_type=F32)
    attended = attended.astype(BF16).reshape(-1, HEAD_DIM)

    partial = mm(attended, w_dense, NT) + mm(hidden, w_fc2, NT)
    branch = scatter_tokens(partial)
    layer_output = (
        layer_input.astype(F32) + branch + dense_bias.astype(F32) + fc2_bias.astype(F32)
    ).astype(BF16)

    grad_dense = mm(cot, attended, TN)
    grad_attended = mm(cot, w_dense, NN).astype(BF16).reshape(4, group_len, HEAD_DIM)
    grad_prob = jnp.einsum("gqd,gkd->gqk", grad_attended, values, preferred_element_type=F32)
    row_dot = jnp.sum(probability * grad_prob, axis=-1, keepdims=True)
    grad_scores = (probability * (grad_prob - row_dot)).astype(BF16)
    grad_query = jnp.einsum("gqk,gkd->gqd", grad_scores, keys, preferred_element_type=F32) * 0.0625
    grad_keys = jnp.einsum("gqk,gqd->gkd", grad_scores, query, preferred_element_type=F32) * 0.0625
    grad_values = jnp.einsum("gqk,gqd->gkd", prob_low, grad_attended, preferred_element_type=F32)
    qkv_grad = jnp.concatenate(
        [
            rotary_back(grad_query, cosines, sines).astype(BF16),
            rotary_back(grad_keys, cosines, sines).astype(BF16),
            grad_values.astype(BF16),
        ],
        axis=-1,
    ).reshape(-1, 3 * HEAD_DIM)
    out_qkv = scatter_grad(mm(normed_attn, qkv_grad, TN))
    out_dense = scatter_grad(grad_dense).T

    attn_part = mm(qkv_grad, w_qkv, NT)
    ffn_part = mm(grad_ffn, w_fc1, NT)
    e_rows = scatter_tokens(attn_part * gains[0] + ffn_part * gains[2])
    own_hat, own_scale = normalize(layer_input)
    cot_rows = cotangent.astype(F32)
    input_grad = cot_rows + own_scale * (
        e_rows
        - jnp.mean(e_rows, axis=-1, keepdims=True)
        - own_hat * jnp.mean(e_rows * own_hat, axis=-1, keepdims=True)
    )

    small = jnp.stack(
        [
            jnp.sum(attn_part * xhat, axis=0),
            jnp.sum(attn_part, axis=0),
            jnp.sum(ffn_part * xhat, axis=0),
            jnp.sum(ffn_part, axis=0),
            jnp.sum(cot_rows, axis=0),
        ]
    )
    small = small + swap_core(small)
    for k in range(bits):
        small = small + swap(small, k)
    columns = jnp.concatenate(
        [jnp.sum(qkv_grad.astype(F32), axis=0), jnp.sum(grad_ffn.astype(F32), axis=0)]
    )
    for k in (BIT_Y,) + zh_bits:
        columns = columns + swap(columns, k)
    columns = ordered(bit[BIT_X], columns, swap(columns, BIT_X), 0)
    columns = ordered(bit[BIT_ZL], columns, swap(columns, BIT_ZL), 0).reshape(4, -1)
    out_qkv_bias = columns[:, : 3 * HEAD_DIM].reshape(-1)
    out_fc1_bias = columns[:, 3 * HEAD_DIM :].reshape(-1)

    return (
        layer_output,
        input_grad,
        small[0],
        small[1],
        small[2],
        small[3],
        out_qkv,
        out_qkv_bias,
        out_dense,
        small[4],
        out_fc1,
        out_fc1_bias,
        out_fc2,
        small[4],
    )


TILE = 256
ORDER = """
g0 sd5 s14 s20 sq4 s113 s11 sq5 s19 s21 sd9 s18 s112 x0 s29 sd4 f18 s24 fd5 fq4 sq8 c0 sq1 f14 f11 f112 f113
f19 sd12 x1 s15 fd4 f24 x2 s28 c2 f29 sd8 sd0 sq12 fd12 fq5 x3 s10 fq1 fd9 sq0 c1 s212 sd1 f21 L f15 s213 s25
sq9 f28 c3 sq13 f212 fd8 W1 fq12 fd1 fq8 C f213 f25 P sd13 fq9 fq13 G2 W2 Wq H r23 A r22 r21 fd13 G1 Wd o0 r13
r20 t21 Gd N r12 B o1 rd2 Gq rd3 r11 t11 rq3 i0 rq2 t20 oa i1 v0 rq1 r10 rq0 tq1 ia rd0 tq0 t10 v1 ob rd1 v2
ib td0 td1
"""


def place():
    return lax.axis_index("dp"), lax.axis_index("tensor")


def feature_of(d):
    return 2 * ((d >> BIT_ZL) & 1) + (d & 1)


def greet(peers):
    barrier = pltpu.get_barrier_semaphore()
    for peer in peers:
        pl.semaphore_signal(barrier, inc=1, device_id=peer, device_id_type=MESH)
    pl.semaphore_wait(barrier, len(peers))


class Copies:
    def __init__(self, local_sems, send_sems, recv_sems):
        self.sems = (local_sems, send_sems, recv_sems)
        self.count, self.open, self.locals = 0, [], 0

    def reserve(self, count):
        self.count += count
        return self.count - count

    def at(self, number, source, target, device):
        return pltpu.make_async_remote_copy(
            src_ref=source,
            dst_ref=target,
            send_sem=self.sems[1].at[number],
            recv_sem=self.sems[2].at[number],
            device_id=device,
            device_id_type=MESH,
        )

    def remote(self, source, target, device):
        copy = self.at(self.reserve(1), source, target, device)
        copy.start()
        self.open.append(copy)
        return copy

    def local(self, source, target):
        copy = pltpu.make_async_copy(source, target, self.sems[0].at[self.locals])
        copy.start()
        self.locals += 1
        return copy

    def now(self, *pairs):
        for copy in [self.local(*pair) for pair in pairs]:
            copy.wait()

    def finish(self):
        for copy in self.open:
            copy.wait_send()


def rows_at(start, size):
    return pl.ds(pl.multiple_of(start * size, size), size)


def fold(v):
    return jnp.sum(v.reshape(v.shape[0] // 8, 8, v.shape[1]), axis=0)


def rope(v, tables, sign):
    first = v[:, :128]
    turned = pltpu.roll(first, 96, 1) * tables[1] + pltpu.roll(first, 32, 1) * tables[2]
    return jnp.concatenate([first * tables[0] + sign * turned, v[:, 128:]], axis=1)


def layer_kernel(
    x_ref, c_ref, w1, w2, wq, wd, flag, norms, turns,
    f1, f2, fq, fd, out_keep, out_got, in_keep, in_got, vec,
    xg, cg, g1, g2, gq, gd, na, r1, r2, rq, rd, z1, z2, zq, zd, co, ci, xo, xi, ob, flags,
    big1, big2, wa, wb, wqv, wdv, hid, gf, qkv, att, d1, d2, dq, dd, xt, st, stats, sums, cols, vec_own, vec_got, vec_sum, vec_core, fl,
    local_sems, send_sems, recv_sems,
):
    me, core = place()
    by, upper, mine = (me >> 1) & 1, me >> 2, feature_of(me)
    rows = w1.shape[0]
    d_model = x_ref.shape[1]
    greet([(me ^ d, core) for d in range(1, 16)] + [(me, 1 - core)])
    copies = Copies(local_sems, send_sems, recv_sems)
    weights = {"1": (w1, g1, 1), "2": (w2, g2, 0), "q": (wq, gq, 1), "d": (wd, gd, 0)}
    tokens = {"x": (x_ref, xg), "c": (c_ref, cg)}
    grads = {"1": (d1, f1, r1, z1, 0), "2": (d2, f2, r2, z2, 1), "q": (dq, fq, rq, zq, 0), "d": (dd, fd, rd, zd, 1)}
    state, kept, landed = {}, [], []
    pieces = {name: [] for name in weights}

    def block(w, dim, d):
        size = w.shape[dim] // 4
        cut = pl.ds(feature_of(d) * size, size)
        return w.at[cut, :] if dim == 0 else w.at[:, cut]

    def slot(g, dim, d):
        cut = pl.ds(d * rows, rows)
        return g.at[:, cut] if dim == 0 else g.at[cut, :]

    def send_flag():
        cols[...] = jnp.zeros_like(cols)
        kept.append(copies.local(flag, flags.at[0]))
        state["flags"] = [copies.remote(flag, flags.at[k], (me ^ d, core)) for k, d in ((1, 1), (2, 4), (3, 5))]

    def send_weight(name, d):
        w, g, dim = weights[name]
        if d == 0:
            state[name, 0] = copies.local(block(w, dim, me), slot(g, dim, me))
            pieces[name].append(copies.remote(block(w, dim, me ^ 2), slot(g, dim, me), (me ^ 2, core)))
        else:
            state[name, d] = copies.remote(block(w, dim, me ^ d), slot(g, dim, me), (me ^ d, core))

    def forward_weight(name, d):
        w, g, dim = weights[name]
        state[name, d].wait_recv()
        held = slot(g, dim, me ^ d)
        pieces[name].append(copies.remote(held, held, (me ^ 2, core)))

    def weight_ready(name):
        state[name, 0].wait()
        for copy in pieces[name]:
            copy.wait_recv()

    def tile_at(ref, rel, half):
        return ref.at[rows_at(rel * 2 + half, TILE), :]

    def token_step(kind, step):
        source, g = tokens[kind]
        if step == "0":
            state[kind] = [
                copies.remote(source, tile_at(g, 2, core), (me ^ 4, core)),
                copies.remote(source, tile_at(g, 1, core), (me ^ 1, core)),
            ]
            state[kind + "p0"] = copies.remote(source, tile_at(g, 0, core), (me, 1 - core))
        elif step == "1":
            state[kind][0].wait_recv()
            state[kind].append(copies.remote(tile_at(g, 2, core), tile_at(g, 3, core), (me ^ 1, core)))
            state[kind + "p2"] = copies.remote(tile_at(g, 2, core), tile_at(g, 2, core), (me, 1 - core))
        elif step == "2":
            state[kind][1].wait_recv()
            state[kind + "p1"] = copies.remote(tile_at(g, 1, core), tile_at(g, 1, core), (me, 1 - core))
        elif step == "3":
            state[kind][2].wait_recv()
            state[kind + "p3"] = copies.remote(tile_at(g, 3, core), tile_at(g, 3, core), (me, 1 - core))

    def normalize():
        for rel in range(4):
            state["xp%d" % rel].wait_recv()
        keep = copies.locals
        copies.locals += 4

        def load(k, source):
            return pltpu.make_async_copy(source, xt.at[k & 1], local_sems.at[keep + (k & 1)])

        def store(k):
            return pltpu.make_async_copy(
                big2.at[rows_at(k & 1, TILE), :], na.at[rows_at(k, TILE), :], local_sems.at[keep + 2 + (k & 1)]
            )

        def start(k):
            @pl.when(k == core)
            def _():
                load(k, x_ref).start()

            @pl.when(k != core)
            def _():
                load(k, xg.at[rows_at(k, TILE), :]).start()

        start(0)

        @pl.loop(0, 8)
        def _(k):
            @pl.when(k < 7)
            def _():
                start(k + 1)

            load(k, x_ref).wait()

            @pl.when(k > 1)
            def _():
                store(k).wait()

            @pl.loop(0, TILE // 32)
            def _(j):
                r = rows_at(j, 32)
                here = rows_at(k * (TILE // 32) + j, 32)
                v = xt[k & 1, r, :].astype(F32)
                mean = jnp.mean(v, axis=-1, keepdims=True)
                center = v - mean
                scale = lax.rsqrt(jnp.mean(center * center, axis=-1, keepdims=True) + 1e-05)
                xhat = center * scale
                big2[rows_at((k & 1) * (TILE // 32) + j, 32), :] = (xhat * norms[0:1, :] + norms[1:2, :]).astype(BF16)
                big1[here, :] = (xhat * norms[2:3, :] + norms[3:4, :]).astype(BF16)
                stats[here, 0:1] = mean
                stats[here, 1:2] = scale

            store(k).start()

        store(0).wait()
        store(1).wait()

    def up(lo, hi):
        @pl.loop(lo, hi)
        def _(i):
            r = rows_at(i, TILE)
            for j in range(0, wa.shape[1], 512):
                c = slice(j, j + 512)
                v = mm(big1[r, :], wa[:, c], NN) + norms[4:5, c]
                cdf = 0.5 * (1.0 + lax.erf(v * (1.0 / math.sqrt(2.0))))
                density = jnp.exp(-0.5 * v * v) * (1.0 / math.sqrt(2.0 * math.pi))
                hid[r, c] = (v * cdf).astype(BF16)
                gf[r, c] = (cdf + v * density).astype(BF16)

    def load_cotangent():
        for k in range(4):
            state["cp%d" % k].wait_recv()
        pairs = [
            (c_ref, tile_at(big2, 0, core)),
            (tile_at(cg, 0, 1 - core), tile_at(big2, 0, 1 - core)),
            (cg.at[pl.ds(2 * TILE, 6 * TILE), :], big2.at[pl.ds(2 * TILE, 6 * TILE), :]),
        ]
        copies.now(*pairs)

        @pl.loop(0, TILE // 32)
        def _(k):
            part = fold(big2[rows_at(core * (TILE // 32) + k, 32), :].astype(F32))
            sums[4] = jnp.where(k == 0, part, sums[4] + part)

    def cut(ref, dim, start, size):
        start = pl.multiple_of(start * size, size)
        return ref.at[pl.ds(start, size), :] if dim == 0 else ref.at[:, pl.ds(start, size)]

    def make_grad(name):
        d, _, r, _, dim = grads[name]
        base = copies.reserve(4)

        def send(k):
            pair = (upper ^ (3 - k)) * 2 + 1 - by
            return copies.at(
                base + k, cut(d, dim, pair, 2 * rows), cut(r, dim, 3 - k, 2 * rows), (me ^ 2, core)
            )

        @pl.loop(0, 8)
        def _(k):
            pair = (upper ^ (3 - (k & 3))) * 2 + (by ^ 1 ^ (k >> 2))
            c = rows_at(pair, 2 * rows)
            if name == "1":
                d[c, :] = mm(big1[:, c], gf[...], TN).astype(BF16)
            elif name == "q":
                d[c, :] = mm(big1[:, c], qkv[...], TN).astype(BF16)
            elif name == "2":
                for j in (0, 512):
                    d[j : j + 512, c] = mm(hid[:, j : j + 512], big2[:, c], TN).astype(BF16)
            else:
                d[:, c] = mm(att[...], big2[:, c], TN).astype(BF16)

            @pl.when(k < 4)
            def _():
                send(k).start()

        for k in range(4):
            state["r" + name, 3 - k] = send(k)
            copies.open.append(send(k))

    def add_slab(name, dim, got, k, own):
        d = grads[name][0]
        stage = st if name == "2" else xt.at[0, :, pl.ds(0, d.shape[1] if dim == 0 else 2 * rows)]
        copies.now((cut(got, dim, k, 2 * rows), stage))
        some = 32 if dim == 0 else 128

        @pl.loop(0, stage.shape[0] // some)
        def _(j):
            c = rows_at(j, some)
            own[c, :] = (own[c, :].astype(F32) + stage[c, :].astype(F32)).astype(BF16)

    def forward_grad(name, u):
        d, f, r, z, dim = grads[name]
        state["r" + name, u].wait_recv()
        own = cut(d, dim, (upper ^ u) * 2 + by, 2 * rows)
        add_slab(name, dim, r, u, own)
        if u & 2:
            state["z" + name, u & 1] = copies.remote(own, cut(z, dim, u & 1, 2 * rows), (me ^ 8, core))

    def deliver_grad(name, u):
        d, f, r, z, dim = grads[name]
        state["z" + name, u].wait_recv()
        add_slab(name, dim, z, u, cut(d, dim, (upper ^ u) * 2 + by, 2 * rows))
        for x in (1, 0):
            piece = cut(d, dim, (upper ^ u) * 4 + by * 2 + ((me & 1) ^ x), rows)
            width = f.shape[1 - dim] // 4
            c = pl.ds(mine * width, width)
            target = f.at[:, c] if dim == 0 else f.at[c, :]
            if u == 0 and x == 0:
                kept.append(copies.local(piece, target))
            else:
                landed.append(copies.remote(piece, target, (me ^ (4 * u + x), core)))

    def hidden_grad():
        @pl.loop(0, 8)
        def _(i):
            r = rows_at(i, TILE)
            for j in range(0, gf.shape[1], 512):
                c = slice(j, j + 512)
                g = (mm(big2[r, :], wb[c, :], NT) * gf[r, c].astype(F32)).astype(BF16)
                gf[r, c] = g
                at = slice(3 * HEAD_DIM + j, 3 * HEAD_DIM + j + 512)
                cols[:, at] += fold(g.astype(F32))

    size, half, quarter = 2 * TILE, TILE, TILE // 2

    def group_rows(number, start, length):
        return pl.ds(pl.multiple_of(number * size + start, TILE), length)

    def group_tables(number):
        three = fl[number, 0:1, 0:1] > 0.5
        tables = []
        for k in range(3):
            again = jnp.concatenate([turns[k, :quarter], turns[k, : 2 * quarter], turns[k, :quarter]], axis=0)
            tables.append(jnp.where(three, again, turns[k]))
        return tables

    def probabilities(number, i):
        seen = (i + 1) * half
        q = qkv[group_rows(number, i * half, half), :HEAD_DIM]
        k = qkv[group_rows(number, 0, seen), HEAD_DIM : 2 * HEAD_DIM]
        v = qkv[group_rows(number, 0, seen), 2 * HEAD_DIM :]
        ti = lax.broadcasted_iota(jnp.int32, (half, seen), 0) + i * half
        tj = lax.broadcasted_iota(jnp.int32, (half, seen), 1)
        part_i = (ti >= quarter).astype(jnp.int32) + (ti >= 3 * quarter).astype(jnp.int32)
        part_j = (tj >= quarter).astype(jnp.int32) + (tj >= 3 * quarter).astype(jnp.int32)
        three = fl[number, 0:1, 0:1] > 0.5
        s = mm(q, k, NT) * 0.0625
        s = jnp.where(tj <= ti, s, -1e30)
        s = jnp.where((part_i != part_j) & three, -1e30, s)
        w = jnp.exp(s - jnp.max(s, axis=-1, keepdims=True))
        return q, k, v, w / jnp.sum(w, axis=-1, keepdims=True)

    def attend(lo, hi):
        @pl.loop(lo, hi)
        def _(number):
            tables = group_tables(number)
            for h in (0, 1):
                copies.now((na.at[group_rows(number, h * half, half), :], xt.at[h]))
            for h in (0, 1):
                r = group_rows(number, h * half, half)
                here = [t[h * half : (h + 1) * half] for t in tables]
                for k in range(3):
                    at = slice(k * HEAD_DIM, (k + 1) * HEAD_DIM)
                    full = mm(xt[h], wqv[:, at], NN) + norms[5:6, at]
                    qkv[r, at] = (rope(full, here, 1.0) if k < 2 else full).astype(BF16)
            for i in (0, 1):
                _, _, v, p = probabilities(number, i)
                att[group_rows(number, i * half, half), :] = mm(p.astype(BF16), v, NN).astype(BF16)

    def attend_back(lo, hi):
        @pl.loop(lo, hi)
        def _(number):
            grad_q, grad_k, grad_v = {}, {}, {}
            tables = group_tables(number)
            for i in (1, 0):
                q, k, v, p = probabilities(number, i)
                low = p.astype(BF16)
                ga = mm(big2[group_rows(number, i * half, half), :], wdv[...], NT).astype(BF16)
                gp = mm(ga, v, NT)
                gs = (p * (gp - jnp.sum(p * gp, axis=-1, keepdims=True))).astype(BF16)
                grad_q[i] = mm(gs, k, NN) * 0.0625
                grad_k[i] = mm(gs, q, TN) * 0.0625
                grad_v[i] = mm(low, ga, TN)

            def put(k, total):
                total = total.astype(BF16)
                at = slice(k * HEAD_DIM, (k + 1) * HEAD_DIM)
                qkv[group_rows(number, 0, size), at] = total
                cols[:, at] += fold(total.astype(F32))

            def joined(one, two):
                return jnp.concatenate([one + two[:half], two[half:]], axis=0)

            put(0, rope(jnp.concatenate([grad_q[0], grad_q[1]], axis=0), tables, -1.0))
            put(1, rope(joined(grad_k[0], grad_k[1]), tables, -1.0))
            put(2, joined(grad_v[0], grad_v[1]))

    def add_tiles(one, other, out):
        @pl.loop(0, TILE // 32)
        def _(k):
            r = rows_at(k, 32)
            out[r, :] = (one[r, :].astype(F32) + other[r, :].astype(F32)).astype(BF16)

    def rel_of(k):
        return 3 - 2 * (k & 1) - (k >> 1)

    def out_sum(received):
        base = copies.reserve(4) if not received else state["o"]
        over = copies.reserve(2) if received else 0

        def to_core(k):
            part = ob.at[rows_at(k, TILE), :]
            return copies.at(base + k, part, co.at[rows_at(k, TILE), :], (me, 1 - core))

        def to_x(k):
            part = ob.at[rows_at(4 + k, TILE), :]
            return copies.at(over + k, part, xo.at[rows_at(k, TILE), :], (me ^ 1, core))

        spare = copies.locals
        copies.locals += 3

        def load(k, slot):
            return pltpu.make_async_copy(
                co.at[rows_at(k, TILE), :], xt.at[slot], local_sems.at[spare + slot]
            )

        def store(k):
            target = ob.at[rows_at(4 * received + k, TILE), :]
            return pltpu.make_async_copy(xt.at[1], target, local_sems.at[spare + 2])

        if received:
            for k in range(4):
                to_core(k).wait_recv()

        @pl.loop(0, 4)
        def _(k):
            r = rows_at(rel_of(k) * 2 + (core if received else 1 - core), TILE)
            if received:
                load(k, 0).start()
                load(k, 0).wait()

            @pl.loop(0, d_model // 512)
            def _(j):
                c = rows_at(j, 512)
                total = mm(att[r, :], wdv[:, c], NN) + mm(hid[r, :], wb[:, c], NN)
                if received:
                    total = total + xt[0, :, c].astype(F32)
                xt[1, :, c] = total.astype(BF16)

            store(k).start()
            store(k).wait()
            if received:

                @pl.when(k < 2)
                def _():
                    to_x(k).start()

            else:
                to_core(k).start()

        if received:
            state["ox"] = [to_x(k) for k in range(2)]
            copies.open.extend(state["ox"])
        else:
            state["o"] = base
            copies.open.extend(to_core(k) for k in range(4))

    def out_end(k):
        state["ox"][k].wait_recv()
        copies.now((ob.at[rows_at(6 + k, TILE), :], xt.at[0]), (xo.at[rows_at(k, TILE), :], xt.at[1]))
        add_tiles(xt.at[0], xt.at[1], xt.at[0])
        if k == 0:
            copies.now((xt.at[0], ob.at[rows_at(6, TILE), :]))
            landed.append(copies.remote(ob.at[rows_at(6, TILE), :], out_got, (me ^ 4, core)))
        else:
            copies.now((xt.at[0], out_keep))

    def in_sum(received):
        base = copies.reserve(4) if not received else state["i"]
        over = copies.reserve(2) if received else 0

        def to_core(k):
            part = big2.at[rows_at(k, TILE), :]
            return copies.at(base + k, part, ci.at[rows_at(k, TILE), :], (me, 1 - core))

        def to_x(k):
            part = big2.at[rows_at(4 + k, TILE), :]
            return copies.at(over + k, part, xi.at[rows_at(k, TILE), :], (me ^ 1, core))

        spare = copies.locals
        copies.locals += 2

        def load(source, slot):
            return pltpu.make_async_copy(source, xt.at[slot], local_sems.at[spare + slot])

        if received:
            for k in range(4):
                to_core(k).wait_recv()
        else:
            sums[0:4] = jnp.zeros_like(sums[0:4])

        @pl.loop(0, 4)
        def _(k):
            tile = rel_of(k) * 2 + (core if received else 1 - core)
            r = rows_at(tile, TILE)
            if received:
                load(ci.at[rows_at(k, TILE), :], 1).start()

                @pl.when(k < 3)
                def _():
                    load(xg.at[r, :], 0).start()

                @pl.when(k == 3)
                def _():
                    load(x_ref, 0).start()

                load(x_ref, 1).wait()
            else:
                load(xg.at[r, :], 0).start()
            load(x_ref, 0).wait()

            @pl.loop(0, d_model // 512)
            def _(j):
                c = rows_at(j, 512)
                a = mm(qkv[r, :], wqv[c, :], NT)
                f = mm(gf[r, :], wa[c, :], NT)
                xhat = (xt[0, :, c].astype(F32) - stats[r, 0:1]) * stats[r, 1:2]
                sums[0, :, c] += fold(a * xhat)
                sums[1, :, c] += fold(a)
                sums[2, :, c] += fold(f * xhat)
                sums[3, :, c] += fold(f)
                total = a * norms[0:1, c] + f * norms[2:3, c]
                if received:
                    total = total + xt[1, :, c].astype(F32)
                big2[rows_at(4 * received + k, TILE), c] = total.astype(BF16)

            if received:

                @pl.when(k < 2)
                def _():
                    to_x(k).start()

            else:
                to_core(k).start()

        if received:
            state["ix"] = [to_x(k) for k in range(2)]
            copies.open.extend(state["ix"])
        else:
            state["i"] = base
            copies.open.extend(to_core(k) for k in range(4))

    def in_end(k):
        state["ix"][k].wait_recv()
        copies.now((xi.at[rows_at(k, TILE), :], xt.at[1]))
        acc = big2.at[rows_at(6 + k, TILE), :]
        add_tiles(acc, xt.at[1], acc)
        if k == 0:
            landed.append(copies.remote(acc, in_got, (me ^ 4, core)))
        else:
            copies.now((acc, in_keep))

    def vector_step(step):
        def piece(ref, d):
            return ref.at[:, rows_at(d, vec_got.shape[-1])]

        if step == "0":
            vec_own[...] = jnp.zeros_like(vec_own)
            for j in range(5):
                vec_own[j : j + 1, :] = jnp.sum(sums[j], axis=0, keepdims=True)
            for j in range(4):
                ours = jnp.where(mine == j, 1.0, 0.0)
                vec_own[8 + j : 9 + j, :] = jnp.sum(cols[...], axis=0, keepdims=True) * ours
            state["v"] = [
                copies.remote(piece(vec_own, me ^ d), vec_got.at[d], (me ^ d, core)) for d in range(1, 16)
            ]
        elif step == "1":
            total = vec_own[:, rows_at(me, vec_got.shape[-1])]
            for d, copy in enumerate(state["v"]):
                copy.wait_recv()
                total = total + vec_got[d + 1]
            vec_sum[...] = total
            state["v"] = copies.remote(vec_sum, vec_core, (me, 1 - core))
        elif step == "2":
            state["v"].wait_recv()
            here = rows_at(me, vec_got.shape[-1])
            vec[8:, here] = vec_sum[8:, :]
            vec[:8, here] = vec_sum[:8, :] + vec_core[:8, :]
            for d in range(1, 16):
                landed.append(copies.remote(piece(vec, me), piece(vec, me), (me ^ d, core)))

    def run(op):
        kind, rest = op[0], op[1:]
        if kind == "g":
            send_flag()
        elif kind in "xc":
            token_step(kind, rest)
        elif kind == "s":
            send_weight(rest[0], int(rest[1:]))
        elif kind == "f":
            forward_weight(rest[0], int(rest[1:]))
        elif kind == "L":
            normalize()
        elif kind == "W":
            weight_ready(rest)
            copies.now({"1": (g1, wa), "2": (g2, wb), "q": (gq, wqv), "d": (gd, wdv)}[rest])
            if rest == "q":
                for copy in state["flags"]:
                    copy.wait_recv()
                kept.pop(0).wait()
                copies.now((flags, fl))
        elif kind == "P":
            up(*{"a": (0, 4), "b": (4, 8)}.get(rest, (0, 8)))
        elif kind == "C":
            load_cotangent()
        elif kind == "G":
            make_grad(rest)
        elif kind == "H":
            hidden_grad()
        elif kind == "r":
            forward_grad(rest[0], int(rest[1]))
        elif kind == "t":
            deliver_grad(rest[0], int(rest[1]))
        elif kind == "A":
            attend(*{"0": (0, 2), "2": (2, 4)}.get(rest, (0, 4)))
        elif kind == "B":
            attend_back(*{"0": (0, 2), "2": (2, 4)}.get(rest, (0, 4)))
        elif kind == "N":
            copies.now((na, big1))
        elif kind == "o":
            if rest in "01":
                out_sum(int(rest))
            else:
                out_end(0 if rest == "a" else 1)
        elif kind == "i":
            if rest in "01":
                in_sum(int(rest))
            else:
                in_end(0 if rest == "a" else 1)
        else:
            vector_step(rest)

    for op in ORDER.split():
        with jax.named_scope("step_" + op):
            run(op)
    for copy in landed:
        copy.wait_recv()
    for copy in kept:
        copy.wait()
    copies.finish()


def turn_tables(group_len):
    inverse = np.exp(
        np.arange(ROT // 2, dtype=np.float32) * np.float32(-2.0 * math.log(10000.0) / ROT)
    ).astype(np.float32)
    angles = np.arange(group_len).astype(np.float32)[:, None] * inverse
    tables = np.zeros((3, group_len, 128), np.float32)
    tables[0] = 1.0
    tables[0, :, : ROT // 2] = tables[0, :, ROT // 2 : ROT] = np.cos(angles)
    tables[1, :, : ROT // 2] = -np.sin(angles)
    tables[2, :, ROT // 2 : ROT] = np.sin(angles)
    return tables


def layer_call(x, c, w1, w2, wq, wd, flag, norms, turns):
    n = lax.axis_size("dp")
    tok, d = x.shape
    rows, u1, uq, ud = w1.shape[0], w1.shape[1] // 4, wq.shape[1] // 4, wd.shape[0] // 4
    many = 8 * tok
    vmem = pl.BlockSpec(memory_space=pltpu.VMEM)
    hbm = pl.BlockSpec(memory_space=pltpu.HBM)

    def low(*shape):
        return jax.ShapeDtypeStruct(shape, BF16)

    results = [low(rows, 4 * u1), low(4 * u1, rows), low(rows, 4 * uq), low(4 * ud, rows)]
    results += [low(tok, d)] * 4 + [jax.ShapeDtypeStruct((16, d), F32)]
    spare = [low(many, d)] * 2 + [low(d, u1), low(u1, d), low(d, uq), low(ud, d), low(many, d)]
    for part in (2, 4):
        spare += [low(d // part, u1), low(u1, d // part), low(d // part, uq), low(ud, d // part)]
    spare += [low(4 * tok, d)] * 2 + [low(2 * tok, d)] * 2 + [low(many, d)] + [jax.ShapeDtypeStruct((4, 8, 128), F32)]
    scratch = [
        (many, d), (many, d), (d, u1), (u1, d), (d, uq), (ud, d), (many, u1), (many, u1), (many, uq), (many, ud),
        (d, u1), (u1, d), (d, uq), (ud, d), (2, tok, d), (u1, 2 * rows),
    ]
    flops = 2 * 3 * many * d * (2 * u1 + uq + ud)
    return pl.pallas_call(
        layer_kernel,
        out_shape=results + spare,
        in_specs=[hbm] * 7 + [vmem] * 2,
        out_specs=[hbm] * 8 + [vmem] + [hbm] * len(spare),
        scratch_shapes=[pltpu.VMEM(s, BF16) for s in scratch]
        + [
            pltpu.VMEM((many, 2), F32),
            pltpu.VMEM((5, 8, d), F32),
            pltpu.VMEM((8, d), F32),
            pltpu.VMEM((16, d), F32),
            pltpu.VMEM((n, 16, d // n), F32),
            pltpu.VMEM((16, d // n), F32),
            pltpu.VMEM((16, d // n), F32),
            pltpu.VMEM((4, 8, 128), F32),
            pltpu.SemaphoreType.DMA((128,)),
            pltpu.SemaphoreType.DMA((176,)),
            pltpu.SemaphoreType.DMA((176,)),
        ],
        compiler_params=pltpu.CompilerParams(
            collective_id=1, has_side_effects=True, vmem_limit_bytes=65000 << 10
        ),
        cost_estimate=pl.CostEstimate(flops=flops, bytes_accessed=200 << 20, transcendentals=0),
        name="layer",
    )(x, c, w1, w2, wq, wd, flag, norms, turns)[:9]


def local_fast(
    layer_input,
    ln1_gain,
    ln1_bias,
    ln2_gain,
    ln2_bias,
    qkv_weight,
    qkv_bias,
    dense_weight,
    dense_bias,
    fc1_weight,
    fc1_bias,
    fc2_weight,
    fc2_bias,
    seq_ids,
    cotangent,
):
    me, core = place()
    rows_here, d_model = layer_input.shape
    feature = feature_of(me)
    units, width = fc1_weight.shape[1] // 4, 3 * HEAD_DIM

    def take_block(v, size):
        return jnp.pad(lax.dynamic_slice_in_dim(v, feature * size, size, 0), (0, d_model - size))

    zero = jnp.zeros_like(ln1_gain)
    norms = jnp.stack(
        [ln1_gain, ln1_bias, ln2_gain, ln2_bias, take_block(fc1_bias, units), take_block(qkv_bias, width), zero, zero]
    ).astype(F32)
    flag = jnp.broadcast_to(jnp.max(seq_ids) > 0, (8, 128)).astype(F32)
    f1, f2, fq, fd, out_keep, out_got, in_keep, in_got, vec = layer_call(
        layer_input,
        cotangent,
        fc1_weight,
        fc2_weight,
        qkv_weight,
        dense_weight,
        flag,
        norms,
        turn_tables(seq_ids.shape[0]),
    )
    out_fc1, out_fc2, out_qkv, out_dense = (v.astype(F32) for v in (f1, f2, fq, fd))
    own = layer_input.astype(F32)
    layer_output = (
        own
        + (out_keep.astype(F32) + out_got.astype(F32))
        + dense_bias.astype(F32)
        + fc2_bias.astype(F32)
    ).astype(BF16)
    center = own - jnp.mean(own, axis=-1, keepdims=True)
    scale = lax.rsqrt(jnp.mean(center * center, axis=-1, keepdims=True) + 1e-05)
    xhat = center * scale
    e_rows = in_keep.astype(F32) + in_got.astype(F32)
    input_grad = cotangent.astype(F32) + scale * (
        e_rows
        - jnp.mean(e_rows, axis=-1, keepdims=True)
        - xhat * jnp.mean(e_rows * xhat, axis=-1, keepdims=True)
    )
    blocks = vec[8:12]
    out_qkv_bias = blocks[:, :width].reshape(-1)
    out_fc1_bias = blocks[:, width : width + units].reshape(-1)
    return (
        layer_output,
        input_grad,
        vec[0],
        vec[1],
        vec[2],
        vec[3],
        out_qkv,
        out_qkv_bias,
        out_dense,
        vec[4],
        out_fc1,
        out_fc1_bias,
        out_fc2,
        vec[4],
    )


def solution(mesh):
    local = local_fast if mesh.shape["dp"] == 16 else local_pairs
    in_specs = (
        P(("dp", "tensor"), None),
        P(),
        P(),
        P(),
        P(),
        P("dp", "tensor"),
        P("tensor"),
        P("tensor", "dp"),
        P(),
        P("dp", "tensor"),
        P("tensor"),
        P("tensor", "dp"),
        P(),
        P("dp"),
        P(("dp", "tensor"), None),
    )
    out_specs = (
        P(("dp", "tensor"), None),
        P(("dp", "tensor"), None),
        P(),
        P(),
        P(),
        P(),
        P("dp", "tensor"),
        P("tensor"),
        P("tensor", "dp"),
        P(),
        P("dp", "tensor"),
        P("tensor"),
        P("tensor", "dp"),
        P(),
    )
    return jax.shard_map(local, mesh=mesh, in_specs=in_specs, out_specs=out_specs, check_vma=False)
```

```python
import math

import jax
import jax.numpy as jnp
import numpy as np
from jax import lax
from jax.experimental import pallas as pl
from jax.experimental.pallas import tpu as pltpu
from jax.sharding import PartitionSpec as P

HEAD_DIM = 256
ROT = 64
BIT_X, BIT_Y, BIT_ZL, FIRST_ZH = 0, 1, 2, 3
F32, BF16 = jnp.float32, jnp.bfloat16
MESH = pl.DeviceIdType.MESH
NN = (((1,), (0,)), ((), ()))
NT = (((1,), (1,)), ((), ()))
TN = (((0,), (0,)), ((), ()))


def mm(a, b, dims):
    return lax.dot_general(a, b, dims, preferred_element_type=F32)


def turn_angles(group_ids):
    places = jnp.arange(group_ids.shape[-1], dtype=jnp.int32)
    starts_flag = jnp.concatenate(
        [jnp.ones_like(group_ids[..., :1], dtype=bool), group_ids[..., 1:] != group_ids[..., :-1]],
        axis=-1,
    )
    starts = lax.cummax(jnp.where(starts_flag, places, 0), axis=group_ids.ndim - 1)
    position = (places - starts).astype(F32)
    steps_rot = jnp.arange(ROT // 2, dtype=F32)
    inverse = jnp.exp(steps_rot * (-2.0 * math.log(10000.0) / ROT))
    angles = position[..., None] * inverse
    angles = jnp.concatenate([angles, angles], axis=-1)
    return (jnp.cos(angles), jnp.sin(angles))


def rotary(vectors, cosine_table, sine_table):
    half_rot = ROT // 2
    rot_part = vectors[..., :ROT]
    rot_rest = vectors[..., ROT:]
    turned = jnp.concatenate([-rot_part[..., half_rot:], rot_part[..., :half_rot]], axis=-1)
    rotated = rot_part * cosine_table + turned * sine_table
    return jnp.concatenate([rotated, rot_rest], axis=-1)


def rotary_back(vectors, cosine_table, sine_table):
    half_rot = ROT // 2
    rot_part = vectors[..., :ROT]
    rot_rest = vectors[..., ROT:]
    turned = jnp.concatenate([rot_part[..., half_rot:], -rot_part[..., :half_rot]], axis=-1)
    rotated = rot_part * cosine_table + turned * sine_table
    return jnp.concatenate([rotated, rot_rest], axis=-1)


def local_pairs(
    layer_input,
    ln1_gain,
    ln1_bias,
    ln2_gain,
    ln2_bias,
    qkv_weight,
    qkv_bias,
    dense_weight,
    dense_bias,
    fc1_weight,
    fc1_bias,
    fc2_weight,
    fc2_bias,
    seq_ids,
    cotangent,
):
    n = lax.axis_size("dp")
    bits = n.bit_length() - 1
    me = lax.axis_index("dp")
    core = lax.axis_index("tensor")
    bit = [(me >> k) & 1 for k in range(bits)]
    zh_bits = tuple(range(FIRST_ZH, bits))
    rows_here, d_model = layer_input.shape
    feature = 2 * bit[BIT_ZL] + bit[BIT_X]

    def swap(v, k):
        return lax.ppermute(v, "dp", [(i, i ^ (1 << k)) for i in range(n)])

    def swap_core(v):
        return lax.ppermute(v, "tensor", [(0, 1), (1, 0)])

    def pick(v, b, axis):
        return lax.dynamic_index_in_dim(v, b, axis, keepdims=False)

    def ordered(b, own, other, axis):
        return jnp.stack(
            [jnp.where(b == 0, own, other), jnp.where(b == 0, other, own)], axis=axis
        )

    def gather_rows(v):
        v = jnp.stack([v, swap(v, BIT_ZL)], axis=0)
        v = jnp.concatenate([v, swap(v, BIT_X)], axis=0)
        return v

    def gather_tokens(v):
        v = gather_rows(v)
        return ordered(core, v, swap_core(v), 1).reshape(4 * 2 * rows_here, d_model)

    def scatter_tokens(v):
        v = v.reshape(4, 2, rows_here, d_model)
        keep = pick(v, core, 1)
        v = keep + swap_core(pick(v, 1 - core, 1).astype(BF16))
        v = v[:2] + swap(v[2:].astype(BF16), BIT_X)
        return v[0] + swap(v[1].astype(BF16), BIT_ZL)

    def gather_weight(w):
        rows, width = w.shape
        w = w.reshape(rows, 2, 2, width // 4)
        w = ordered(bit[BIT_X], pick(w, bit[BIT_X], 2), swap(pick(w, 1 - bit[BIT_X], 2), BIT_X), 0)
        w = ordered(bit[BIT_ZL], pick(w, bit[BIT_ZL], 2), swap(pick(w, 1 - bit[BIT_ZL], 2), BIT_ZL), 0)
        for k in zh_bits:
            w = ordered(bit[k], w, swap(w, k), 0)
        w = ordered(bit[BIT_Y], w, swap(w, BIT_Y), w.ndim - 3)
        return w.reshape(rows * n, width // 4)

    def scatter_grad(g):
        rows, width = g.shape[0] // n, g.shape[1]
        g = g.reshape((2,) * bits + (rows, width))
        axis = bits - 1 - BIT_Y
        g = pick(g, bit[BIT_Y], axis) + swap(pick(g, 1 - bit[BIT_Y], axis).astype(BF16), BIT_Y)
        for k in reversed(zh_bits):
            g = pick(g, bit[k], 0) + swap(pick(g, 1 - bit[k], 0).astype(BF16), k)
        g = g.astype(BF16)
        g = ordered(bit[BIT_ZL], pick(g, bit[BIT_ZL], 0), swap(pick(g, 1 - bit[BIT_ZL], 0), BIT_ZL), 2)
        g = ordered(bit[BIT_X], pick(g, bit[BIT_X], 0), swap(pick(g, 1 - bit[BIT_X], 0), BIT_X), 2)
        return g.reshape(rows, 4 * width).astype(F32)

    def take_block(v, parts):
        return lax.dynamic_slice_in_dim(v, feature * (v.shape[0] // parts), v.shape[0] // parts, 0)

    gains = [v.astype(F32) for v in (ln1_gain, ln1_bias, ln2_gain, ln2_bias)]

    rows_in = gather_tokens(layer_input)
    w_fc1 = gather_weight(fc1_weight)
    cot = gather_tokens(cotangent)
    w_fc2 = gather_weight(fc2_weight.T)
    w_qkv = gather_weight(qkv_weight)
    w_dense = gather_weight(dense_weight.T)
    ids = gather_rows(seq_ids)
    group_len = seq_ids.shape[0]

    def normalize(v):
        v = v.astype(F32)
        center = v - jnp.mean(v, axis=-1, keepdims=True)
        spread = jnp.mean(center * center, axis=-1, keepdims=True)
        scale = lax.rsqrt(spread + 1e-05)
        return center * scale, scale

    xhat, _ = normalize(rows_in)
    normed_attn = (xhat * gains[0] + gains[1]).astype(BF16)
    normed_ffn = (xhat * gains[2] + gains[3]).astype(BF16)

    ffn_input = mm(normed_ffn, w_fc1, NN) + take_block(fc1_bias, 4).astype(F32)
    cdf = 0.5 * (1.0 + lax.erf(ffn_input * (1.0 / math.sqrt(2.0))))
    density = jnp.exp(-0.5 * ffn_input * ffn_input) * (1.0 / math.sqrt(2.0 * math.pi))
    hidden = (ffn_input * cdf).astype(BF16)
    slope = cdf + ffn_input * density
    grad_fc2 = mm(cot, hidden, TN)
    out_fc2 = scatter_grad(grad_fc2).T

    grad_ffn = (mm(cot, w_fc2, NN) * slope).astype(BF16)
    grad_fc1 = mm(normed_ffn, grad_ffn, TN)
    out_fc1 = scatter_grad(grad_fc1)

    qkv = mm(normed_attn, w_qkv, NN) + take_block(qkv_bias, 4).astype(F32)
    qkv = qkv.reshape(4, group_len, 3, HEAD_DIM)
    cosines, sines = turn_angles(ids)
    query = rotary(qkv[:, :, 0], cosines, sines).astype(BF16)
    keys = rotary(qkv[:, :, 1], cosines, sines).astype(BF16)
    values = qkv[:, :, 2].astype(BF16)
    places = jnp.arange(group_len, dtype=jnp.int32)
    allowed = (ids[:, :, None] == ids[:, None, :]) & (places[None, None, :] <= places[None, :, None])
    scores = jnp.einsum("gqd,gkd->gqk", query, keys, preferred_element_type=F32) * 0.0625
    scores = jnp.where(allowed, scores, -1e30)
    weights = jnp.exp(scores - jnp.max(scores, axis=-1, keepdims=True))
    probability = weights / jnp.sum(weights, axis=-1, keepdims=True)
    prob_low = probability.astype(BF16)
    attended = jnp.einsum("gqk,gkd->gqd", prob_low, values, preferred_element_type=F32)
    attended = attended.astype(BF16).reshape(-1, HEAD_DIM)

    partial = mm(attended, w_dense, NT) + mm(hidden, w_fc2, NT)
    branch = scatter_tokens(partial)
    layer_output = (
        layer_input.astype(F32) + branch + dense_bias.astype(F32) + fc2_bias.astype(F32)
    ).astype(BF16)

    grad_dense = mm(cot, attended, TN)
    grad_attended = mm(cot, w_dense, NN).astype(BF16).reshape(4, group_len, HEAD_DIM)
    grad_prob = jnp.einsum("gqd,gkd->gqk", grad_attended, values, preferred_element_type=F32)
    row_dot = jnp.sum(probability * grad_prob, axis=-1, keepdims=True)
    grad_scores = (probability * (grad_prob - row_dot)).astype(BF16)
    grad_query = jnp.einsum("gqk,gkd->gqd", grad_scores, keys, preferred_element_type=F32) * 0.0625
    grad_keys = jnp.einsum("gqk,gqd->gkd", grad_scores, query, preferred_element_type=F32) * 0.0625
    grad_values = jnp.einsum("gqk,gqd->gkd", prob_low, grad_attended, preferred_element_type=F32)
    qkv_grad = jnp.concatenate(
        [
            rotary_back(grad_query, cosines, sines).astype(BF16),
            rotary_back(grad_keys, cosines, sines).astype(BF16),
            grad_values.astype(BF16),
        ],
        axis=-1,
    ).reshape(-1, 3 * HEAD_DIM)
    out_qkv = scatter_grad(mm(normed_attn, qkv_grad, TN))
    out_dense = scatter_grad(grad_dense).T

    attn_part = mm(qkv_grad, w_qkv, NT)
    ffn_part = mm(grad_ffn, w_fc1, NT)
    e_rows = scatter_tokens(attn_part * gains[0] + ffn_part * gains[2])
    own_hat, own_scale = normalize(layer_input)
    cot_rows = cotangent.astype(F32)
    input_grad = cot_rows + own_scale * (
        e_rows
        - jnp.mean(e_rows, axis=-1, keepdims=True)
        - own_hat * jnp.mean(e_rows * own_hat, axis=-1, keepdims=True)
    )

    small = jnp.stack(
        [
            jnp.sum(attn_part * xhat, axis=0),
            jnp.sum(attn_part, axis=0),
            jnp.sum(ffn_part * xhat, axis=0),
            jnp.sum(ffn_part, axis=0),
            jnp.sum(cot_rows, axis=0),
        ]
    )
    small = small + swap_core(small)
    for k in range(bits):
        small = small + swap(small, k)
    columns = jnp.concatenate(
        [jnp.sum(qkv_grad.astype(F32), axis=0), jnp.sum(grad_ffn.astype(F32), axis=0)]
    )
    for k in (BIT_Y,) + zh_bits:
        columns = columns + swap(columns, k)
    columns = ordered(bit[BIT_X], columns, swap(columns, BIT_X), 0)
    columns = ordered(bit[BIT_ZL], columns, swap(columns, BIT_ZL), 0).reshape(4, -1)
    out_qkv_bias = columns[:, : 3 * HEAD_DIM].reshape(-1)
    out_fc1_bias = columns[:, 3 * HEAD_DIM :].reshape(-1)

    return (
        layer_output,
        input_grad,
        small[0],
        small[1],
        small[2],
        small[3],
        out_qkv,
        out_qkv_bias,
        out_dense,
        small[4],
        out_fc1,
        out_fc1_bias,
        out_fc2,
        small[4],
    )


TILE = 256
ORDER = """
g0 sq5 sq13 sd13 sd1 sd5 s18 sq9 x0 s15 sq8 sd9 sd0 s113 fq13 sq4 fd1 f18 s112 s20 s10 s19 sq12 fq5 sd8 s11
sq1 x1 s25 s21 sd4 c0 s14 f15 sq0 fq1 s29 f11 f113 fq4 s212 fq8 sd12 x2 s28 f19 s213 x3 fq12 fq9 L fd9 fd8 s24
f112 f21 f14 f212 c1 Wq fd5 fd13 f25 A W1 f24 fd12 f29 c2 P f28 fd4 c3 f213 C G2 W2 Wd r23 o0 H r22 r21 t21 G1
o1 r13 B N r20 r12 oa Gd Gq X i0 t20 r11 rd2 rq3 t11 i1 rq1 rq2 tq1 rd3 v0 rq0 rd0 ia rd1 tq0 r10 t10 v1 v2
td1 td0 ib ob
"""


def place():
    return lax.axis_index("dp"), lax.axis_index("tensor")


def feature_of(d):
    return 2 * ((d >> BIT_ZL) & 1) + (d & 1)


def greet(peers):
    barrier = pltpu.get_barrier_semaphore()
    for peer in peers:
        pl.semaphore_signal(barrier, inc=1, device_id=peer, device_id_type=MESH)
    pl.semaphore_wait(barrier, len(peers))


class Copies:
    def __init__(self, local_sems, send_sems, recv_sems):
        self.sems = (local_sems, send_sems, recv_sems)
        self.count, self.open, self.locals = 0, [], 0

    def reserve(self, count):
        self.count += count
        return self.count - count

    def at(self, number, source, target, device):
        return pltpu.make_async_remote_copy(
            src_ref=source,
            dst_ref=target,
            send_sem=self.sems[1].at[number],
            recv_sem=self.sems[2].at[number],
            device_id=device,
            device_id_type=MESH,
        )

    def remote(self, source, target, device):
        copy = self.at(self.reserve(1), source, target, device)
        copy.start()
        self.open.append(copy)
        return copy

    def local(self, source, target):
        copy = pltpu.make_async_copy(source, target, self.sems[0].at[self.locals])
        copy.start()
        self.locals += 1
        return copy

    def now(self, *pairs):
        for copy in [self.local(*pair) for pair in pairs]:
            copy.wait()

    def finish(self):
        for copy in self.open:
            copy.wait_send()


def rows_at(start, size):
    return pl.ds(pl.multiple_of(start * size, size), size)


def fold(v):
    return jnp.sum(v.reshape(v.shape[0] // 8, 8, v.shape[1]), axis=0)


def rope(v, tables, sign):
    first = v[:, :128]
    turned = pltpu.roll(first, 96, 1) * tables[1] + pltpu.roll(first, 32, 1) * tables[2]
    return jnp.concatenate([first * tables[0] + sign * turned, v[:, 128:]], axis=1)


def layer_kernel(
    x_ref, c_ref, w1, w2, wq, wd, ids, turns, p0, p1, p2, p3, p4, p5, p6, p7,
    f1, f2, fq, fd, out_keep, out_got, in_keep, in_got, vec, norms,
    xg, cg, g1, g2, gq, gd, na, r1, r2, rq, rd, z1, z2, zq, zd, co, ci, xo, xi, ob, flags,
    big1, big2, wa, wb, wqv, wdv, hid, gf, qkv, att, d1, d2, dq, dd, xt, st, stats, sums, cols, vec_own, vec_got, vec_sum, vec_core, fl, flag, vectors,
    local_sems, send_sems, recv_sems,
):
    me, core = place()
    by, upper, mine = (me >> 1) & 1, me >> 2, feature_of(me)
    rows = w1.shape[0]
    d_model = x_ref.shape[1]
    greet([(me ^ d, core) for d in range(1, 16)] + [(me, 1 - core)])
    copies = Copies(local_sems, send_sems, recv_sems)
    weights = {"1": (w1, g1, 1), "2": (w2, g2, 0), "q": (wq, gq, 1), "d": (wd, gd, 0)}
    tokens = {"x": (x_ref, xg), "c": (c_ref, cg)}
    grads = {"1": (d1, f1, r1, z1, 0), "2": (d2, f2, r2, z2, 1), "q": (dq, fq, rq, zq, 0), "d": (dd, fd, rd, zd, 1)}
    state, kept, landed = {}, [], []
    pieces = {name: [] for name in weights}

    def spread():
        lanes = vectors.shape[1]
        norms[...] = jnp.zeros_like(norms)
        wide = d_model // lanes
        start = 0
        for part in (p0, p1, p2, p3, p4, p5, p6, p7):
            vectors[start : start + part.shape[0], :] = part[...].astype(F32)
            start += part.shape[0]
        units, width = wa.shape[1] // lanes, wqv.shape[1] // lanes
        places = [(row, row * wide, wide) for row in range(4)]
        places.append((4, 6 * wide + mine * units, units))
        places.append((5, 6 * wide + 4 * units + mine * width, width))
        for row, start, count in places:
            for k in range(count):
                norms[row : row + 1, k * lanes : (k + 1) * lanes] = vectors[pl.ds(start + k, 1), :]
        for k in range(wide):
            both = vectors[pl.ds(4 * wide + k, 1), :] + vectors[pl.ds(5 * wide + k, 1), :]
            norms[6:7, k * lanes : (k + 1) * lanes] = both

    def block(w, dim, d):
        size = w.shape[dim] // 4
        cut = pl.ds(feature_of(d) * size, size)
        return w.at[cut, :] if dim == 0 else w.at[:, cut]

    def slot(g, dim, d):
        cut = pl.ds(d * rows, rows)
        return g.at[:, cut] if dim == 0 else g.at[cut, :]

    def send_flag():
        cols[...] = jnp.zeros_like(cols)
        flag[...] = jnp.full(flag.shape, ids[ids.shape[0] - 1], jnp.int32).astype(F32)
        kept.append(copies.local(flag, flags.at[0]))
        state["flags"] = [copies.remote(flag, flags.at[k], (me ^ d, core)) for k, d in ((1, 1), (2, 4), (3, 5))]

    def send_weight(name, d):
        w, g, dim = weights[name]
        if d == 0:
            state[name, 0] = copies.local(block(w, dim, me), slot(g, dim, me))
            pieces[name].append(copies.remote(block(w, dim, me ^ 2), slot(g, dim, me), (me ^ 2, core)))
        else:
            state[name, d] = copies.remote(block(w, dim, me ^ d), slot(g, dim, me), (me ^ d, core))

    def forward_weight(name, d):
        w, g, dim = weights[name]
        state[name, d].wait_recv()
        held = slot(g, dim, me ^ d)
        pieces[name].append(copies.remote(held, held, (me ^ 2, core)))

    def weight_ready(name):
        state[name, 0].wait()
        for copy in pieces[name]:
            copy.wait_recv()

    def tile_at(ref, rel, half):
        return ref.at[rows_at(rel * 2 + half, TILE), :]

    def token_step(kind, step):
        source, g = tokens[kind]
        if step == "0":
            state[kind] = [
                copies.remote(source, tile_at(g, 2, core), (me ^ 4, core)),
                copies.remote(source, tile_at(g, 1, core), (me ^ 1, core)),
            ]
            state[kind + "p0"] = copies.remote(source, tile_at(g, 0, core), (me, 1 - core))
        elif step == "1":
            state[kind][0].wait_recv()
            state[kind].append(copies.remote(tile_at(g, 2, core), tile_at(g, 3, core), (me ^ 1, core)))
            state[kind + "p2"] = copies.remote(tile_at(g, 2, core), tile_at(g, 2, core), (me, 1 - core))
        elif step == "2":
            state[kind][1].wait_recv()
            state[kind + "p1"] = copies.remote(tile_at(g, 1, core), tile_at(g, 1, core), (me, 1 - core))
        elif step == "3":
            state[kind][2].wait_recv()
            state[kind + "p3"] = copies.remote(tile_at(g, 3, core), tile_at(g, 3, core), (me, 1 - core))

    def normalize():
        for rel in range(4):
            state["xp%d" % rel].wait_recv()
        keep = copies.locals
        copies.locals += 4

        def load(k, source):
            return pltpu.make_async_copy(source, xt.at[k & 1], local_sems.at[keep + (k & 1)])

        def store(k):
            return pltpu.make_async_copy(
                big2.at[rows_at(k & 1, TILE), :], na.at[rows_at(k, TILE), :], local_sems.at[keep + 2 + (k & 1)]
            )

        def start(k):
            @pl.when(k == core)
            def _():
                load(k, x_ref).start()

            @pl.when(k != core)
            def _():
                load(k, xg.at[rows_at(k, TILE), :]).start()

        start(0)

        @pl.loop(0, 8)
        def _(k):
            @pl.when(k < 7)
            def _():
                start(k + 1)

            load(k, x_ref).wait()

            @pl.when(k > 1)
            def _():
                store(k).wait()

            @pl.loop(0, TILE // 32)
            def _(j):
                r = rows_at(j, 32)
                here = rows_at(k * (TILE // 32) + j, 32)
                v = xt[k & 1, r, :].astype(F32)
                mean = jnp.mean(v, axis=-1, keepdims=True)
                center = v - mean
                scale = lax.rsqrt(jnp.mean(center * center, axis=-1, keepdims=True) + 1e-05)
                xhat = center * scale
                big2[rows_at((k & 1) * (TILE // 32) + j, 32), :] = (xhat * norms[0:1, :] + norms[1:2, :]).astype(BF16)
                big1[here, :] = (xhat * norms[2:3, :] + norms[3:4, :]).astype(BF16)
                stats[here, 0:1] = mean
                stats[here, 1:2] = scale

            store(k).start()

        store(0).wait()
        store(1).wait()

    def up(lo, hi):
        @pl.loop(lo, hi)
        def _(i):
            r = rows_at(i, TILE)
            for j in range(0, wa.shape[1], 512):
                c = slice(j, j + 512)
                v = mm(big1[r, :], wa[:, c], NN) + norms[4:5, c]
                cdf = 0.5 * (1.0 + lax.erf(v * (1.0 / math.sqrt(2.0))))
                density = jnp.exp(-0.5 * v * v) * (1.0 / math.sqrt(2.0 * math.pi))
                hid[r, c] = (v * cdf).astype(BF16)
                gf[r, c] = (cdf + v * density).astype(BF16)

    def group_tiles(own, gathered, target):
        after = pl.ds(2 * TILE, 6 * TILE)
        return [
            (own, tile_at(target, 0, core)),
            (tile_at(gathered, 0, 1 - core), tile_at(target, 0, 1 - core)),
            (gathered.at[after, :], target.at[after, :]),
        ]

    def load_cotangent():
        for k in range(4):
            state["cp%d" % k].wait_recv()
        copies.now(*group_tiles(c_ref, cg, big2))

        @pl.loop(0, TILE // 32)
        def _(k):
            part = fold(big2[rows_at(core * (TILE // 32) + k, 32), :].astype(F32))
            sums[4] = jnp.where(k == 0, part, sums[4] + part)

    def cut(ref, dim, start, size):
        start = pl.multiple_of(start * size, size)
        return ref.at[pl.ds(start, size), :] if dim == 0 else ref.at[:, pl.ds(start, size)]

    def make_grad(name):
        d, _, r, _, dim = grads[name]
        base = copies.reserve(4)

        def send(k):
            pair = (upper ^ (3 - k)) * 2 + 1 - by
            return copies.at(
                base + k, cut(d, dim, pair, 2 * rows), cut(r, dim, 3 - k, 2 * rows), (me ^ 2, core)
            )

        @pl.loop(0, 8)
        def _(k):
            pair = (upper ^ (3 - (k & 3))) * 2 + (by ^ 1 ^ (k >> 2))
            c = rows_at(pair, 2 * rows)
            if name == "1":
                d[c, :] = mm(big1[:, c], gf[...], TN).astype(BF16)
            elif name == "q":
                d[c, :] = mm(big1[:, c], qkv[...], TN).astype(BF16)
            elif name == "2":
                for j in (0, 512):
                    d[j : j + 512, c] = mm(hid[:, j : j + 512], big2[:, c], TN).astype(BF16)
            else:
                d[:, c] = mm(att[...], big2[:, c], TN).astype(BF16)

            @pl.when(k < 4)
            def _():
                send(k).start()

        for k in range(4):
            state["r" + name, 3 - k] = send(k)
            copies.open.append(send(k))

    def add_slab(name, dim, got, k, own):
        d = grads[name][0]
        stage = st if name == "2" else xt.at[0, :, pl.ds(0, d.shape[1] if dim == 0 else 2 * rows)]
        copies.now((cut(got, dim, k, 2 * rows), stage))
        some = 32 if dim == 0 else 128

        @pl.loop(0, stage.shape[0] // some)
        def _(j):
            c = rows_at(j, some)
            own[c, :] = (own[c, :].astype(F32) + stage[c, :].astype(F32)).astype(BF16)

    def forward_grad(name, u):
        d, f, r, z, dim = grads[name]
        state["r" + name, u].wait_recv()
        own = cut(d, dim, (upper ^ u) * 2 + by, 2 * rows)
        add_slab(name, dim, r, u, own)
        if u & 2:
            state["z" + name, u & 1] = copies.remote(own, cut(z, dim, u & 1, 2 * rows), (me ^ 8, core))

    def deliver_grad(name, u):
        d, f, r, z, dim = grads[name]
        state["z" + name, u].wait_recv()
        add_slab(name, dim, z, u, cut(d, dim, (upper ^ u) * 2 + by, 2 * rows))
        for x in (1, 0):
            piece = cut(d, dim, (upper ^ u) * 4 + by * 2 + ((me & 1) ^ x), rows)
            width = f.shape[1 - dim] // 4
            c = pl.ds(mine * width, width)
            target = f.at[:, c] if dim == 0 else f.at[c, :]
            if u == 0 and x == 0:
                kept.append(copies.local(piece, target))
            else:
                landed.append(copies.remote(piece, target, (me ^ (4 * u + x), core)))

    def hidden_grad():
        @pl.loop(0, 8)
        def _(i):
            r = rows_at(i, TILE)
            for j in range(0, gf.shape[1], 512):
                c = slice(j, j + 512)
                g = (mm(big2[r, :], wb[c, :], NT) * gf[r, c].astype(F32)).astype(BF16)
                gf[r, c] = g
                at = slice(3 * HEAD_DIM + j, 3 * HEAD_DIM + j + 512)
                cols[:, at] += fold(g.astype(F32))

    size, half, quarter = 2 * TILE, TILE, TILE // 2

    def group_rows(number, start, length):
        return pl.ds(pl.multiple_of(number * size + start, TILE), length)

    def group_tables(number):
        three = fl[number, 0:1, 0:1] > 0.5
        tables = []
        for k in range(3):
            again = jnp.concatenate([turns[k, :quarter], turns[k, : 2 * quarter], turns[k, :quarter]], axis=0)
            tables.append(jnp.where(three, again, turns[k]))
        return tables

    def probabilities(number, i):
        seen = (i + 1) * half
        q = qkv[group_rows(number, i * half, half), :HEAD_DIM]
        k = qkv[group_rows(number, 0, seen), HEAD_DIM : 2 * HEAD_DIM]
        v = qkv[group_rows(number, 0, seen), 2 * HEAD_DIM :]
        ti = lax.broadcasted_iota(jnp.int32, (half, seen), 0) + i * half
        tj = lax.broadcasted_iota(jnp.int32, (half, seen), 1)
        part_i = (ti >= quarter).astype(jnp.int32) + (ti >= 3 * quarter).astype(jnp.int32)
        part_j = (tj >= quarter).astype(jnp.int32) + (tj >= 3 * quarter).astype(jnp.int32)
        three = fl[number, 0:1, 0:1] > 0.5
        s = mm(q, k, NT) * 0.0625
        s = jnp.where(tj <= ti, s, -1e30)
        s = jnp.where((part_i != part_j) & three, -1e30, s)
        w = jnp.exp(s - jnp.max(s, axis=-1, keepdims=True))
        return q, k, v, w / jnp.sum(w, axis=-1, keepdims=True)

    def attend(lo, hi):
        spare = copies.locals
        copies.locals += 4

        def load(number, h):
            at = 2 * (number & 1) + h
            source = na.at[group_rows(number, h * half, half), :]
            return pltpu.make_async_copy(source, xt.at[at], local_sems.at[spare + at])

        for h in (0, 1):
            load(lo, h).start()

        @pl.loop(lo, hi)
        def _(number):
            @pl.when(number + 1 < hi)
            def _():
                for h in (0, 1):
                    load(number + 1, h).start()

            tables = group_tables(number)
            for h in (0, 1):
                load(number, h).wait()
                r = group_rows(number, h * half, half)
                here = [t[h * half : (h + 1) * half] for t in tables]
                for k in range(3):
                    at = slice(k * HEAD_DIM, (k + 1) * HEAD_DIM)
                    full = mm(xt[2 * (number & 1) + h], wqv[:, at], NN) + norms[5:6, at]
                    qkv[r, at] = (rope(full, here, 1.0) if k < 2 else full).astype(BF16)
            for i in (0, 1):
                _, _, v, p = probabilities(number, i)
                att[group_rows(number, i * half, half), :] = mm(p.astype(BF16), v, NN).astype(BF16)

    def attend_back(lo, hi):
        @pl.loop(lo, hi)
        def _(number):
            grad_q, grad_k, grad_v = {}, {}, {}
            tables = group_tables(number)
            for i in (1, 0):
                q, k, v, p = probabilities(number, i)
                low = p.astype(BF16)
                ga = mm(big2[group_rows(number, i * half, half), :], wdv[...], NT).astype(BF16)
                gp = mm(ga, v, NT)
                gs = (p * (gp - jnp.sum(p * gp, axis=-1, keepdims=True))).astype(BF16)
                grad_q[i] = mm(gs, k, NN) * 0.0625
                grad_k[i] = mm(gs, q, TN) * 0.0625
                grad_v[i] = mm(low, ga, TN)

            def put(k, total):
                total = total.astype(BF16)
                at = slice(k * HEAD_DIM, (k + 1) * HEAD_DIM)
                qkv[group_rows(number, 0, size), at] = total
                cols[:, at] += fold(total.astype(F32))

            def joined(one, two):
                return jnp.concatenate([one + two[:half], two[half:]], axis=0)

            put(0, rope(jnp.concatenate([grad_q[0], grad_q[1]], axis=0), tables, -1.0))
            put(1, rope(joined(grad_k[0], grad_k[1]), tables, -1.0))
            put(2, joined(grad_v[0], grad_v[1]))

    def add_tiles(one, other, out):
        @pl.loop(0, TILE // 32)
        def _(k):
            r = rows_at(k, 32)
            out[r, :] = (one[r, :].astype(F32) + other[r, :].astype(F32)).astype(BF16)

    def rel_of(k):
        return 3 - 2 * (k & 1) - (k >> 1)

    def out_sum(received):
        base = copies.reserve(4) if not received else state["o"]
        over = copies.reserve(2) if received else 0

        def to_core(k):
            part = ob.at[rows_at(k, TILE), :]
            return copies.at(base + k, part, co.at[rows_at(k, TILE), :], (me, 1 - core))

        def to_x(k):
            part = ob.at[rows_at(4 + k, TILE), :]
            return copies.at(over + k, part, xo.at[rows_at(k, TILE), :], (me ^ 1, core))

        spare = copies.locals
        copies.locals += 4

        def load(k):
            at = k & 1
            return pltpu.make_async_copy(co.at[rows_at(k, TILE), :], xt.at[at], local_sems.at[spare + at])

        def store(k):
            at = 2 + (k & 1)
            target = ob.at[rows_at(4 * received + k, TILE), :]
            return pltpu.make_async_copy(xt.at[at], target, local_sems.at[spare + at])

        def send(k):
            store(k).wait()
            if received:

                @pl.when(k < 2)
                def _():
                    to_x(k).start()

            else:
                to_core(k).start()

        if received:
            for k in range(4):
                to_core(k).wait_recv()
            for k in range(2):
                load(k).start()

        @pl.loop(0, 4)
        def _(k):
            r = rows_at(rel_of(k) * 2 + (core if received else 1 - core), TILE)
            if received:
                load(k).wait()

            @pl.loop(0, d_model // 1024)
            def _(jj):
                for j in range(2):
                    c = rows_at(2 * jj + j, 512)
                    total = mm(att[r, :], wdv[:, c], NN) + mm(hid[r, :], wb[:, c], NN)
                    if received:
                        total = total + xt[k & 1, :, c].astype(F32)
                    xt[2 + (k & 1), :, c] = total.astype(BF16)

            store(k).start()
            if received:

                @pl.when(k < 2)
                def _():
                    load(k + 2).start()

            @pl.when(k > 0)
            def _():
                send(k - 1)

        send(3)
        if received:
            state["ox"] = [to_x(k) for k in range(2)]
            copies.open.extend(state["ox"])
        else:
            state["o"] = base
            copies.open.extend(to_core(k) for k in range(4))

    def out_end(k):
        state["ox"][k].wait_recv()
        copies.now((ob.at[rows_at(6 + k, TILE), :], xt.at[0]), (xo.at[rows_at(k, TILE), :], xt.at[1]))
        add_tiles(xt.at[0], xt.at[1], xt.at[0])
        if k == 0:
            copies.now((xt.at[0], ob.at[rows_at(6, TILE), :]))
            landed.append(copies.remote(ob.at[rows_at(6, TILE), :], out_got, (me ^ 4, core)))
        else:
            copies.now((xt.at[0], out_keep))

    def in_sum(received):
        base = copies.reserve(4) if not received else state["i"]
        over = copies.reserve(2) if received else 0

        def to_core(k):
            part = big2.at[rows_at(k, TILE), :]
            return copies.at(base + k, part, ci.at[rows_at(k, TILE), :], (me, 1 - core))

        def to_x(k):
            part = big2.at[rows_at(4 + k, TILE), :]
            return copies.at(over + k, part, xi.at[rows_at(k, TILE), :], (me ^ 1, core))

        spare = copies.locals
        copies.locals += 2

        def load(k):
            at = k & 1
            return pltpu.make_async_copy(ci.at[rows_at(k, TILE), :], xt.at[at], local_sems.at[spare + at])

        if received:
            for k in range(4):
                to_core(k).wait_recv()
            for k in range(2):
                load(k).start()
        else:
            sums[0:4] = jnp.zeros_like(sums[0:4])
            for copy in state["X"]:
                copy.wait()

        @pl.loop(0, 4)
        def _(k):
            r = rows_at(rel_of(k) * 2 + (core if received else 1 - core), TILE)
            if received:
                load(k).wait()

            @pl.loop(0, d_model // 1024)
            def _(jj):
                for j in range(2):
                    c = rows_at(2 * jj + j, 512)
                    a = mm(qkv[r, :], wqv[c, :], NT)
                    f = mm(gf[r, :], wa[c, :], NT)
                    xhat = (big1[r, c].astype(F32) - stats[r, 0:1]) * stats[r, 1:2]
                    sums[0, :, c] += fold(a * xhat)
                    sums[1, :, c] += fold(a)
                    sums[2, :, c] += fold(f * xhat)
                    sums[3, :, c] += fold(f)
                    total = a * norms[0:1, c] + f * norms[2:3, c]
                    if received:
                        total = total + xt[k & 1, :, c].astype(F32)
                    big2[rows_at(4 * received + k, TILE), c] = total.astype(BF16)

            if received:

                @pl.when(k < 2)
                def _():
                    load(k + 2).start()
                    to_x(k).start()

            else:
                to_core(k).start()

        if received:
            state["ix"] = [to_x(k) for k in range(2)]
            copies.open.extend(state["ix"])
        else:
            state["i"] = base
            copies.open.extend(to_core(k) for k in range(4))

    def in_end(k):
        state["ix"][k].wait_recv()
        copies.now((xi.at[rows_at(k, TILE), :], xt.at[1]))
        acc = big2.at[rows_at(6 + k, TILE), :]
        add_tiles(acc, xt.at[1], acc)
        if k == 0:
            landed.append(copies.remote(acc, in_got, (me ^ 4, core)))
        else:
            copies.now((acc, in_keep))

    def vector_step(step):
        def piece(ref, d):
            return ref.at[:, rows_at(d, vec_got.shape[-1])]

        if step == "0":
            vec_own[...] = jnp.zeros_like(vec_own)
            for j in range(5):
                vec_own[j : j + 1, :] = jnp.sum(sums[j], axis=0, keepdims=True)
            for j in range(4):
                ours = jnp.where(mine == j, 1.0, 0.0)
                vec_own[8 + j : 9 + j, :] = jnp.sum(cols[...], axis=0, keepdims=True) * ours
            state["v"] = [
                copies.remote(piece(vec_own, me ^ d), vec_got.at[d], (me ^ d, core)) for d in range(1, 16)
            ]
        elif step == "1":
            total = vec_own[:, rows_at(me, vec_got.shape[-1])]
            for d, copy in enumerate(state["v"]):
                copy.wait_recv()
                total = total + vec_got[d + 1]
            vec_sum[...] = total
            state["v"] = copies.remote(vec_sum, vec_core, (me, 1 - core))
        elif step == "2":
            state["v"].wait_recv()
            here = rows_at(me, vec_got.shape[-1])
            vec[8:, here] = vec_sum[8:, :]
            vec[:8, here] = vec_sum[:8, :] + vec_core[:8, :]
            for d in range(1, 16):
                landed.append(copies.remote(piece(vec, me), piece(vec, me), (me ^ d, core)))

    def run(op):
        kind, rest = op[0], op[1:]
        if kind == "g":
            send_flag()
            spread()
        elif kind in "xc":
            token_step(kind, rest)
        elif kind == "s":
            send_weight(rest[0], int(rest[1:]))
        elif kind == "f":
            forward_weight(rest[0], int(rest[1:]))
        elif kind == "L":
            normalize()
        elif kind == "W":
            weight_ready(rest)
            copies.now({"1": (g1, wa), "2": (g2, wb), "q": (gq, wqv), "d": (gd, wdv)}[rest])
            if rest == "q":
                for copy in state["flags"]:
                    copy.wait_recv()
                kept.pop(0).wait()
                copies.now((flags, fl))
        elif kind == "P":
            up(*{"a": (0, 4), "b": (4, 8)}.get(rest, (0, 8)))
        elif kind == "C":
            load_cotangent()
        elif kind == "G":
            make_grad(rest)
        elif kind == "H":
            hidden_grad()
        elif kind == "r":
            forward_grad(rest[0], int(rest[1]))
        elif kind == "t":
            deliver_grad(rest[0], int(rest[1]))
        elif kind == "A":
            attend(*{"0": (0, 2), "2": (2, 4)}.get(rest, (0, 4)))
        elif kind == "B":
            attend_back(*{"0": (0, 2), "2": (2, 4)}.get(rest, (0, 4)))
        elif kind == "N":
            copies.now((na, big1))
        elif kind == "X":
            state["X"] = [copies.local(*pair) for pair in group_tiles(x_ref, xg, big1)]
        elif kind == "o":
            if rest in "01":
                out_sum(int(rest))
            else:
                out_end(0 if rest == "a" else 1)
        elif kind == "i":
            if rest in "01":
                in_sum(int(rest))
            else:
                in_end(0 if rest == "a" else 1)
        else:
            vector_step(rest)

    for op in ORDER.split():
        with jax.named_scope("step_" + op):
            run(op)
    for copy in landed:
        copy.wait_recv()
    for copy in kept:
        copy.wait()
    copies.finish()


def turn_tables(group_len):
    inverse = np.exp(
        np.arange(ROT // 2, dtype=np.float32) * np.float32(-2.0 * math.log(10000.0) / ROT)
    ).astype(np.float32)
    angles = np.arange(group_len).astype(np.float32)[:, None] * inverse
    tables = np.zeros((3, group_len, 128), np.float32)
    tables[0] = 1.0
    tables[0, :, : ROT // 2] = tables[0, :, ROT // 2 : ROT] = np.cos(angles)
    tables[1, :, : ROT // 2] = -np.sin(angles)
    tables[2, :, ROT // 2 : ROT] = np.sin(angles)
    return tables


def layer_call(x, c, w1, w2, wq, wd, ids, turns, *parts):
    n = lax.axis_size("dp")
    tok, d = x.shape
    rows, u1, uq, ud = w1.shape[0], w1.shape[1] // 4, wq.shape[1] // 4, wd.shape[0] // 4
    many = 8 * tok
    vmem = pl.BlockSpec(memory_space=pltpu.VMEM)
    hbm = pl.BlockSpec(memory_space=pltpu.HBM)

    def low(*shape):
        return jax.ShapeDtypeStruct(shape, BF16)

    results = [low(rows, 4 * u1), low(4 * u1, rows), low(rows, 4 * uq), low(4 * ud, rows)]
    results += [low(tok, d)] * 4 + [jax.ShapeDtypeStruct((16, d), F32), jax.ShapeDtypeStruct((8, d), F32)]
    spare = [low(many, d)] * 2 + [low(d, u1), low(u1, d), low(d, uq), low(ud, d), low(many, d)]
    for part in (2, 4):
        spare += [low(d // part, u1), low(u1, d // part), low(d // part, uq), low(ud, d // part)]
    spare += [low(4 * tok, d)] * 2 + [low(2 * tok, d)] * 2 + [low(many, d)] + [jax.ShapeDtypeStruct((4, 8, 128), F32)]
    scratch = [
        (many, d), (many, d), (d, u1), (u1, d), (d, uq), (ud, d), (many, u1), (many, u1), (many, uq), (many, ud),
        (d, u1), (u1, d), (d, uq), (ud, d), (4, tok, d), (u1, 2 * rows),
    ]
    flops = 2 * 3 * many * d * (2 * u1 + uq + ud)
    return pl.pallas_call(
        layer_kernel,
        out_shape=results + spare,
        in_specs=[hbm] * 6 + [pl.BlockSpec(memory_space=pltpu.SMEM)] + [vmem] * (1 + len(parts)),
        out_specs=[hbm] * 8 + [vmem] * 2 + [hbm] * len(spare),
        scratch_shapes=[pltpu.VMEM(s, BF16) for s in scratch]
        + [
            pltpu.VMEM((many, 2), F32),
            pltpu.VMEM((5, 8, d), F32),
            pltpu.VMEM((8, d), F32),
            pltpu.VMEM((16, d), F32),
            pltpu.VMEM((n, 16, d // n), F32),
            pltpu.VMEM((16, d // n), F32),
            pltpu.VMEM((16, d // n), F32),
            pltpu.VMEM((4, 8, 128), F32),
            pltpu.VMEM((8, 128), F32),
            pltpu.VMEM((sum(p.shape[0] for p in parts), 128), F32),
            pltpu.SemaphoreType.DMA((128,)),
            pltpu.SemaphoreType.DMA((176,)),
            pltpu.SemaphoreType.DMA((176,)),
        ],
        compiler_params=pltpu.CompilerParams(
            collective_id=1, has_side_effects=True, vmem_limit_bytes=65000 << 10
        ),
        cost_estimate=pl.CostEstimate(flops=flops, bytes_accessed=200 << 20, transcendentals=0),
        name="layer",
    )(x, c, w1, w2, wq, wd, ids, turns, *parts)[:10]


def finish_kernel(
    x, c, out_keep, out_got, in_keep, in_got, norms, vec, f1, f2, fq, fd,
    layer_output, input_grad, o1, o2, oq, od, v0, v1, v2, v3, v4, v5, bias_1, bias_q,
):
    own = x[...].astype(F32)
    branch = out_keep[...].astype(F32) + out_got[...].astype(F32)
    layer_output[...] = (own + branch + norms[6:7, :]).astype(BF16)
    center = own - jnp.mean(own, axis=-1, keepdims=True)
    scale = lax.rsqrt(jnp.mean(center * center, axis=-1, keepdims=True) + 1e-05)
    xhat = center * scale
    e = in_keep[...].astype(F32) + in_got[...].astype(F32)
    input_grad[...] = c[...].astype(F32) + scale * (
        e - jnp.mean(e, axis=-1, keepdims=True) - xhat * jnp.mean(e * xhat, axis=-1, keepdims=True)
    )
    for source, target in ((f1, o1), (f2, o2), (fq, oq), (fd, od)):
        target[...] = source[...].astype(F32)

    @pl.when(pl.program_id(0) == 0)
    def _():
        for target, row in ((v0, 0), (v1, 1), (v2, 2), (v3, 3), (v4, 4), (v5, 4)):
            for k in range(target.shape[0]):
                target[k : k + 1, :] = vec[row : row + 1, k * 128 : (k + 1) * 128]
        width = bias_q.shape[0] // 4
        for target, first in ((bias_q, 0), (bias_1, width)):
            count = target.shape[0] // 4
            for block in range(4):
                for k in range(count):
                    at = (first + k) * 128
                    target[block * count + k : block * count + k + 1, :] = vec[8 + block : 9 + block, at : at + 128]


def finish_call(x, c, out_keep, out_got, in_keep, in_got, norms, vec, f1, f2, fq, fd, units, width):
    steps = 8

    def rows_of(v):
        return pl.BlockSpec((v.shape[0] // steps, v.shape[1]), lambda i: (i, 0))

    tokens = [x, c, out_keep, out_got, in_keep, in_got]
    sums = [f1, f2, fq, fd]
    outs = [jax.ShapeDtypeStruct(x.shape, BF16)]
    outs += [jax.ShapeDtypeStruct(v.shape, F32) for v in [x] + sums]
    rows = [x.shape[1] // 128] * 6 + [4 * units // 128, 4 * width // 128]
    vectors = [jax.ShapeDtypeStruct((count, 128), F32) for count in rows]

    def whole(v):
        return pl.BlockSpec(v.shape, lambda i: (0, 0))

    return pl.pallas_call(
        finish_kernel,
        grid=(steps,),
        out_shape=outs + vectors,
        in_specs=[rows_of(v) for v in tokens]
        + [whole(norms), whole(vec)]
        + [rows_of(v) for v in sums],
        out_specs=[rows_of(v) for v in outs] + [whole(v) for v in vectors],
        compiler_params=pltpu.CompilerParams(vmem_limit_bytes=64000 << 10),
        name="finish",
    )(*tokens, norms, vec, *sums)


def local_fast(
    layer_input,
    ln1_gain,
    ln1_bias,
    ln2_gain,
    ln2_bias,
    qkv_weight,
    qkv_bias,
    dense_weight,
    dense_bias,
    fc1_weight,
    fc1_bias,
    fc2_weight,
    fc2_bias,
    seq_ids,
    cotangent,
):
    units, width = fc1_weight.shape[1] // 4, 3 * HEAD_DIM
    parts = (ln1_gain, ln1_bias, ln2_gain, ln2_bias, dense_bias, fc2_bias, fc1_bias, qkv_bias)
    f1, f2, fq, fd, out_keep, out_got, in_keep, in_got, vec, norms = layer_call(
        layer_input,
        cotangent,
        fc1_weight,
        fc2_weight,
        qkv_weight,
        dense_weight,
        seq_ids,
        turn_tables(seq_ids.shape[0]),
        *(v.reshape(-1, 128) for v in parts),
    )
    layer_output, input_grad, out_fc1, out_fc2, out_qkv, out_dense, *rest = finish_call(
        layer_input, cotangent, out_keep, out_got, in_keep, in_got, norms, vec, f1, f2, fq, fd, units, width
    )
    gain_1, shift_1, gain_2, shift_2, bias_d, bias_2, bias_1, bias_q = (v.reshape(-1) for v in rest)
    return (
        layer_output,
        input_grad,
        gain_1,
        shift_1,
        gain_2,
        shift_2,
        out_qkv,
        bias_q,
        out_dense,
        bias_d,
        out_fc1,
        bias_1,
        out_fc2,
        bias_2,
    )


def solution(mesh):
    local = local_fast if mesh.shape["dp"] == 16 else local_pairs
    in_specs = (
        P(("dp", "tensor"), None),
        P(),
        P(),
        P(),
        P(),
        P("dp", "tensor"),
        P("tensor"),
        P("tensor", "dp"),
        P(),
        P("dp", "tensor"),
        P("tensor"),
        P("tensor", "dp"),
        P(),
        P("dp"),
        P(("dp", "tensor"), None),
    )
    out_specs = (
        P(("dp", "tensor"), None),
        P(("dp", "tensor"), None),
        P(),
        P(),
        P(),
        P(),
        P("dp", "tensor"),
        P("tensor"),
        P("tensor", "dp"),
        P(),
        P("dp", "tensor"),
        P("tensor"),
        P("tensor", "dp"),
        P(),
    )
    return jax.shard_map(local, mesh=mesh, in_specs=in_specs, out_specs=out_specs, check_vma=False)
```

```python
import math

import jax
import jax.numpy as jnp
import numpy as np
from jax import lax
from jax.experimental import pallas as pl
from jax.experimental.pallas import tpu as pltpu
from jax.sharding import PartitionSpec as P

HEAD_DIM = 256
ROT = 64
BIT_X, BIT_Y, BIT_ZL, FIRST_ZH = 0, 1, 2, 3
F32, BF16 = jnp.float32, jnp.bfloat16
MESH = pl.DeviceIdType.MESH
NN = (((1,), (0,)), ((), ()))
NT = (((1,), (1,)), ((), ()))
TN = (((0,), (0,)), ((), ()))


def mm(a, b, dims):
    return lax.dot_general(a, b, dims, preferred_element_type=F32)


def turn_angles(group_ids):
    places = jnp.arange(group_ids.shape[-1], dtype=jnp.int32)
    starts_flag = jnp.concatenate(
        [jnp.ones_like(group_ids[..., :1], dtype=bool), group_ids[..., 1:] != group_ids[..., :-1]],
        axis=-1,
    )
    starts = lax.cummax(jnp.where(starts_flag, places, 0), axis=group_ids.ndim - 1)
    position = (places - starts).astype(F32)
    steps_rot = jnp.arange(ROT // 2, dtype=F32)
    inverse = jnp.exp(steps_rot * (-2.0 * math.log(10000.0) / ROT))
    angles = position[..., None] * inverse
    angles = jnp.concatenate([angles, angles], axis=-1)
    return (jnp.cos(angles), jnp.sin(angles))


def rotary(vectors, cosine_table, sine_table):
    half_rot = ROT // 2
    rot_part = vectors[..., :ROT]
    rot_rest = vectors[..., ROT:]
    turned = jnp.concatenate([-rot_part[..., half_rot:], rot_part[..., :half_rot]], axis=-1)
    rotated = rot_part * cosine_table + turned * sine_table
    return jnp.concatenate([rotated, rot_rest], axis=-1)


def rotary_back(vectors, cosine_table, sine_table):
    half_rot = ROT // 2
    rot_part = vectors[..., :ROT]
    rot_rest = vectors[..., ROT:]
    turned = jnp.concatenate([rot_part[..., half_rot:], -rot_part[..., :half_rot]], axis=-1)
    rotated = rot_part * cosine_table + turned * sine_table
    return jnp.concatenate([rotated, rot_rest], axis=-1)


def local_pairs(
    layer_input,
    ln1_gain,
    ln1_bias,
    ln2_gain,
    ln2_bias,
    qkv_weight,
    qkv_bias,
    dense_weight,
    dense_bias,
    fc1_weight,
    fc1_bias,
    fc2_weight,
    fc2_bias,
    seq_ids,
    cotangent,
):
    n = lax.axis_size("dp")
    bits = n.bit_length() - 1
    me = lax.axis_index("dp")
    core = lax.axis_index("tensor")
    bit = [(me >> k) & 1 for k in range(bits)]
    zh_bits = tuple(range(FIRST_ZH, bits))
    rows_here, d_model = layer_input.shape
    feature = 2 * bit[BIT_ZL] + bit[BIT_X]

    def swap(v, k):
        return lax.ppermute(v, "dp", [(i, i ^ (1 << k)) for i in range(n)])

    def swap_core(v):
        return lax.ppermute(v, "tensor", [(0, 1), (1, 0)])

    def pick(v, b, axis):
        return lax.dynamic_index_in_dim(v, b, axis, keepdims=False)

    def ordered(b, own, other, axis):
        return jnp.stack(
            [jnp.where(b == 0, own, other), jnp.where(b == 0, other, own)], axis=axis
        )

    def gather_rows(v):
        v = jnp.stack([v, swap(v, BIT_ZL)], axis=0)
        v = jnp.concatenate([v, swap(v, BIT_X)], axis=0)
        return v

    def gather_tokens(v):
        v = gather_rows(v)
        return ordered(core, v, swap_core(v), 1).reshape(4 * 2 * rows_here, d_model)

    def scatter_tokens(v):
        v = v.reshape(4, 2, rows_here, d_model)
        keep = pick(v, core, 1)
        v = keep + swap_core(pick(v, 1 - core, 1).astype(BF16))
        v = v[:2] + swap(v[2:].astype(BF16), BIT_X)
        return v[0] + swap(v[1].astype(BF16), BIT_ZL)

    def gather_weight(w):
        rows, width = w.shape
        w = w.reshape(rows, 2, 2, width // 4)
        w = ordered(bit[BIT_X], pick(w, bit[BIT_X], 2), swap(pick(w, 1 - bit[BIT_X], 2), BIT_X), 0)
        w = ordered(bit[BIT_ZL], pick(w, bit[BIT_ZL], 2), swap(pick(w, 1 - bit[BIT_ZL], 2), BIT_ZL), 0)
        for k in zh_bits:
            w = ordered(bit[k], w, swap(w, k), 0)
        w = ordered(bit[BIT_Y], w, swap(w, BIT_Y), w.ndim - 3)
        return w.reshape(rows * n, width // 4)

    def scatter_grad(g):
        rows, width = g.shape[0] // n, g.shape[1]
        g = g.reshape((2,) * bits + (rows, width))
        axis = bits - 1 - BIT_Y
        g = pick(g, bit[BIT_Y], axis) + swap(pick(g, 1 - bit[BIT_Y], axis).astype(BF16), BIT_Y)
        for k in reversed(zh_bits):
            g = pick(g, bit[k], 0) + swap(pick(g, 1 - bit[k], 0).astype(BF16), k)
        g = g.astype(BF16)
        g = ordered(bit[BIT_ZL], pick(g, bit[BIT_ZL], 0), swap(pick(g, 1 - bit[BIT_ZL], 0), BIT_ZL), 2)
        g = ordered(bit[BIT_X], pick(g, bit[BIT_X], 0), swap(pick(g, 1 - bit[BIT_X], 0), BIT_X), 2)
        return g.reshape(rows, 4 * width).astype(F32)

    def take_block(v, parts):
        return lax.dynamic_slice_in_dim(v, feature * (v.shape[0] // parts), v.shape[0] // parts, 0)

    gains = [v.astype(F32) for v in (ln1_gain, ln1_bias, ln2_gain, ln2_bias)]

    rows_in = gather_tokens(layer_input)
    w_fc1 = gather_weight(fc1_weight)
    cot = gather_tokens(cotangent)
    w_fc2 = gather_weight(fc2_weight.T)
    w_qkv = gather_weight(qkv_weight)
    w_dense = gather_weight(dense_weight.T)
    ids = gather_rows(seq_ids)
    group_len = seq_ids.shape[0]

    def normalize(v):
        v = v.astype(F32)
        center = v - jnp.mean(v, axis=-1, keepdims=True)
        spread = jnp.mean(center * center, axis=-1, keepdims=True)
        scale = lax.rsqrt(spread + 1e-05)
        return center * scale, scale

    xhat, _ = normalize(rows_in)
    normed_attn = (xhat * gains[0] + gains[1]).astype(BF16)
    normed_ffn = (xhat * gains[2] + gains[3]).astype(BF16)

    ffn_input = mm(normed_ffn, w_fc1, NN) + take_block(fc1_bias, 4).astype(F32)
    cdf = 0.5 * (1.0 + lax.erf(ffn_input * (1.0 / math.sqrt(2.0))))
    density = jnp.exp(-0.5 * ffn_input * ffn_input) * (1.0 / math.sqrt(2.0 * math.pi))
    hidden = (ffn_input * cdf).astype(BF16)
    slope = cdf + ffn_input * density
    grad_fc2 = mm(cot, hidden, TN)
    out_fc2 = scatter_grad(grad_fc2).T

    grad_ffn = (mm(cot, w_fc2, NN) * slope).astype(BF16)
    grad_fc1 = mm(normed_ffn, grad_ffn, TN)
    out_fc1 = scatter_grad(grad_fc1)

    qkv = mm(normed_attn, w_qkv, NN) + take_block(qkv_bias, 4).astype(F32)
    qkv = qkv.reshape(4, group_len, 3, HEAD_DIM)
    cosines, sines = turn_angles(ids)
    query = rotary(qkv[:, :, 0], cosines, sines).astype(BF16)
    keys = rotary(qkv[:, :, 1], cosines, sines).astype(BF16)
    values = qkv[:, :, 2].astype(BF16)
    places = jnp.arange(group_len, dtype=jnp.int32)
    allowed = (ids[:, :, None] == ids[:, None, :]) & (places[None, None, :] <= places[None, :, None])
    scores = jnp.einsum("gqd,gkd->gqk", query, keys, preferred_element_type=F32) * 0.0625
    scores = jnp.where(allowed, scores, -1e30)
    weights = jnp.exp(scores - jnp.max(scores, axis=-1, keepdims=True))
    probability = weights / jnp.sum(weights, axis=-1, keepdims=True)
    prob_low = probability.astype(BF16)
    attended = jnp.einsum("gqk,gkd->gqd", prob_low, values, preferred_element_type=F32)
    attended = attended.astype(BF16).reshape(-1, HEAD_DIM)

    partial = mm(attended, w_dense, NT) + mm(hidden, w_fc2, NT)
    branch = scatter_tokens(partial)
    layer_output = (
        layer_input.astype(F32) + branch + dense_bias.astype(F32) + fc2_bias.astype(F32)
    ).astype(BF16)

    grad_dense = mm(cot, attended, TN)
    grad_attended = mm(cot, w_dense, NN).astype(BF16).reshape(4, group_len, HEAD_DIM)
    grad_prob = jnp.einsum("gqd,gkd->gqk", grad_attended, values, preferred_element_type=F32)
    row_dot = jnp.sum(probability * grad_prob, axis=-1, keepdims=True)
    grad_scores = (probability * (grad_prob - row_dot)).astype(BF16)
    grad_query = jnp.einsum("gqk,gkd->gqd", grad_scores, keys, preferred_element_type=F32) * 0.0625
    grad_keys = jnp.einsum("gqk,gqd->gkd", grad_scores, query, preferred_element_type=F32) * 0.0625
    grad_values = jnp.einsum("gqk,gqd->gkd", prob_low, grad_attended, preferred_element_type=F32)
    qkv_grad = jnp.concatenate(
        [
            rotary_back(grad_query, cosines, sines).astype(BF16),
            rotary_back(grad_keys, cosines, sines).astype(BF16),
            grad_values.astype(BF16),
        ],
        axis=-1,
    ).reshape(-1, 3 * HEAD_DIM)
    out_qkv = scatter_grad(mm(normed_attn, qkv_grad, TN))
    out_dense = scatter_grad(grad_dense).T

    attn_part = mm(qkv_grad, w_qkv, NT)
    ffn_part = mm(grad_ffn, w_fc1, NT)
    e_rows = scatter_tokens(attn_part * gains[0] + ffn_part * gains[2])
    own_hat, own_scale = normalize(layer_input)
    cot_rows = cotangent.astype(F32)
    input_grad = cot_rows + own_scale * (
        e_rows
        - jnp.mean(e_rows, axis=-1, keepdims=True)
        - own_hat * jnp.mean(e_rows * own_hat, axis=-1, keepdims=True)
    )

    small = jnp.stack(
        [
            jnp.sum(attn_part * xhat, axis=0),
            jnp.sum(attn_part, axis=0),
            jnp.sum(ffn_part * xhat, axis=0),
            jnp.sum(ffn_part, axis=0),
            jnp.sum(cot_rows, axis=0),
        ]
    )
    small = small + swap_core(small)
    for k in range(bits):
        small = small + swap(small, k)
    columns = jnp.concatenate(
        [jnp.sum(qkv_grad.astype(F32), axis=0), jnp.sum(grad_ffn.astype(F32), axis=0)]
    )
    for k in (BIT_Y,) + zh_bits:
        columns = columns + swap(columns, k)
    columns = ordered(bit[BIT_X], columns, swap(columns, BIT_X), 0)
    columns = ordered(bit[BIT_ZL], columns, swap(columns, BIT_ZL), 0).reshape(4, -1)
    out_qkv_bias = columns[:, : 3 * HEAD_DIM].reshape(-1)
    out_fc1_bias = columns[:, 3 * HEAD_DIM :].reshape(-1)

    return (
        layer_output,
        input_grad,
        small[0],
        small[1],
        small[2],
        small[3],
        out_qkv,
        out_qkv_bias,
        out_dense,
        small[4],
        out_fc1,
        out_fc1_bias,
        out_fc2,
        small[4],
    )


TILE = 256
ORDER = """
g0 sq1 sd5 sd1 sq9 sq0 s14 s11 sd4 s112 s113 x0 sq4 sd9 fd1 sq12 sd12 s19 sq13 sq8 s15 f11 s20 s21 s10 sd0 s18
sd8 fd4 f14 f113 x1 f112 sd13 fd9 x2 fq13 f21 fq12 sq5 c0 fq8 s212 fq4 fq1 fd8 s29 x3 fq9 fq5 fd13 L f19 s28
f18 Wq c1 f15 fd5 fd12 s24 A s213 c2 s25 f212 f24 f29 W1 P f28 c3 Wd f25 C f213 G2 W2 o0 r23 H o1 r22 Gd G1
rd3 oa N B r21 r13 t21 Gq X i0 r11 rd1 r12 t11 i1 rq2 td1 r20 v0 rd2 rd0 rq3 ia rq1 r10 t20 td0 rq0 ib tq0 v1
ob v2 tq1 t10
"""


def place():
    return lax.axis_index("dp"), lax.axis_index("tensor")


def feature_of(d):
    return 2 * ((d >> BIT_ZL) & 1) + (d & 1)


def greet(peers):
    barrier = pltpu.get_barrier_semaphore()
    for peer in peers:
        pl.semaphore_signal(barrier, inc=1, device_id=peer, device_id_type=MESH)
    pl.semaphore_wait(barrier, len(peers))


class Copies:
    def __init__(self, local_sems, send_sems, recv_sems):
        self.sems = (local_sems, send_sems, recv_sems)
        self.count, self.open, self.locals = 0, [], 0

    def reserve(self, count):
        self.count += count
        return self.count - count

    def at(self, number, source, target, device):
        return pltpu.make_async_remote_copy(
            src_ref=source,
            dst_ref=target,
            send_sem=self.sems[1].at[number],
            recv_sem=self.sems[2].at[number],
            device_id=device,
            device_id_type=MESH,
        )

    def remote(self, source, target, device):
        copy = self.at(self.reserve(1), source, target, device)
        copy.start()
        self.open.append(copy)
        return copy

    def local(self, source, target):
        copy = pltpu.make_async_copy(source, target, self.sems[0].at[self.locals])
        copy.start()
        self.locals += 1
        return copy

    def now(self, *pairs):
        for copy in [self.local(*pair) for pair in pairs]:
            copy.wait()

    def finish(self):
        for copy in self.open:
            copy.wait_send()


def rows_at(start, size):
    return pl.ds(pl.multiple_of(start * size, size), size)


def fold(v):
    return jnp.sum(v.reshape(v.shape[0] // 8, 8, v.shape[1]), axis=0)


def rope(v, tables, sign):
    first = v[:, :128]
    turned = pltpu.roll(first, 96, 1) * tables[1] + pltpu.roll(first, 32, 1) * tables[2]
    return jnp.concatenate([first * tables[0] + sign * turned, v[:, 128:]], axis=1)


def layer_kernel(
    x_ref, c_ref, w1, w2, wq, wd, ids, turns, p0, p1, p2, p3, p4, p5, p6, p7,
    f1, f2, fq, fd, out_keep, out_got, in_keep, in_got, vec, norms,
    xg, cg, g1, g2, gq, gd, na, r1, r2, rq, rd, z1, z2, zq, zd, co, ci, xo, xi, ob, flags,
    big1, big2, wa, wb, wqv, wdv, hid, gf, qkv, att, d1, d2, dq, dd, xt, st, stats, sums, cols, vec_own, vec_got, vec_sum, vec_core, fl, flag, vectors,
    local_sems, send_sems, recv_sems,
):
    me, core = place()
    by, upper, mine = (me >> 1) & 1, me >> 2, feature_of(me)
    rows = w1.shape[0]
    d_model = x_ref.shape[1]
    greet([(me ^ d, core) for d in range(1, 16)] + [(me, 1 - core)])
    copies = Copies(local_sems, send_sems, recv_sems)
    weights = {"1": (w1, g1, 1), "2": (w2, g2, 0), "q": (wq, gq, 1), "d": (wd, gd, 0)}
    tokens = {"x": (x_ref, xg), "c": (c_ref, cg)}
    grads = {"1": (d1, f1, r1, z1, 0), "2": (d2, f2, r2, z2, 1), "q": (dq, fq, rq, zq, 0), "d": (dd, fd, rd, zd, 1)}
    state, kept, landed = {}, [], []
    pieces = {name: [] for name in weights}

    def spread():
        lanes = vectors.shape[1]
        norms[...] = jnp.zeros_like(norms)
        wide = d_model // lanes
        start = 0
        for part in (p0, p1, p2, p3, p4, p5, p6, p7):
            vectors[start : start + part.shape[0], :] = part[...].astype(F32)
            start += part.shape[0]
        units, width = wa.shape[1] // lanes, wqv.shape[1] // lanes
        places = [(row, row * wide, wide) for row in range(4)]
        places.append((4, 6 * wide + mine * units, units))
        places.append((5, 6 * wide + 4 * units + mine * width, width))
        for row, start, count in places:
            for k in range(count):
                norms[row : row + 1, k * lanes : (k + 1) * lanes] = vectors[pl.ds(start + k, 1), :]
        for k in range(wide):
            both = vectors[pl.ds(4 * wide + k, 1), :] + vectors[pl.ds(5 * wide + k, 1), :]
            norms[6:7, k * lanes : (k + 1) * lanes] = both

    def block(w, dim, d):
        size = w.shape[dim] // 4
        cut = pl.ds(feature_of(d) * size, size)
        return w.at[cut, :] if dim == 0 else w.at[:, cut]

    def slot(g, dim, d):
        cut = pl.ds(d * rows, rows)
        return g.at[:, cut] if dim == 0 else g.at[cut, :]

    def send_flag():
        cols[...] = jnp.zeros_like(cols)
        flag[...] = jnp.full(flag.shape, ids[ids.shape[0] - 1], jnp.int32).astype(F32)
        kept.append(copies.local(flag, flags.at[0]))
        state["flags"] = [copies.remote(flag, flags.at[k], (me ^ d, core)) for k, d in ((1, 1), (2, 4), (3, 5))]

    def send_weight(name, d):
        w, g, dim = weights[name]
        if d == 0:
            state[name, 0] = copies.local(block(w, dim, me), slot(g, dim, me))
            pieces[name].append(copies.remote(block(w, dim, me ^ 2), slot(g, dim, me), (me ^ 2, core)))
        else:
            state[name, d] = copies.remote(block(w, dim, me ^ d), slot(g, dim, me), (me ^ d, core))

    def forward_weight(name, d):
        w, g, dim = weights[name]
        state[name, d].wait_recv()
        held = slot(g, dim, me ^ d)
        pieces[name].append(copies.remote(held, held, (me ^ 2, core)))

    def weight_ready(name):
        state[name, 0].wait()
        for copy in pieces[name]:
            copy.wait_recv()

    def tile_at(ref, rel, half):
        return ref.at[rows_at(rel * 2 + half, TILE), :]

    def token_step(kind, step):
        source, g = tokens[kind]
        if step == "0":
            state[kind] = [
                copies.remote(source, tile_at(g, 2, core), (me ^ 4, core)),
                copies.remote(source, tile_at(g, 1, core), (me ^ 1, core)),
            ]
            state[kind + "p0"] = copies.remote(source, tile_at(g, 0, core), (me, 1 - core))
        elif step == "1":
            state[kind][0].wait_recv()
            state[kind].append(copies.remote(tile_at(g, 2, core), tile_at(g, 3, core), (me ^ 1, core)))
            state[kind + "p2"] = copies.remote(tile_at(g, 2, core), tile_at(g, 2, core), (me, 1 - core))
        elif step == "2":
            state[kind][1].wait_recv()
            state[kind + "p1"] = copies.remote(tile_at(g, 1, core), tile_at(g, 1, core), (me, 1 - core))
        elif step == "3":
            state[kind][2].wait_recv()
            state[kind + "p3"] = copies.remote(tile_at(g, 3, core), tile_at(g, 3, core), (me, 1 - core))

    def normalize():
        for rel in range(4):
            state["xp%d" % rel].wait_recv()
        keep = copies.locals
        copies.locals += 4

        def load(k, source):
            return pltpu.make_async_copy(source, xt.at[k & 1], local_sems.at[keep + (k & 1)])

        def store(k):
            return pltpu.make_async_copy(
                big2.at[rows_at(k & 1, TILE), :], na.at[rows_at(k, TILE), :], local_sems.at[keep + 2 + (k & 1)]
            )

        def start(k):
            @pl.when(k == core)
            def _():
                load(k, x_ref).start()

            @pl.when(k != core)
            def _():
                load(k, xg.at[rows_at(k, TILE), :]).start()

        start(0)

        @pl.loop(0, 8)
        def _(k):
            @pl.when(k < 7)
            def _():
                start(k + 1)

            load(k, x_ref).wait()

            @pl.when(k > 1)
            def _():
                store(k).wait()

            @pl.loop(0, TILE // 32)
            def _(j):
                r = rows_at(j, 32)
                here = rows_at(k * (TILE // 32) + j, 32)
                v = xt[k & 1, r, :].astype(F32)
                mean = jnp.mean(v, axis=-1, keepdims=True)
                center = v - mean
                scale = lax.rsqrt(jnp.mean(center * center, axis=-1, keepdims=True) + 1e-05)
                xhat = center * scale
                big2[rows_at((k & 1) * (TILE // 32) + j, 32), :] = (xhat * norms[0:1, :] + norms[1:2, :]).astype(BF16)
                big1[here, :] = (xhat * norms[2:3, :] + norms[3:4, :]).astype(BF16)
                stats[here, 0:1] = mean
                stats[here, 1:2] = scale

            store(k).start()

        store(0).wait()
        store(1).wait()

    def up(lo, hi):
        @pl.loop(lo, hi)
        def _(i):
            r = rows_at(i, TILE)
            for j in range(0, wa.shape[1], 512):
                c = slice(j, j + 512)
                v = mm(big1[r, :], wa[:, c], NN) + norms[4:5, c]
                cdf = 0.5 * (1.0 + lax.erf(v * (1.0 / math.sqrt(2.0))))
                density = jnp.exp(-0.5 * v * v) * (1.0 / math.sqrt(2.0 * math.pi))
                hid[r, c] = (v * cdf).astype(BF16)
                gf[r, c] = (cdf + v * density).astype(BF16)

    def group_tiles(own, gathered, target):
        after = pl.ds(2 * TILE, 6 * TILE)
        return [
            (own, tile_at(target, 0, core)),
            (tile_at(gathered, 0, 1 - core), tile_at(target, 0, 1 - core)),
            (gathered.at[after, :], target.at[after, :]),
        ]

    def load_cotangent():
        for k in range(4):
            state["cp%d" % k].wait_recv()
        copies.now(*group_tiles(c_ref, cg, big2))

        @pl.loop(0, TILE // 32)
        def _(k):
            part = fold(big2[rows_at(core * (TILE // 32) + k, 32), :].astype(F32))
            sums[4] = jnp.where(k == 0, part, sums[4] + part)

    def cut(ref, dim, start, size):
        start = pl.multiple_of(start * size, size)
        return ref.at[pl.ds(start, size), :] if dim == 0 else ref.at[:, pl.ds(start, size)]

    def make_grad(name):
        d, _, r, _, dim = grads[name]
        base = copies.reserve(4)

        def send(k):
            pair = (upper ^ (3 - k)) * 2 + 1 - by
            return copies.at(
                base + k, cut(d, dim, pair, 2 * rows), cut(r, dim, 3 - k, 2 * rows), (me ^ 2, core)
            )

        @pl.loop(0, 8)
        def _(k):
            pair = (upper ^ (3 - (k & 3))) * 2 + (by ^ 1 ^ (k >> 2))
            c = rows_at(pair, 2 * rows)
            if name == "1":
                d[c, :] = mm(big1[:, c], gf[...], TN).astype(BF16)
            elif name == "q":
                d[c, :] = mm(big1[:, c], qkv[...], TN).astype(BF16)
            elif name == "2":
                for j in (0, 512):
                    d[j : j + 512, c] = mm(hid[:, j : j + 512], big2[:, c], TN).astype(BF16)
            else:
                d[:, c] = mm(att[...], big2[:, c], TN).astype(BF16)

            @pl.when(k < 4)
            def _():
                send(k).start()

        for k in range(4):
            state["r" + name, 3 - k] = send(k)
            copies.open.append(send(k))

    def add_slab(name, dim, got, k, own):
        d = grads[name][0]
        stage = st if name == "2" else xt.at[0, :, pl.ds(0, d.shape[1] if dim == 0 else 2 * rows)]
        copies.now((cut(got, dim, k, 2 * rows), stage))
        some = 32 if dim == 0 else 128

        @pl.loop(0, stage.shape[0] // some)
        def _(j):
            c = rows_at(j, some)
            own[c, :] = (own[c, :].astype(F32) + stage[c, :].astype(F32)).astype(BF16)

    def forward_grad(name, u):
        d, f, r, z, dim = grads[name]
        state["r" + name, u].wait_recv()
        own = cut(d, dim, (upper ^ u) * 2 + by, 2 * rows)
        add_slab(name, dim, r, u, own)
        if u & 2:
            state["z" + name, u & 1] = copies.remote(own, cut(z, dim, u & 1, 2 * rows), (me ^ 8, core))

    def deliver_grad(name, u):
        d, f, r, z, dim = grads[name]
        state["z" + name, u].wait_recv()
        add_slab(name, dim, z, u, cut(d, dim, (upper ^ u) * 2 + by, 2 * rows))
        for x in (1, 0):
            piece = cut(d, dim, (upper ^ u) * 4 + by * 2 + ((me & 1) ^ x), rows)
            width = f.shape[1 - dim] // 4
            c = pl.ds(mine * width, width)
            target = f.at[:, c] if dim == 0 else f.at[c, :]
            if u == 0 and x == 0:
                kept.append(copies.local(piece, target))
            else:
                landed.append(copies.remote(piece, target, (me ^ (4 * u + x), core)))

    def hidden_grad():
        @pl.loop(0, 8)
        def _(i):
            r = rows_at(i, TILE)
            for j in range(0, gf.shape[1], 512):
                c = slice(j, j + 512)
                g = (mm(big2[r, :], wb[c, :], NT) * gf[r, c].astype(F32)).astype(BF16)
                gf[r, c] = g
                at = slice(3 * HEAD_DIM + j, 3 * HEAD_DIM + j + 512)
                cols[:, at] += fold(g.astype(F32))

    size, half, quarter = 2 * TILE, TILE, TILE // 2

    def group_rows(number, start, length):
        return pl.ds(pl.multiple_of(number * size + start, TILE), length)

    def group_tables(number):
        three = fl[number, 0:1, 0:1] > 0.5
        tables = []
        for k in range(3):
            again = jnp.concatenate([turns[k, :quarter], turns[k, : 2 * quarter], turns[k, :quarter]], axis=0)
            tables.append(jnp.where(three, again, turns[k]))
        return tables

    def probabilities(number, i):
        seen = (i + 1) * half
        q = qkv[group_rows(number, i * half, half), :HEAD_DIM]
        k = qkv[group_rows(number, 0, seen), HEAD_DIM : 2 * HEAD_DIM]
        v = qkv[group_rows(number, 0, seen), 2 * HEAD_DIM :]
        ti = lax.broadcasted_iota(jnp.int32, (half, seen), 0) + i * half
        tj = lax.broadcasted_iota(jnp.int32, (half, seen), 1)
        part_i = (ti >= quarter).astype(jnp.int32) + (ti >= 3 * quarter).astype(jnp.int32)
        part_j = (tj >= quarter).astype(jnp.int32) + (tj >= 3 * quarter).astype(jnp.int32)
        three = fl[number, 0:1, 0:1] > 0.5
        s = mm(q, k, NT) * 0.0625
        s = jnp.where(tj <= ti, s, -1e30)
        s = jnp.where((part_i != part_j) & three, -1e30, s)
        w = jnp.exp(s - jnp.max(s, axis=-1, keepdims=True))
        return q, k, v, w / jnp.sum(w, axis=-1, keepdims=True)

    def attend(lo, hi):
        spare = copies.locals
        copies.locals += 4

        def load(number, h):
            at = 2 * (number & 1) + h
            source = na.at[group_rows(number, h * half, half), :]
            return pltpu.make_async_copy(source, xt.at[at], local_sems.at[spare + at])

        for h in (0, 1):
            load(lo, h).start()

        @pl.loop(lo, hi)
        def _(number):
            @pl.when(number + 1 < hi)
            def _():
                for h in (0, 1):
                    load(number + 1, h).start()

            tables = group_tables(number)
            for h in (0, 1):
                load(number, h).wait()
                r = group_rows(number, h * half, half)
                here = [t[h * half : (h + 1) * half] for t in tables]
                for k in range(3):
                    at = slice(k * HEAD_DIM, (k + 1) * HEAD_DIM)
                    full = mm(xt[2 * (number & 1) + h], wqv[:, at], NN) + norms[5:6, at]
                    qkv[r, at] = (rope(full, here, 1.0) if k < 2 else full).astype(BF16)
            for i in (0, 1):
                _, _, v, p = probabilities(number, i)
                att[group_rows(number, i * half, half), :] = mm(p.astype(BF16), v, NN).astype(BF16)

    def attend_back(lo, hi):
        @pl.loop(lo, hi)
        def _(number):
            grad_q, grad_k, grad_v = {}, {}, {}
            tables = group_tables(number)
            for i in (1, 0):
                q, k, v, p = probabilities(number, i)
                low = p.astype(BF16)
                ga = mm(big2[group_rows(number, i * half, half), :], wdv[...], NT).astype(BF16)
                gp = mm(ga, v, NT)
                gs = (p * (gp - jnp.sum(p * gp, axis=-1, keepdims=True))).astype(BF16)
                grad_q[i] = mm(gs, k, NN) * 0.0625
                grad_k[i] = mm(gs, q, TN) * 0.0625
                grad_v[i] = mm(low, ga, TN)

            def put(k, total):
                total = total.astype(BF16)
                at = slice(k * HEAD_DIM, (k + 1) * HEAD_DIM)
                qkv[group_rows(number, 0, size), at] = total
                cols[:, at] += fold(total.astype(F32))

            def joined(one, two):
                return jnp.concatenate([one + two[:half], two[half:]], axis=0)

            put(0, rope(jnp.concatenate([grad_q[0], grad_q[1]], axis=0), tables, -1.0))
            put(1, rope(joined(grad_k[0], grad_k[1]), tables, -1.0))
            put(2, joined(grad_v[0], grad_v[1]))

    def add_tiles(one, other, out):
        @pl.loop(0, TILE // 32)
        def _(k):
            r = rows_at(k, 32)
            out[r, :] = (one[r, :].astype(F32) + other[r, :].astype(F32)).astype(BF16)

    def rel_of(k):
        return 3 - 2 * (k & 1) - (k >> 1)

    def out_sum(received):
        base = copies.reserve(4) if not received else state["o"]
        over = copies.reserve(2) if received else 0

        def to_core(k):
            part = ob.at[rows_at(k, TILE), :]
            return copies.at(base + k, part, co.at[rows_at(k, TILE), :], (me, 1 - core))

        def to_x(k):
            part = ob.at[rows_at(4 + k, TILE), :]
            return copies.at(over + k, part, xo.at[rows_at(k, TILE), :], (me ^ 1, core))

        spare = copies.locals
        copies.locals += 4

        def load(k):
            at = k & 1
            return pltpu.make_async_copy(co.at[rows_at(k, TILE), :], xt.at[at], local_sems.at[spare + at])

        def store(k):
            at = 2 + (k & 1)
            target = ob.at[rows_at(4 * received + k, TILE), :]
            return pltpu.make_async_copy(xt.at[at], target, local_sems.at[spare + at])

        def send(k):
            store(k).wait()
            if received:

                @pl.when(k < 2)
                def _():
                    to_x(k).start()

            else:
                to_core(k).start()

        if received:
            for k in range(4):
                to_core(k).wait_recv()
            for k in range(2):
                load(k).start()

        @pl.loop(0, 4)
        def _(k):
            r = rows_at(rel_of(k) * 2 + (core if received else 1 - core), TILE)
            if received:
                load(k).wait()

            @pl.loop(0, d_model // 1024)
            def _(jj):
                for j in range(2):
                    c = rows_at(2 * jj + j, 512)
                    total = mm(att[r, :], wdv[:, c], NN) + mm(hid[r, :], wb[:, c], NN)
                    if received:
                        total = total + xt[k & 1, :, c].astype(F32)
                    xt[2 + (k & 1), :, c] = total.astype(BF16)

            store(k).start()
            if received:

                @pl.when(k < 2)
                def _():
                    load(k + 2).start()

            @pl.when(k > 0)
            def _():
                send(k - 1)

        send(3)
        if received:
            state["ox"] = [to_x(k) for k in range(2)]
            copies.open.extend(state["ox"])
        else:
            state["o"] = base
            copies.open.extend(to_core(k) for k in range(4))

    def out_end(k):
        state["ox"][k].wait_recv()
        copies.now((ob.at[rows_at(6 + k, TILE), :], xt.at[0]), (xo.at[rows_at(k, TILE), :], xt.at[1]))
        add_tiles(xt.at[0], xt.at[1], xt.at[0])
        if k == 0:
            copies.now((xt.at[0], ob.at[rows_at(6, TILE), :]))
            landed.append(copies.remote(ob.at[rows_at(6, TILE), :], out_got, (me ^ 4, core)))
        else:
            copies.now((xt.at[0], out_keep))

    def in_sum(received):
        base = copies.reserve(4) if not received else state["i"]
        over = copies.reserve(2) if received else 0

        def to_core(k):
            part = big2.at[rows_at(k, TILE), :]
            return copies.at(base + k, part, ci.at[rows_at(k, TILE), :], (me, 1 - core))

        def to_x(k):
            part = big2.at[rows_at(4 + k, TILE), :]
            return copies.at(over + k, part, xi.at[rows_at(k, TILE), :], (me ^ 1, core))

        spare = copies.locals
        copies.locals += 2

        def load(k):
            at = k & 1
            return pltpu.make_async_copy(ci.at[rows_at(k, TILE), :], xt.at[at], local_sems.at[spare + at])

        if received:
            for k in range(4):
                to_core(k).wait_recv()
            for k in range(2):
                load(k).start()
        else:
            sums[0:4] = jnp.zeros_like(sums[0:4])
            for copy in state["X"]:
                copy.wait()

        @pl.loop(0, 4)
        def _(k):
            r = rows_at(rel_of(k) * 2 + (core if received else 1 - core), TILE)
            if received:
                load(k).wait()

            @pl.loop(0, d_model // 1024)
            def _(jj):
                for j in range(2):
                    c = rows_at(2 * jj + j, 512)
                    a = mm(qkv[r, :], wqv[c, :], NT)
                    f = mm(gf[r, :], wa[c, :], NT)
                    xhat = (big1[r, c].astype(F32) - stats[r, 0:1]) * stats[r, 1:2]
                    sums[0, :, c] += fold(a * xhat)
                    sums[1, :, c] += fold(a)
                    sums[2, :, c] += fold(f * xhat)
                    sums[3, :, c] += fold(f)
                    total = a * norms[0:1, c] + f * norms[2:3, c]
                    if received:
                        total = total + xt[k & 1, :, c].astype(F32)
                    big2[rows_at(4 * received + k, TILE), c] = total.astype(BF16)

            if received:

                @pl.when(k < 2)
                def _():
                    load(k + 2).start()
                    to_x(k).start()

            else:
                to_core(k).start()

        if received:
            state["ix"] = [to_x(k) for k in range(2)]
            copies.open.extend(state["ix"])
        else:
            state["i"] = base
            copies.open.extend(to_core(k) for k in range(4))

    def in_end(k):
        state["ix"][k].wait_recv()
        copies.now((xi.at[rows_at(k, TILE), :], xt.at[1]))
        acc = big2.at[rows_at(6 + k, TILE), :]
        add_tiles(acc, xt.at[1], acc)
        if k == 0:
            landed.append(copies.remote(acc, in_got, (me ^ 4, core)))
        else:
            copies.now((acc, in_keep))

    def vector_step(step):
        def piece(ref, d):
            return ref.at[:, rows_at(d, vec_got.shape[-1])]

        if step == "0":
            vec_own[...] = jnp.zeros_like(vec_own)
            for j in range(5):
                vec_own[j : j + 1, :] = jnp.sum(sums[j], axis=0, keepdims=True)
            for j in range(4):
                ours = jnp.where(mine == j, 1.0, 0.0)
                vec_own[8 + j : 9 + j, :] = jnp.sum(cols[...], axis=0, keepdims=True) * ours
            state["v"] = [
                copies.remote(piece(vec_own, me ^ d), vec_got.at[d], (me ^ d, core)) for d in range(1, 16)
            ]
        elif step == "1":
            total = vec_own[:, rows_at(me, vec_got.shape[-1])]
            for d, copy in enumerate(state["v"]):
                copy.wait_recv()
                total = total + vec_got[d + 1]
            vec_sum[...] = total
            state["v"] = copies.remote(vec_sum, vec_core, (me, 1 - core))
        elif step == "2":
            state["v"].wait_recv()
            here = rows_at(me, vec_got.shape[-1])
            vec[8:, here] = vec_sum[8:, :]
            vec[:8, here] = vec_sum[:8, :] + vec_core[:8, :]
            for d in range(1, 16):
                landed.append(copies.remote(piece(vec, me), piece(vec, me), (me ^ d, core)))

    def run(op):
        kind, rest = op[0], op[1:]
        if kind == "g":
            send_flag()
            spread()
        elif kind in "xc":
            token_step(kind, rest)
        elif kind == "s":
            send_weight(rest[0], int(rest[1:]))
        elif kind == "f":
            forward_weight(rest[0], int(rest[1:]))
        elif kind == "L":
            normalize()
        elif kind == "W":
            weight_ready(rest)
            copies.now({"1": (g1, wa), "2": (g2, wb), "q": (gq, wqv), "d": (gd, wdv)}[rest])
            if rest == "q":
                for copy in state["flags"]:
                    copy.wait_recv()
                kept.pop(0).wait()
                copies.now((flags, fl))
        elif kind == "P":
            up(*{"a": (0, 4), "b": (4, 8)}.get(rest, (0, 8)))
        elif kind == "C":
            load_cotangent()
        elif kind == "G":
            make_grad(rest)
        elif kind == "H":
            hidden_grad()
        elif kind == "r":
            forward_grad(rest[0], int(rest[1]))
        elif kind == "t":
            deliver_grad(rest[0], int(rest[1]))
        elif kind == "A":
            attend(*{"0": (0, 2), "2": (2, 4)}.get(rest, (0, 4)))
        elif kind == "B":
            attend_back(*{"0": (0, 2), "2": (2, 4)}.get(rest, (0, 4)))
        elif kind == "N":
            copies.now((na, big1))
        elif kind == "X":
            state["X"] = [copies.local(*pair) for pair in group_tiles(x_ref, xg, big1)]
        elif kind == "o":
            if rest in "01":
                out_sum(int(rest))
            else:
                out_end(0 if rest == "a" else 1)
        elif kind == "i":
            if rest in "01":
                in_sum(int(rest))
            else:
                in_end(0 if rest == "a" else 1)
        else:
            vector_step(rest)

    for op in ORDER.split():
        with jax.named_scope("step_" + op):
            run(op)
    for copy in landed:
        copy.wait_recv()
    for copy in kept:
        copy.wait()
    copies.finish()


def turn_tables(group_len):
    inverse = np.exp(
        np.arange(ROT // 2, dtype=np.float32) * np.float32(-2.0 * math.log(10000.0) / ROT)
    ).astype(np.float32)
    angles = np.arange(group_len).astype(np.float32)[:, None] * inverse
    tables = np.zeros((3, group_len, 128), np.float32)
    tables[0] = 1.0
    tables[0, :, : ROT // 2] = tables[0, :, ROT // 2 : ROT] = np.cos(angles)
    tables[1, :, : ROT // 2] = -np.sin(angles)
    tables[2, :, ROT // 2 : ROT] = np.sin(angles)
    return tables


def layer_call(x, c, w1, w2, wq, wd, ids, turns, *parts):
    n = lax.axis_size("dp")
    tok, d = x.shape
    rows, u1, uq, ud = w1.shape[0], w1.shape[1] // 4, wq.shape[1] // 4, wd.shape[0] // 4
    many = 8 * tok
    vmem = pl.BlockSpec(memory_space=pltpu.VMEM)
    hbm = pl.BlockSpec(memory_space=pltpu.HBM)

    def low(*shape):
        return jax.ShapeDtypeStruct(shape, BF16)

    results = [low(rows, 4 * u1), low(4 * u1, rows), low(rows, 4 * uq), low(4 * ud, rows)]
    results += [low(tok, d)] * 4 + [jax.ShapeDtypeStruct((16, d), F32), jax.ShapeDtypeStruct((8, d), F32)]
    spare = [low(many, d)] * 2 + [low(d, u1), low(u1, d), low(d, uq), low(ud, d), low(many, d)]
    for part in (2, 4):
        spare += [low(d // part, u1), low(u1, d // part), low(d // part, uq), low(ud, d // part)]
    spare += [low(4 * tok, d)] * 2 + [low(2 * tok, d)] * 2 + [low(many, d)] + [jax.ShapeDtypeStruct((4, 8, 128), F32)]
    scratch = [
        (many, d), (many, d), (d, u1), (u1, d), (d, uq), (ud, d), (many, u1), (many, u1), (many, uq), (many, ud),
        (d, u1), (u1, d), (d, uq), (ud, d), (4, tok, d), (u1, 2 * rows),
    ]
    flops = 2 * 3 * many * d * (2 * u1 + uq + ud)
    return pl.pallas_call(
        layer_kernel,
        out_shape=results + spare,
        in_specs=[hbm] * 6 + [pl.BlockSpec(memory_space=pltpu.SMEM)] + [vmem] * (1 + len(parts)),
        out_specs=[hbm] * 8 + [vmem] * 2 + [hbm] * len(spare),
        scratch_shapes=[pltpu.VMEM(s, BF16) for s in scratch]
        + [
            pltpu.VMEM((many, 2), F32),
            pltpu.VMEM((5, 8, d), F32),
            pltpu.VMEM((8, d), F32),
            pltpu.VMEM((16, d), F32),
            pltpu.VMEM((n, 16, d // n), F32),
            pltpu.VMEM((16, d // n), F32),
            pltpu.VMEM((16, d // n), F32),
            pltpu.VMEM((4, 8, 128), F32),
            pltpu.VMEM((8, 128), F32),
            pltpu.VMEM((sum(p.shape[0] for p in parts), 128), F32),
            pltpu.SemaphoreType.DMA((128,)),
            pltpu.SemaphoreType.DMA((176,)),
            pltpu.SemaphoreType.DMA((176,)),
        ],
        compiler_params=pltpu.CompilerParams(
            collective_id=1, has_side_effects=True, vmem_limit_bytes=65000 << 10
        ),
        cost_estimate=pl.CostEstimate(flops=flops, bytes_accessed=200 << 20, transcendentals=0),
        name="layer",
    )(x, c, w1, w2, wq, wd, ids, turns, *parts)[:10]


def finish_kernel(
    x, c, out_keep, out_got, in_keep, in_got, norms, vec, f1, f2, fq, fd,
    layer_output, input_grad, o1, o2, oq, od, v0, v1, v2, v3, v4, v5, bias_1, bias_q,
):
    own = x[...].astype(F32)
    branch = out_keep[...].astype(F32) + out_got[...].astype(F32)
    layer_output[...] = (own + branch + norms[6:7, :]).astype(BF16)
    center = own - jnp.mean(own, axis=-1, keepdims=True)
    scale = lax.rsqrt(jnp.mean(center * center, axis=-1, keepdims=True) + 1e-05)
    xhat = center * scale
    e = in_keep[...].astype(F32) + in_got[...].astype(F32)
    input_grad[...] = c[...].astype(F32) + scale * (
        e - jnp.mean(e, axis=-1, keepdims=True) - xhat * jnp.mean(e * xhat, axis=-1, keepdims=True)
    )
    for source, target in ((f1, o1), (f2, o2), (fq, oq), (fd, od)):
        target[...] = source[...].astype(F32)

    @pl.when(pl.program_id(0) == 0)
    def _():
        for target, row in ((v0, 0), (v1, 1), (v2, 2), (v3, 3), (v4, 4), (v5, 4)):
            for k in range(target.shape[0]):
                target[k : k + 1, :] = vec[row : row + 1, k * 128 : (k + 1) * 128]
        width = bias_q.shape[0] // 4
        for target, first in ((bias_q, 0), (bias_1, width)):
            count = target.shape[0] // 4
            for block in range(4):
                for k in range(count):
                    at = (first + k) * 128
                    target[block * count + k : block * count + k + 1, :] = vec[8 + block : 9 + block, at : at + 128]


def finish_call(x, c, out_keep, out_got, in_keep, in_got, norms, vec, f1, f2, fq, fd, units, width):
    steps = 4

    def rows_of(v):
        return pl.BlockSpec((v.shape[0] // steps, v.shape[1]), lambda i: (i, 0))

    tokens = [x, c, out_keep, out_got, in_keep, in_got]
    sums = [f1, f2, fq, fd]
    outs = [jax.ShapeDtypeStruct(x.shape, BF16)]
    outs += [jax.ShapeDtypeStruct(v.shape, F32) for v in [x] + sums]
    rows = [x.shape[1] // 128] * 6 + [4 * units // 128, 4 * width // 128]
    vectors = [jax.ShapeDtypeStruct((count, 128), F32) for count in rows]

    def whole(v):
        return pl.BlockSpec(v.shape, lambda i: (0, 0))

    return pl.pallas_call(
        finish_kernel,
        grid=(steps,),
        out_shape=outs + vectors,
        in_specs=[rows_of(v) for v in tokens]
        + [whole(norms), whole(vec)]
        + [rows_of(v) for v in sums],
        out_specs=[rows_of(v) for v in outs] + [whole(v) for v in vectors],
        compiler_params=pltpu.CompilerParams(vmem_limit_bytes=64000 << 10),
        name="finish",
    )(*tokens, norms, vec, *sums)


def local_fast(
    layer_input,
    ln1_gain,
    ln1_bias,
    ln2_gain,
    ln2_bias,
    qkv_weight,
    qkv_bias,
    dense_weight,
    dense_bias,
    fc1_weight,
    fc1_bias,
    fc2_weight,
    fc2_bias,
    seq_ids,
    cotangent,
):
    units, width = fc1_weight.shape[1] // 4, 3 * HEAD_DIM
    parts = (ln1_gain, ln1_bias, ln2_gain, ln2_bias, dense_bias, fc2_bias, fc1_bias, qkv_bias)
    f1, f2, fq, fd, out_keep, out_got, in_keep, in_got, vec, norms = layer_call(
        layer_input,
        cotangent,
        fc1_weight,
        fc2_weight,
        qkv_weight,
        dense_weight,
        seq_ids,
        turn_tables(seq_ids.shape[0]),
        *(v.reshape(-1, 128) for v in parts),
    )
    layer_output, input_grad, out_fc1, out_fc2, out_qkv, out_dense, *rest = finish_call(
        layer_input, cotangent, out_keep, out_got, in_keep, in_got, norms, vec, f1, f2, fq, fd, units, width
    )
    gain_1, shift_1, gain_2, shift_2, bias_d, bias_2, bias_1, bias_q = (v.reshape(-1) for v in rest)
    return (
        layer_output,
        input_grad,
        gain_1,
        shift_1,
        gain_2,
        shift_2,
        out_qkv,
        bias_q,
        out_dense,
        bias_d,
        out_fc1,
        bias_1,
        out_fc2,
        bias_2,
    )


def solution(mesh):
    local = local_fast if mesh.shape["dp"] == 16 else local_pairs
    in_specs = (
        P(("dp", "tensor"), None),
        P(),
        P(),
        P(),
        P(),
        P("dp", "tensor"),
        P("tensor"),
        P("tensor", "dp"),
        P(),
        P("dp", "tensor"),
        P("tensor"),
        P("tensor", "dp"),
        P(),
        P("dp"),
        P(("dp", "tensor"), None),
    )
    out_specs = (
        P(("dp", "tensor"), None),
        P(("dp", "tensor"), None),
        P(),
        P(),
        P(),
        P(),
        P("dp", "tensor"),
        P("tensor"),
        P("tensor", "dp"),
        P(),
        P("dp", "tensor"),
        P("tensor"),
        P("tensor", "dp"),
        P(),
    )
    return jax.shard_map(local, mesh=mesh, in_specs=in_specs, out_specs=out_specs, check_vma=False)
```
